32 devices in a mesh: dp: 8 (over z, y), shard: 4 (over x, core).
Axes of the slice: x: 2, y: 2, z: 4, core: 2. Of those that a mesh axis runs over, the one named last changes fastest.
Arguments:
- inputs: bfloat16 [32, 512, 1024], P('dp', 'shard'), may hold values from -6 to 6
- cotangent: bfloat16 [32, 512, 1024], P('dp', 'shard'), may hold values from -6 to 6
- lengths: int32 [32], P('dp'), may hold values from 128 to 512, as said below
- attend_weight: float32 [3, 1024, 1024], P(None, ('dp', 'shard')), may hold values from -0.1875 to 0.1875
- attend_first: float32 [3, 1024, 1024], P(None, ('dp', 'shard')), may hold values from -64 to 64
- attend_second: float32 [3, 1024, 1024], P(None, ('dp', 'shard')), may hold values from 8.02816 to 32.11264
- mixing_weight: float32 [1024, 1024], P(('dp', 'shard')), may hold values from -2 to 2
- mixing_first: float32 [1024, 1024], P(('dp', 'shard')), may hold values from -6 to 6
- mixing_second: float32 [1024, 1024], P(('dp', 'shard')), may hold values from 0.0442368 to 0.180224
- expand_weight: float32 [1024, 4096], P(('dp', 'shard')), may hold values from -0.1875 to 0.1875
- expand_first: float32 [1024, 4096], P(('dp', 'shard')), may hold values from -24 to 24
- expand_second: float32 [1024, 4096], P(('dp', 'shard')), may hold values from 1.114112 to 4.42368
- reduce_weight: float32 [4096, 1024], P(('dp', 'shard')), may hold values from -0.09375 to 0.09375
- reduce_first: float32 [4096, 1024], P(('dp', 'shard')), may hold values from -48 to 48
- reduce_second: float32 [4096, 1024], P(('dp', 'shard')), may hold values from 5.07904 to 20.48
- vectors: float32 [12, 1024], P(None, ('dp', 'shard')), may hold values from -0.4 to 1.3
- vectors_first: float32 [12, 1024], P(None, ('dp', 'shard')), may hold values from -44.8 to 44.8
- vectors_second: float32 [12, 1024], P(None, ('dp', 'shard')), may hold values from 1.114112 to 72.0896
Outputs:
- result: bfloat16 [32, 512, 1024], P('dp', 'shard')
- input_gradient: float32 [32, 512, 1024], P('dp', 'shard')
- first_attend: float32 [3, 1024, 1024], P(None, ('dp', 'shard'))
- second_attend: float32 [3, 1024, 1024], P(None, ('dp', 'shard'))
- weight_attend: float32 [3, 1024, 1024], P(None, ('dp', 'shard'))
- first_mixing: float32 [1024, 1024], P(('dp', 'shard'))
- second_mixing: float32 [1024, 1024], P(('dp', 'shard'))
- weight_mixing: float32 [1024, 1024], P(('dp', 'shard'))
- first_expand: float32 [1024, 4096], P(('dp', 'shard'))
- second_expand: float32 [1024, 4096], P(('dp', 'shard'))
- weight_expand: float32 [1024, 4096], P(('dp', 'shard'))
- first_reduce: float32 [4096, 1024], P(('dp', 'shard'))
- second_reduce: float32 [4096, 1024], P(('dp', 'shard'))
- weight_reduce: float32 [4096, 1024], P(('dp', 'shard'))
- first_vectors: float32 [12, 1024], P(None, ('dp', 'shard'))
- second_vectors: float32 [12, 1024], P(None, ('dp', 'shard'))
- weight_vectors: float32 [12, 1024], P(None, ('dp', 'shard'))
- mixing_bias_grad: float32 [1024], P(('dp', 'shard'))
The draws below stay inside these ranges and needn't reach their ends.
Inputs may be any that keep to these rules, and one draw needn't show every extreme that they name: `lengths`: in each micro-batch of each index of dp, one of its 2 sequences, drawn at random, holds more than 384 positions; some sequence holds all 512.
All inputs are finite; a program needn't handle non-finite values.
Results may differ from the reference program's by a relative error of at most 0.013.
The reference program's roundings to bfloat16 on the way count: a program that leaves them out, or rounds other values in their place, can miss the bound.
Values may be sent and summed in bfloat16 or wider, within the bound.
A program may use at most 192 MiB of HBM per device.

```python
import math
import jax
import jax.numpy as jnp
from jax import lax

D = 1024
H = 16
HD = 64
FF = 4096
MB = 2
SEQ_MB = 2
STEP = 10
LEN = 512
SEQS = 32
NV = 12


row_scales = (0.7, 0.9, 1.0, 1.2, 1.2, 1.0, 1.0, 1.0)


def vector_scale():
    head_part = jnp.array(row_scales, jnp.float32)
    tail_part = jnp.full((NV - 8,), 0.3, jnp.float32)
    return jnp.concatenate([head_part, tail_part])[:, None] * (0.87 * math.sqrt(SEQS * LEN))


def draw_lengths(key, part):
    key = jax.random.fold_in(key, 11)
    key_short = jax.random.fold_in(key, 1)
    key_long = jax.random.fold_in(key, 2)
    key_which = jax.random.fold_in(key, 3)
    key_top = jax.random.fold_in(key, 4)
    groups = SEQS // SEQ_MB
    short_len = jax.random.randint(key_short, (groups, SEQ_MB), LEN // 4, LEN + 1)
    long_len = jax.random.randint(key_long, (groups,), 3 * LEN // 4 + 1, LEN + 1)
    chosen = jax.random.randint(key_which, (groups,), 0, SEQ_MB)
    top_group = jax.random.randint(key_top, (), 0, groups)
    long_len = jnp.where(jnp.arange(groups) == top_group, LEN, long_len)
    picked = jnp.arange(SEQ_MB)[None, :] == chosen[:, None]
    return jnp.where(picked, long_len[:, None], short_len).reshape(SEQS).astype(jnp.int32)


def draw_vectors(key, part):
    key = jax.random.fold_in(key, 21)
    key_bias = jax.random.fold_in(key, 1)
    key_gain = jax.random.fold_in(key, 2)
    biases = jax.random.uniform(key_bias, (NV, D), jnp.float32, -0.4, 0.4)
    gains = jax.random.uniform(key_gain, (NV, D), jnp.float32, 0.7, 1.3)
    row_ids = jnp.arange(NV)[:, None]
    gain_rows = (row_ids == 3) | (row_ids == 5)
    return jnp.where(gain_rows, gains, biases)


def draw_vectors_first(key, part):
    key = jax.random.fold_in(key, 23)
    base = jax.random.truncated_normal(key, -3.0, 3.0, (NV, D), jnp.float32)
    return base * 0.111 * vector_scale()


def draw_vectors_second(key, part):
    key = jax.random.fold_in(key, 29)
    factor = jnp.exp(jax.random.uniform(key, (NV, D), jnp.float32, 0.0, math.log(4.0)))
    scale_rows = vector_scale()
    return factor * 0.001 * scale_rows * scale_rows


def raised(entries, rng, source, target, blocks, factor):
    owner, partner = [(jnp.arange(entries.shape[dim]) // (entries.shape[dim] // blocks)).reshape([-1 if axis == dim else 1 for axis in range(entries.ndim)]) for dim in (source, target)]
    chosen = jax.random.permutation(rng, blocks)[partner]
    strong = (owner == chosen) | (owner == (partner + blocks // 2) % blocks)
    return jnp.where(strong, factor * entries, entries)


def steps_of(stream_key, extent, shards, smallest, largest):
    level = 1.0
    for dim, blocks in shards:
        steps = jax.random.uniform(jax.random.fold_in(jax.random.fold_in(stream_key, 6), dim), (blocks,), jnp.float32, smallest / len(shards), largest / len(shards))
        level = level * jnp.repeat(jnp.exp(steps), extent[dim] // blocks).reshape((-1,) + (1,) * (len(extent) - 1 - dim))
    return level


def bell_draw(rng, dims, scale, bound, cuts=(), kind=jnp.bfloat16):
    values = scale * jax.random.normal(rng, dims, jnp.float32)
    if cuts:
        values = values * steps_of(rng, dims, cuts, -0.22, 0.18)
    return jnp.clip(values, -bound, bound).astype(kind)


def noise_with(rng, extent, width, reach, split, heavy, kind=jnp.bfloat16):
    drawn = width * jax.random.normal(rng, extent, jnp.float32)
    if split:
        drawn = drawn * steps_of(rng, extent, split, -0.22, 0.18)
    return jnp.clip(raised(drawn, jax.random.fold_in(rng, 3), *heavy), -reach, reach).astype(kind)


def setup_inputs(seed: int = 0) -> dict:
    arg_keys = jax.random.split(jax.random.key(seed), 19)
    return {
        "inputs": bell_draw(arg_keys[0], (SEQS, LEN, D), 1.0, 6.0, ((0, 8), (1, 4))),
        "cotangent": noise_with(arg_keys[1], (SEQS, LEN, D), 1.0, 6.0, ((0, 8), (1, 4)), (0, 2, 8, 2.0)),
        "lengths": draw_lengths(jax.random.fold_in(arg_keys[18], 71), 0),
        "attend_weight": bell_draw(arg_keys[3], (3, D, D), D ** -0.5, 0.1875, ((1, 32),), jnp.float32),
        "attend_first": bell_draw(arg_keys[4], (3, D, D), (0.078 * (SEQS * LEN) ** 0.5), 64.0, ((1, 32),), jnp.float32),
        "attend_second": jnp.clip(jnp.exp(math.log(32.11264) - 1.3862944 * jax.random.uniform(arg_keys[5], (3, D, D), jnp.float32) ** steps_of(arg_keys[5], (3, D, D), ((1, 32),), -0.2, 0.2)), 8.02816, 32.11264),
        "mixing_weight": bell_draw(arg_keys[6], (D, D), (max(1, 4 * D // LEN)) ** -0.5, 2.0, ((0, 32),), jnp.float32),
        "mixing_first": bell_draw(arg_keys[7], (D, D), (0.0058 * (SEQS * LEN) ** 0.5), 6.0, ((0, 32),), jnp.float32),
        "mixing_second": jnp.clip(jnp.exp(math.log(0.180224) - 1.40464347 * jax.random.uniform(arg_keys[8], (D, D), jnp.float32) ** steps_of(arg_keys[8], (D, D), ((0, 32),), -0.2, 0.2)), 0.0442368, 0.180224),
        "expand_weight": bell_draw(arg_keys[9], (D, FF), D ** -0.5, 0.1875, ((0, 32),), jnp.float32),
        "expand_first": bell_draw(arg_keys[10], (D, FF), (0.029 * (SEQS * LEN) ** 0.5), 24.0, ((0, 32),), jnp.float32),
        "expand_second": jnp.clip(jnp.exp(math.log(4.42368) - 1.3789142 * jax.random.uniform(arg_keys[11], (D, FF), jnp.float32) ** steps_of(arg_keys[11], (D, FF), ((0, 32),), -0.2, 0.2)), 1.114112, 4.42368),
        "reduce_weight": bell_draw(arg_keys[12], (FF, D), FF ** -0.5, 0.09375, ((0, 32),), jnp.float32),
        "reduce_first": bell_draw(arg_keys[13], (FF, D), (0.062 * (SEQS * LEN) ** 0.5), 48.0, ((0, 32),), jnp.float32),
        "reduce_second": jnp.clip(jnp.exp(math.log(20.48) - 1.3943265 * jax.random.uniform(arg_keys[14], (FF, D), jnp.float32) ** steps_of(arg_keys[14], (FF, D), ((0, 32),), -0.2, 0.2)), 5.07904, 20.48),
        "vectors": draw_vectors(jax.random.fold_in(arg_keys[18], 71), 0),
        "vectors_first": draw_vectors_first(jax.random.fold_in(arg_keys[18], 71), 0),
        "vectors_second": draw_vectors_second(jax.random.fold_in(arg_keys[18], 71), 0),
    }


@jax.custom_vjp
def low(v):
    return lax.optimization_barrier(v.astype(jnp.bfloat16)).astype(jnp.float32)

@jax.custom_vjp
def low_back(v):
    return v

def low_keep(v):
    return (low(v), None)

def low_pass(kept, grad):
    return (grad,)

def back_keep(v):
    return (v, None)

def back_low(kept, grad):
    return (low(grad),)
low.defvjp(low_keep, low_pass)
low_back.defvjp(back_keep, back_low)
beta_one = 0.9
beta_two = 0.999
adam_eps = 1e-08
norm_eps = 1e-05
matrix_decay = 0.01
masked_score = -1e+30
rates = (0.06, 1.0, 0.06, 0.03, 0.5)

def layer_norm(tensor, gain, shift):
    center = tensor - lax.optimization_barrier(jnp.mean(tensor, axis=-1, keepdims=True))
    spread = lax.optimization_barrier(jnp.mean(center * center, axis=-1, keepdims=True))
    return center * lax.rsqrt(spread + norm_eps) * gain + shift

def project(tensor, weight):
    return jnp.einsum('sri,ij->srj', tensor, weight, precision=lax.Precision.HIGHEST)

def split_heads(tensor):
    return tensor.reshape(tensor.shape[0], tensor.shape[1], H, HD)

def forward(attend_weight, mixing_weight, expand_weight, reduce_weight, vectors, inputs, lengths):
    attend_weight = low(attend_weight)
    mixing_weight = low(mixing_weight)
    expand_weight = low(expand_weight)
    reduce_weight = low(reduce_weight)
    vectors = low(vectors)
    seq_count = inputs.shape[0]
    positions = jnp.arange(inputs.shape[1])
    key_valid = positions[None, :] < lengths[:, None]
    row_valid = key_valid.astype(inputs.dtype)
    queries = low(low_back(project(inputs, attend_weight[0]) + vectors[0]))
    keys_all = low(low_back(project(inputs, attend_weight[1])))
    values = low(low_back(project(inputs, attend_weight[2]) + vectors[1]))
    raw_scores = jnp.einsum('sqhd,skhd->shqk', split_heads(queries), split_heads(keys_all), precision=lax.Precision.HIGHEST)
    scores = jnp.where(key_valid[:, None, None, :], low_back(raw_scores * HD ** (-0.5)), masked_score)
    row_peak = lax.optimization_barrier(jnp.max(scores, axis=-1, keepdims=True))
    row_sum = lax.optimization_barrier(jnp.sum(jnp.exp(scores - row_peak), axis=-1, keepdims=True))
    shares = jnp.exp(scores - (row_peak + jnp.log(row_sum)))
    shares_low = low(shares)
    blended = jnp.einsum('shqk,skhd->sqhd', shares_low, split_heads(values), precision=lax.Precision.HIGHEST)
    blended = low(low_back(blended.reshape(seq_count, inputs.shape[1], D)))
    attended = low_back(project(blended, mixing_weight) + vectors[2])
    settled = layer_norm(inputs + attended, vectors[3], vectors[4])
    expanded = low_back(project(low(settled), expand_weight) + vectors[8:].reshape(FF))
    activated = low(jax.nn.gelu(expanded, approximate=False))
    contracted = low_back(project(activated, reduce_weight) + vectors[7])
    finished = layer_norm(settled + contracted, vectors[5], vectors[6])
    return finished * row_valid[:, :, None]

def adam_update(weight, first, second, gradient, rate, decay):
    first_new = beta_one * first + (1.0 - beta_one) * gradient
    second_new = beta_two * second + (1.0 - beta_two) * gradient * gradient
    first_hat = first_new / (1.0 - beta_one ** STEP)
    second_hat = second_new / (1.0 - beta_two ** STEP)
    weight_new = weight - rate * (first_hat / (jnp.sqrt(second_hat) + adam_eps) + decay * weight)
    return (first_new, second_new, weight_new)

def reference(inputs, cotangent, lengths, attend_weight, attend_first, attend_second, mixing_weight, mixing_first, mixing_second, expand_weight, expand_first, expand_second, reduce_weight, reduce_first, reduce_second, vectors, vectors_first, vectors_second):
    masters = (attend_weight, mixing_weight, expand_weight, reduce_weight, vectors)
    per_block = MB * SEQ_MB
    count_blocks = SEQS // per_block
    input_blocks = inputs.astype(jnp.float32).reshape(count_blocks, per_block, LEN, D)
    cot_blocks = cotangent.astype(jnp.float32).reshape(count_blocks, per_block, LEN, D)
    length_blocks = lengths.reshape(count_blocks, per_block)

    def one_block(totals, pieces):
        input_piece, cot_piece, length_piece = pieces

        def layer_call(params, tensor):
            return forward(params[0], params[1], params[2], params[3], params[4], tensor, length_piece)
        output_piece, pullback = jax.vjp(layer_call, masters, input_piece)
        grads, grad_input = pullback(cot_piece)
        totals = jax.tree.map(jnp.add, totals, grads)
        return (totals, (output_piece.astype(jnp.bfloat16), grad_input))
    zeros = jax.tree.map(jnp.zeros_like, masters)
    totals, (outputs, grad_inputs) = lax.scan(one_block, zeros, (input_blocks, cot_blocks, length_blocks))
    result = outputs.reshape(SEQS, LEN, D)
    input_gradient = grad_inputs.reshape(SEQS, LEN, D)
    moments = ((attend_first, attend_second), (mixing_first, mixing_second), (expand_first, expand_second), (reduce_first, reduce_second), (vectors_first, vectors_second))
    updated = []
    for number in range(5):
        decay = matrix_decay if number < 4 else 0.0
        updated.append(adam_update(masters[number], moments[number][0], moments[number][1], totals[number], rates[number], decay))
    return (result, input_gradient, updated[0][0], updated[0][1], updated[0][2], updated[1][0], updated[1][1], updated[1][2], updated[2][0], updated[2][1], updated[2][2], updated[3][0], updated[3][1], updated[3][2], updated[4][0], updated[4][1], updated[4][2], totals[4][2])
```

```python
import functools

import jax
import jax.numpy as jnp
from jax import lax
from jax.experimental import pallas as pl
from jax.experimental.pallas import tpu as pltpu
from jax.sharding import PartitionSpec as P

D = 1024
HD = 64
FF = 4096
STEP = 10
NV = 12
MESH = pl.DeviceIdType.MESH
ALL = slice(None)

beta_one = 0.9
beta_two = 0.999
adam_eps = 1e-08
norm_eps = 1e-05
matrix_decay = 0.01
masked_score = -1e30
rates = (0.06, 1.0, 0.06, 0.03, 0.5)
bf16 = jnp.bfloat16
f32 = jnp.float32


def place():
    dp = lax.axis_index("dp")
    sh = lax.axis_index("shard")
    return lax.div(dp, 2), lax.rem(dp, 2), lax.div(sh, 2), lax.rem(sh, 2)


def device(z, y, x, c):
    return (z * 2 + y, x * 2 + c)


def meet(z, y, x, c):
    bar = pltpu.get_barrier_semaphore()
    others = [device(z, y, x, 1 - c), device(z, y, 1 - x, c), device(z, 1 - y, x, c)]
    others += [device(lax.rem(z + k, 4), y, x, c) for k in (1, 2, 3)]
    for other in others:
        pl.semaphore_signal(bar, inc=1, device_id=other, device_id_type=MESH)
    pl.semaphore_wait(bar, len(others))


GATHER_ORDER = ("zyx", "zxy")
GATHER_LAGS = (0, 2, 4, 6, 8)


def gather_kernel(sa, sm, se, sr, wa, wm, we, wr, own_sem, ssem, rsem):
    z, y, x, c = place()
    pieces = [(sa.at[i], wa.at[i], pl.ds(k * 512, 512)) for i in range(3) for k in range(2)]
    pieces += [(sm, wm, pl.ds(k * 512, 512)) for k in range(2)]
    pieces += [(se, we, pl.ds(k * 512, 512)) for k in range(8)]
    pieces += [(sr, wr, pl.ds(k * 128, 128)) for k in range(8)]
    n = len(pieces)

    def part(p, *index):
        return pieces[p][1].at[(*index, ALL, pieces[p][2])]

    def own(p):
        return pltpu.make_async_copy(pieces[p][0].at[:, pieces[p][2]], part(p, z, y, x, c), own_sem.at[p])

    def send(p, slot, ref, to):
        return pltpu.make_async_remote_copy(
            ref, ref, ssem.at[p, slot], rsem.at[p, slot], device_id=to, device_id_type=MESH
        )

    def copies(p, core, stage):
        if stage == 3:
            return [send(p, 5, part(p, ALL, ALL, ALL, c), device(z, y, x, 1 - c))]
        order = GATHER_ORDER[core]
        done, axis = order[:stage], order[stage]
        here = dict(z=z, y=y, x=x)
        ref = part(p, *[ALL if a in done else here[a] for a in "zyx"], c)
        if axis == "z":
            return [send(p, k - 1, ref, device(lax.rem(z + k, 4), y, x, c)) for k in (1, 2, 3)]
        if axis == "y":
            return [send(p, 3, ref, device(z, 1 - y, x, c))]
        return [send(p, 4, ref, device(z, y, 1 - x, c))]

    for p in range(n):
        own(p).start()
    meet(z, y, x, c)

    def run(core):
        events = sorted((p + GATHER_LAGS[stage], -stage, p) for p in range(n) for stage in range(5))
        for _, negative, p in events:
            stage = -negative
            if stage == 0:
                own(p).wait()
            else:
                for copy in copies(p, core, stage - 1):
                    copy.wait_recv()
            if stage < 4:
                for copy in copies(p, core, stage):
                    copy.start()
        for p in range(n):
            for stage in range(4):
                for copy in copies(p, core, stage):
                    copy.wait_send()

    pl.when(c == 0)(lambda: run(0))
    pl.when(c == 1)(lambda: run(1))


def gather_weights(sa, sm, se, sr):
    n = 24
    outs = pl.pallas_call(
        gather_kernel,
        out_shape=(
            jax.ShapeDtypeStruct((3, 4, 2, 2, 2, 32, D), bf16),
            jax.ShapeDtypeStruct((4, 2, 2, 2, 32, D), bf16),
            jax.ShapeDtypeStruct((4, 2, 2, 2, 32, FF), bf16),
            jax.ShapeDtypeStruct((4, 2, 2, 2, 128, D), bf16),
        ),
        in_specs=[pl.BlockSpec(memory_space=pltpu.VMEM)] * 4,
        out_specs=[pl.BlockSpec(memory_space=pl.ANY)] * 4,
        scratch_shapes=[
            pltpu.SemaphoreType.DMA((n,)),
            pltpu.SemaphoreType.DMA((n, 6)),
            pltpu.SemaphoreType.DMA((n, 6)),
        ],
        compiler_params=pltpu.CompilerParams(collective_id=1, has_side_effects=True),
        name="gather_weights",
    )(sa, sm, se, sr)
    wa, wm, we, wr = outs
    return wa.reshape(3, D, D), wm.reshape(D, D), we.reshape(D, FF), wr.reshape(FF, D)


def scatter_kernel(
    ga, gm, ge, gr, oa, om, oe, out_r,
    h, r1, r2, r3, r4, h2, h3, fin, th, t1, t2, t3, t4, th2, th3, tfin,
    own_sem, out_sem, ssem, rsem,
):
    z, y, x, c = place()
    src = [(gr, pl.ds(j * 256, 256)) for j in range(4)] + [(ge, pl.ds(j * 1024, 1024)) for j in range(4)]
    src += [(gm, ALL)] + [(ga.at[i], ALL) for i in range(3)]
    dst = [out_r.at[:, pl.ds(j * 256, 256)] for j in range(4)] + [oe.at[:, pl.ds(j * 1024, 1024)] for j in range(4)]
    dst += [om] + [oa.at[i] for i in range(3)]
    n = 12
    tall = (th, t1, t2, t3, t4, th2, th3, tfin)
    wide = (h, r1, r2, r3, r4, h2, h3, fin)
    held = [[r.at[p] for r in tall] if p < 4 else [r.at[p - 4] for r in wide] for p in range(n)]

    def own(p):
        ref, cols = src[p]
        return pltpu.make_async_copy(ref.at[:, :, :, c, :, cols], held[p][0], own_sem.at[p])

    def out(p):
        return pltpu.make_async_copy(held[p][7], dst[p], out_sem.at[p])

    def send(p, slot, a, b, to):
        return pltpu.make_async_remote_copy(
            a, b, ssem.at[p, slot], rsem.at[p, slot], device_id=to, device_id_type=MESH
        )

    def copies(p, core, stage):
        H, R1, R2, R3, R4, H2, H3, F = held[p]
        ref, cols = src[p]
        if stage == 0:
            return [send(p, 0, ref.at[:, :, :, 1 - c, :, cols], R1, device(z, y, x, 1 - c))]
        up = [lax.rem(z + k, 4) for k in (1, 2, 3)]
        if core == 0:
            if stage == 1:
                return [send(p, 1, H.at[:, :, 1 - x], R2, device(z, y, 1 - x, c))]
            if stage == 2:
                return [send(p, 2, H2.at[:, 1 - y], R3.at[pl.ds(0, 4)], device(z, 1 - y, x, c))]
            return [send(p, 3 + k, H3.at[up[k]], R4.at[k], device(up[k], y, x, c)) for k in range(3)]
        if stage == 1:
            return [send(p, 1, H.at[:, 1 - y], R2, device(z, 1 - y, x, c))]
        if stage == 2:
            return [send(p, 3 + k, H2.at[up[k]], R3.at[pl.ds(2 * k, 2)], device(up[k], y, x, c)) for k in range(3)]
        return [send(p, 2, H3.at[1 - x], R4.at[0], device(z, y, 1 - x, c))]

    def wide_of(v):
        return v.astype(f32)

    def add(p, core, stage):
        H, R1, R2, R3, R4, H2, H3, F = held[p]
        if stage == 0:

            @pl.loop(0, 16)
            def _(i):
                a, b, d = i // 4, (i // 2) % 2, i % 2
                H[a, b, d] = (wide_of(H[a, b, d]) + wide_of(R1[a, b, d])).astype(bf16)

        elif stage == 1:

            @pl.loop(0, 8)
            def _(i):
                a, b = i // 2, i % 2
                mine = H[a, b, x] if core == 0 else H[a, y, b]
                H2[a, b] = (wide_of(mine) + wide_of(R2[a, b])).astype(bf16)

        elif stage == 2 and core == 0:

            @pl.loop(0, 4)
            def _(a):
                H3[a] = (wide_of(H2[a, y]) + wide_of(R3[a])).astype(bf16)

        elif stage == 2:

            @pl.loop(0, 2)
            def _(a):
                H3[a] = (wide_of(H2[z, a]) + wide_of(R3[a]) + wide_of(R3[2 + a]) + wide_of(R3[4 + a])).astype(bf16)

        elif core == 0:
            F[...] = wide_of(H3[z]) + wide_of(R4[0]) + wide_of(R4[1]) + wide_of(R4[2])
        else:
            F[...] = wide_of(H3[x]) + wide_of(R4[0])

    for p in range(n):
        own(p).start()
    meet(z, y, x, c)

    def run(core):
        for t in range(n + 4):
            if t < n:
                for copy in copies(t, core, 0):
                    copy.start()
            for stage in range(4):
                p = t - 1 - stage
                if 0 <= p < n:
                    if stage == 0:
                        own(p).wait()
                    for copy in copies(p, core, stage):
                        copy.wait_recv()
                    add(p, core, stage)
                    if stage < 3:
                        for copy in copies(p, core, stage + 1):
                            copy.start()
                    else:
                        out(p).start()
        for p in range(n):
            out(p).wait()
            for stage in range(4):
                for copy in copies(p, core, stage):
                    copy.wait_send()

    pl.when(c == 0)(lambda: run(0))
    pl.when(c == 1)(lambda: run(1))


def scatter_gradients(ga, gm, ge, gr):
    n = 12

    def buffers(k, r, w):
        blocks = [(4, 2, 2), (4, 2, 2), (4, 2), (6,), (3,), (4, 2), (4,)]
        return [pltpu.VMEM((k, *b, r, w), bf16) for b in blocks] + [pltpu.VMEM((k, r, w), f32)]

    return pl.pallas_call(
        scatter_kernel,
        out_shape=(
            jax.ShapeDtypeStruct((3, 32, D), f32),
            jax.ShapeDtypeStruct((32, D), f32),
            jax.ShapeDtypeStruct((32, FF), f32),
            jax.ShapeDtypeStruct((128, D), f32),
        ),
        in_specs=[pl.BlockSpec(memory_space=pl.ANY)] * 4,
        out_specs=[pl.BlockSpec(memory_space=pl.ANY)] * 4,
        scratch_shapes=buffers(8, 32, 1024)
        + buffers(4, 128, 256)
        + [
            pltpu.SemaphoreType.DMA((n,)),
            pltpu.SemaphoreType.DMA((n,)),
            pltpu.SemaphoreType.DMA((n, 6)),
            pltpu.SemaphoreType.DMA((n, 6)),
        ],
        compiler_params=pltpu.CompilerParams(
            collective_id=2, has_side_effects=True, vmem_limit_bytes=60 * 1024 * 1024
        ),
        name="scatter_gradients",
    )(
        ga.reshape(3, 4, 2, 2, 2, 32, D),
        gm.reshape(4, 2, 2, 2, 32, D),
        ge.reshape(4, 2, 2, 2, 32, FF),
        gr.reshape(4, 2, 2, 2, 128, D),
    )


def product(left_side, right_side):
    return jnp.einsum("sri,ij->srj", left_side, right_side, preferred_element_type=f32)


def product_back(gradient, right_side):
    return jnp.einsum("srj,ij->sri", gradient, right_side, preferred_element_type=f32)


def outer_sum(left_side, gradient):
    return jnp.einsum("sri,srj->ij", left_side, gradient, preferred_element_type=f32)


def sum_rows(tensor):
    return jnp.sum(tensor.astype(f32), axis=(0, 1))


def split_heads(tensor):
    return tensor.reshape(tensor.shape[0], tensor.shape[1], -1, HD)


def norm_forward(tensor, gain, shift):
    center = tensor - jnp.mean(tensor, axis=-1, keepdims=True)
    spread = jnp.mean(center * center, axis=-1, keepdims=True)
    factor = lax.rsqrt(spread + norm_eps)
    normed = center * factor
    return (normed * gain + shift, normed, factor)


def norm_backward(gradient, normed, factor, gain):
    grad_normed = gradient * gain
    return factor * (
        grad_normed
        - jnp.mean(grad_normed, axis=-1, keepdims=True)
        - normed * jnp.mean(grad_normed * normed, axis=-1, keepdims=True)
    )


def attention_core(queries, keys, values, key_valid):
    score_scale = HD ** (-0.5)
    scores = (
        jnp.einsum("sqhd,skhd->shqk", split_heads(queries), split_heads(keys), preferred_element_type=f32)
        * score_scale
    )
    scores = jnp.where(key_valid[:, None, None, :], scores, masked_score)
    row_peak = jnp.max(scores, axis=-1, keepdims=True)
    row_sum = jnp.sum(jnp.exp(scores - row_peak), axis=-1, keepdims=True)
    shares = jnp.exp(scores - (row_peak + jnp.log(row_sum)))
    shares_low = shares.astype(bf16)
    blended = jnp.einsum("shqk,skhd->sqhd", shares_low, split_heads(values), preferred_element_type=f32)
    blended = blended.reshape(queries.shape).astype(bf16)
    return (blended, shares, shares_low)


def attention_back(grad_blended, queries, keys, values, shares, shares_low):
    score_scale = HD ** (-0.5)
    heads_grad = split_heads(grad_blended)
    grad_shares = jnp.einsum("sqhd,skhd->shqk", heads_grad, split_heads(values), preferred_element_type=f32)
    share_dot = jnp.sum(shares * grad_shares, axis=-1, keepdims=True)
    grad_scores = (shares * (grad_shares - share_dot)).astype(bf16)
    grad_query = (
        jnp.einsum("shqk,skhd->sqhd", grad_scores, split_heads(keys), preferred_element_type=f32) * score_scale
    )
    key_part = (
        jnp.einsum("shqk,sqhd->skhd", grad_scores, split_heads(queries), preferred_element_type=f32) * score_scale
    )
    value_part = jnp.einsum("shqk,sqhd->skhd", shares_low, heads_grad, preferred_element_type=f32)
    return (
        grad_query.reshape(queries.shape).astype(bf16),
        key_part.reshape(keys.shape).astype(bf16),
        value_part.reshape(values.shape).astype(bf16),
    )


def adam_update(weight, first, second, gradient, rate, decay):
    first_new = beta_one * first + (1.0 - beta_one) * gradient
    second_new = beta_two * second + (1.0 - beta_two) * gradient * gradient
    first_hat = first_new / (1.0 - beta_one**STEP)
    second_hat = second_new / (1.0 - beta_two**STEP)
    weight_new = weight - rate * (first_hat / (jnp.sqrt(second_hat) + adam_eps) + decay * weight)
    return (first_new, second_new, weight_new)


def local(fast, inputs, cotangent, lengths, *states):
    masters, firsts, seconds = states[0::3], states[1::3], states[2::3]
    attend_low, mixing_low, expand_low, reduce_low = [w.astype(bf16) for w in masters[:4]]
    if fast:
        attend_full, mixing_full, expand_full, reduce_full = gather_weights(
            attend_low, mixing_low, expand_low, reduce_low
        )
    else:
        attend_full = lax.all_gather(attend_low, ("dp", "shard"), axis=1, tiled=True)
        mixing_full, expand_full, reduce_full = [
            lax.all_gather(w, ("dp", "shard"), axis=0, tiled=True) for w in (mixing_low, expand_low, reduce_low)
        ]
    vec = lax.all_gather(masters[4].astype(bf16), ("dp", "shard"), axis=1, tiled=True).astype(f32)

    block_in = lax.all_to_all(inputs, "shard", split_axis=0, concat_axis=1, tiled=True)
    block_cot = lax.all_to_all(cotangent, "shard", split_axis=0, concat_axis=1, tiled=True)
    count, length = block_in.shape[0], block_in.shape[1]
    used = lax.dynamic_slice_in_dim(lengths, lax.axis_index("shard") * count, count)
    valid = jnp.arange(length)[None, :] < used[:, None]
    row_valid = valid.astype(f32)

    queries = (product(block_in, attend_full[0]) + vec[0]).astype(bf16)
    keys = product(block_in, attend_full[1]).astype(bf16)
    values = (product(block_in, attend_full[2]) + vec[1]).astype(bf16)
    blended, shares, shares_low = attention_core(queries, keys, values, valid)
    attended = product(blended, mixing_full) + vec[2]
    settled, normed_one, factor_one = norm_forward(block_in.astype(f32) + attended, vec[3], vec[4])
    settled_low = settled.astype(bf16)
    expanded = product(settled_low, expand_full) + vec[8:].reshape(FF)
    activated = jax.nn.gelu(expanded, approximate=False).astype(bf16)
    contracted = product(activated, reduce_full) + vec[7]
    finished, normed_two, factor_two = norm_forward(settled + contracted, vec[5], vec[6])
    result = (finished * row_valid[:, :, None]).astype(bf16)
    result = lax.all_to_all(result, "shard", split_axis=1, concat_axis=0, tiled=True)

    grad_out = block_cot.astype(f32) * row_valid[:, :, None]
    gain_two = sum_rows(grad_out * normed_two)
    shift_two = sum_rows(grad_out)
    grad_two = norm_backward(grad_out, normed_two, factor_two, vec[5])
    grad_contract = grad_two.astype(bf16)
    grad_reduce = outer_sum(activated, grad_contract)
    bias_reduce = sum_rows(grad_contract)
    grad_active = product_back(grad_contract, reduce_full)
    gelu_pull = jax.vjp(functools.partial(jax.nn.gelu, approximate=False), expanded)[1]
    grad_expanded = gelu_pull(grad_active)[0].astype(bf16)
    grad_expand = outer_sum(settled_low, grad_expanded)
    bias_expand = sum_rows(grad_expanded)
    grad_settled = grad_two + product_back(grad_expanded, expand_full)
    gain_one = sum_rows(grad_settled * normed_one)
    shift_one = sum_rows(grad_settled)
    grad_one = norm_backward(grad_settled, normed_one, factor_one, vec[3])
    grad_attended = grad_one.astype(bf16)
    grad_mixing = outer_sum(blended, grad_attended)
    bias_mixing = sum_rows(grad_attended)
    grad_blended = product_back(grad_attended, mixing_full).astype(bf16)
    query_grad, key_grad, value_grad = attention_back(grad_blended, queries, keys, values, shares, shares_low)
    grad_attend = jnp.stack([outer_sum(block_in, g) for g in (query_grad, key_grad, value_grad)])
    input_gradient = (
        grad_one
        + product_back(query_grad, attend_full[0])
        + product_back(key_grad, attend_full[1])
        + product_back(value_grad, attend_full[2])
    )
    input_gradient = lax.all_to_all(input_gradient, "shard", split_axis=1, concat_axis=0, tiled=True)
    small_rows = [sum_rows(query_grad), sum_rows(value_grad), bias_mixing, gain_one, shift_one, gain_two, shift_two]
    small_rows = jnp.stack([*small_rows, bias_reduce])
    grad_vectors = jnp.concatenate([small_rows, bias_expand.reshape(NV - 8, D)], axis=0)

    if fast:
        reduced = scatter_gradients(*[g.astype(bf16) for g in (grad_attend, grad_mixing, grad_expand, grad_reduce)])
    else:
        reduced = [lax.psum_scatter(grad_attend, ("dp", "shard"), scatter_dimension=1, tiled=True)]
        for g in (grad_mixing, grad_expand, grad_reduce):
            reduced.append(lax.psum_scatter(g, ("dp", "shard"), scatter_dimension=0, tiled=True))
    reduced = (*reduced, lax.psum_scatter(grad_vectors, ("dp", "shard"), scatter_dimension=1, tiled=True))
    updated = []
    for number in range(5):
        decay = matrix_decay if number < 4 else 0.0
        updated += adam_update(
            masters[number], firsts[number], seconds[number], reduced[number], rates[number], decay
        )
    return (result, input_gradient, *updated, reduced[4][2])


def solution(mesh):
    fast = mesh.shape["dp"] == 8 and mesh.shape["shard"] == 4
    rows = P("dp", "shard", None)
    both = ("dp", "shard")
    middle, first, last = P(None, both, None), P(both, None), P(None, both)
    states = [middle] * 3 + [first] * 9 + [last] * 3
    return jax.shard_map(
        functools.partial(local, fast),
        mesh=mesh,
        in_specs=(rows, rows, P("dp"), *states),
        out_specs=(rows, rows, *states, P(both)),
        check_vma=False,
    )
```

```python
import functools

import jax
import jax.numpy as jnp
from jax import lax
from jax.experimental import pallas as pl
from jax.experimental.pallas import tpu as pltpu
from jax.sharding import PartitionSpec as P

D = 1024
HD = 64
FF = 4096
STEP = 10
NV = 12
MESH = pl.DeviceIdType.MESH
ALL = slice(None)

beta_one = 0.9
beta_two = 0.999
adam_eps = 1e-08
norm_eps = 1e-05
matrix_decay = 0.01
masked_score = -1e30
rates = (0.06, 1.0, 0.06, 0.03, 0.5)
bf16 = jnp.bfloat16
f32 = jnp.float32


def place():
    dp = lax.axis_index("dp")
    sh = lax.axis_index("shard")
    return lax.div(dp, 2), lax.rem(dp, 2), lax.div(sh, 2), lax.rem(sh, 2)


def device(z, y, x, c):
    return (z * 2 + y, x * 2 + c)


def meet(z, y, x, c):
    bar = pltpu.get_barrier_semaphore()
    others = [device(z, y, x, 1 - c), device(z, y, 1 - x, c), device(z, 1 - y, x, c)]
    others += [device(lax.rem(z + k, 4), y, x, c) for k in (1, 2, 3)]
    for other in others:
        pl.semaphore_signal(bar, inc=1, device_id=other, device_id_type=MESH)
    pl.semaphore_wait(bar, len(others))


GATHER_ORDER = ("zyx", "zxy")
def scatter_kernel(
    ga, gm, ge, gr, oa, om, oe, out_r,
    h, r1, r2, r3, r4, h2, h3, fin, th, t1, t2, t3, t4, th2, th3, tfin,
    own_sem, out_sem, ssem, rsem,
):
    z, y, x, c = place()
    src = [(gr, pl.ds(j * 256, 256)) for j in range(4)] + [(ge, pl.ds(j * 1024, 1024)) for j in range(4)]
    src += [(gm, ALL)] + [(ga.at[i], ALL) for i in range(3)]
    dst = [out_r.at[:, pl.ds(j * 256, 256)] for j in range(4)] + [oe.at[:, pl.ds(j * 1024, 1024)] for j in range(4)]
    dst += [om] + [oa.at[i] for i in range(3)]
    n = 12
    tall = (th, t1, t2, t3, t4, th2, th3, tfin)
    wide = (h, r1, r2, r3, r4, h2, h3, fin)
    held = [[r.at[p] for r in tall] if p < 4 else [r.at[p - 4] for r in wide] for p in range(n)]

    def own(p):
        ref, cols = src[p]
        return pltpu.make_async_copy(ref.at[:, :, :, c, :, cols], held[p][0], own_sem.at[p])

    def out(p):
        return pltpu.make_async_copy(held[p][7], dst[p], out_sem.at[p])

    def send(p, slot, a, b, to):
        return pltpu.make_async_remote_copy(
            a, b, ssem.at[p, slot], rsem.at[p, slot], device_id=to, device_id_type=MESH
        )

    def copies(p, core, stage):
        H, R1, R2, R3, R4, H2, H3, F = held[p]
        ref, cols = src[p]
        if stage == 0:
            return [send(p, 0, ref.at[:, :, :, 1 - c, :, cols], R1, device(z, y, x, 1 - c))]
        up = [lax.rem(z + k, 4) for k in (1, 2, 3)]
        if core == 0:
            if stage == 1:
                return [send(p, 1, H.at[:, :, 1 - x], R2, device(z, y, 1 - x, c))]
            if stage == 2:
                return [send(p, 2, H2.at[:, 1 - y], R3.at[pl.ds(0, 4)], device(z, 1 - y, x, c))]
            return [send(p, 3 + k, H3.at[up[k]], R4.at[k], device(up[k], y, x, c)) for k in range(3)]
        if stage == 1:
            return [send(p, 1, H.at[:, 1 - y], R2, device(z, 1 - y, x, c))]
        if stage == 2:
            return [send(p, 3 + k, H2.at[up[k]], R3.at[pl.ds(2 * k, 2)], device(up[k], y, x, c)) for k in range(3)]
        return [send(p, 2, H3.at[1 - x], R4.at[0], device(z, y, 1 - x, c))]

    def wide_of(v):
        return v.astype(f32)

    def add(p, core, stage):
        H, R1, R2, R3, R4, H2, H3, F = held[p]
        if stage == 0:

            @pl.loop(0, 16)
            def _(i):
                a, b, d = i // 4, (i // 2) % 2, i % 2
                H[a, b, d] = (wide_of(H[a, b, d]) + wide_of(R1[a, b, d])).astype(bf16)

        elif stage == 1:

            @pl.loop(0, 8)
            def _(i):
                a, b = i // 2, i % 2
                mine = H[a, b, x] if core == 0 else H[a, y, b]
                H2[a, b] = (wide_of(mine) + wide_of(R2[a, b])).astype(bf16)

        elif stage == 2 and core == 0:

            @pl.loop(0, 4)
            def _(a):
                H3[a] = (wide_of(H2[a, y]) + wide_of(R3[a])).astype(bf16)

        elif stage == 2:

            @pl.loop(0, 2)
            def _(a):
                H3[a] = (wide_of(H2[z, a]) + wide_of(R3[a]) + wide_of(R3[2 + a]) + wide_of(R3[4 + a])).astype(bf16)

        elif core == 0:
            F[...] = wide_of(H3[z]) + wide_of(R4[0]) + wide_of(R4[1]) + wide_of(R4[2])
        else:
            F[...] = wide_of(H3[x]) + wide_of(R4[0])

    for p in range(n):
        own(p).start()
    meet(z, y, x, c)

    def run(core):
        for t in range(n + 4):
            if t < n:
                for copy in copies(t, core, 0):
                    copy.start()
            for stage in range(4):
                p = t - 1 - stage
                if 0 <= p < n:
                    if stage == 0:
                        own(p).wait()
                    for copy in copies(p, core, stage):
                        copy.wait_recv()
                    add(p, core, stage)
                    if stage < 3:
                        for copy in copies(p, core, stage + 1):
                            copy.start()
                    else:
                        out(p).start()
        for p in range(n):
            out(p).wait()
            for stage in range(4):
                for copy in copies(p, core, stage):
                    copy.wait_send()

    pl.when(c == 0)(lambda: run(0))
    pl.when(c == 1)(lambda: run(1))


def scatter_gradients(ga, gm, ge, gr):
    n = 12

    def buffers(k, r, w):
        blocks = [(4, 2, 2), (4, 2, 2), (4, 2), (6,), (3,), (4, 2), (4,)]
        return [pltpu.VMEM((k, *b, r, w), bf16) for b in blocks] + [pltpu.VMEM((k, r, w), f32)]

    return pl.pallas_call(
        scatter_kernel,
        out_shape=(
            jax.ShapeDtypeStruct((3, 32, D), f32),
            jax.ShapeDtypeStruct((32, D), f32),
            jax.ShapeDtypeStruct((32, FF), f32),
            jax.ShapeDtypeStruct((128, D), f32),
        ),
        in_specs=[pl.BlockSpec(memory_space=pl.ANY)] * 4,
        out_specs=[pl.BlockSpec(memory_space=pl.ANY)] * 4,
        scratch_shapes=buffers(8, 32, 1024)
        + buffers(4, 128, 256)
        + [
            pltpu.SemaphoreType.DMA((n,)),
            pltpu.SemaphoreType.DMA((n,)),
            pltpu.SemaphoreType.DMA((n, 6)),
            pltpu.SemaphoreType.DMA((n, 6)),
        ],
        compiler_params=pltpu.CompilerParams(
            collective_id=2, has_side_effects=True, vmem_limit_bytes=60 * 1024 * 1024
        ),
        name="scatter_gradients",
    )(
        ga.reshape(3, 4, 2, 2, 2, 32, D),
        gm.reshape(4, 2, 2, 2, 32, D),
        ge.reshape(4, 2, 2, 2, 32, FF),
        gr.reshape(4, 2, 2, 2, 128, D),
    )


def dot(a, b, left=1, right=0):
    return lax.dot_general(a, b, (((left,), (right,)), ((), ())), preferred_element_type=f32)


def when(cond, run):
    if isinstance(cond, bool):
        if cond:
            run()
    else:
        pl.when(cond)(run)


def within(p, low, high):
    if isinstance(p, int):
        return low <= p < high
    return jnp.logical_and(p >= low, p < high)


def gelu_parts(v):
    u = jnp.abs(v) * (0.5**0.5)
    t = 1.0 / (1.0 + 0.3275911 * u)
    bell = jnp.exp(-u * u)
    poly = ((((1.061405429 * t - 1.453152027) * t + 1.421413741) * t - 0.284496736) * t + 0.254829592) * t
    tail = 0.5 * poly * bell
    share = jnp.where(v < 0.0, tail, 1.0 - tail)
    return v * share, share + v * bell * 0.3989422804014327


def forward_kernel(
    sa, sm, se, sr, vt, x_loc, cot_loc, lengths,
    w1h, w2h, vec, x_o, qkv_o, lse_o, bt_o, n1_o, f1_o, sl_o, act_o, gp_o, g2_o, res_o, small_o,
    w1, w2, vg, xs, cots, qkv, bt, bl, att, settled, n1, sl, act, gp, bias3, be3,
    ssem, rsem, wsem, vssem, vrsem, xssem, xrsem, xlsem, osem,
):
    z, y, x, c = place()
    sh = x * 2 + c
    dp = z * 2 + y

    for m in range(3):
        for h in range(2):
            w1[m * 2 + h, z, y, x, c] = sa[m, :, h * 512 : h * 512 + 512].astype(bf16)
    for h in range(2):
        w1[6 + h, z, y, x, c] = sm[:, h * 512 : h * 512 + 512].astype(bf16)
    for j in range(8):
        w1[8 + j, z, y, x, c] = se[:, j * 512 : j * 512 + 512].astype(bf16)
        w2[j, z, y, x, c] = sr[:, j * 128 : j * 128 + 128].astype(bf16)
    vg[z, y, x, c] = vt[...]

    def remote(src, dst, s, r, to):
        return pltpu.make_async_remote_copy(src, dst, s, r, device_id=to, device_id_type=MESH)

    def route(view, core, stage, s, r):
        if stage == 3:
            ref = view(ALL, ALL, ALL, c)
            return [remote(ref, ref, s(5), r(5), device(z, y, x, 1 - c))]
        order = GATHER_ORDER[core]
        done, axis = order[:stage], order[stage]
        here = dict(z=z, y=y, x=x)
        ref = view(*[ALL if a in done else here[a] for a in "zyx"], c)
        if axis == "z":
            up = [lax.rem(z + k, 4) for k in (1, 2, 3)]
            return [remote(ref, ref, s(k), r(k), device(up[k], y, x, c)) for k in range(3)]
        if axis == "y":
            return [remote(ref, ref, s(3), r(3), device(z, 1 - y, x, c))]
        return [remote(ref, ref, s(4), r(4), device(z, y, 1 - x, c))]

    def copies(kind, p, core, stage):
        buf = w1 if kind == 0 else w2
        q = p if kind == 0 else p - 16
        return route(lambda *i: buf.at[(q, *i)], core, stage, lambda k: ssem.at[p, k], lambda k: rsem.at[p, k])

    def vector_copies(core, stage):
        return route(lambda *i: vg.at[i], core, stage, lambda k: vssem.at[k], lambda k: vrsem.at[k])

    def keep(kind, p):
        if kind == 0:
            return pltpu.make_async_copy(w1.at[p], w1h.at[p], wsem.at[p])
        return pltpu.make_async_copy(w2.at[p - 16], w2h.at[p - 16], wsem.at[p])

    def by_core(stage, run):
        if stage in (0, 3):
            run(0)
        else:
            pl.when(c == 0)(lambda: run(0))
            pl.when(c == 1)(lambda: run(1))

    def step(make, stage):
        def arrive(core):
            for copy in make(core, stage - 1):
                copy.wait_recv()

        def leave(core):
            for copy in make(core, stage):
                copy.start()

        if stage > 0:
            by_core(stage - 1, arrive)
        if stage < 4:
            by_core(stage, leave)

    def tick(t):
        for stage in (4, 3, 2, 1, 0):
            p = t - 2 * stage
            for kind, low, high in ((0, 0, 16), (1, 16, 24)):

                def run(kind=kind, p=p, stage=stage):
                    step(lambda core, s: copies(kind, p, core, s), stage)
                    if stage == 4:
                        keep(kind, p).start()

                when(within(p, low, high), run)

    bar = pltpu.get_barrier_semaphore()
    others = [device(z, y, x, 1 - c), device(z, y, 1 - x, c), device(z, y, 1 - x, 1 - c), device(z, 1 - y, x, c)]
    others += [device(lax.rem(z + k, 4), y, x, c) for k in (1, 2, 3)]
    for other in others:
        pl.semaphore_signal(bar, inc=1, device_id=other, device_id_type=MESH)
    pl.semaphore_wait(bar, len(others))

    def exchange(src, dst, which):
        sends = []
        for k in (1, 2, 3):
            to = lax.rem(sh + k, 4)
            sends.append(
                remote(src.at[to], dst.at[sh], xssem.at[which, k - 1], xrsem.at[which, k - 1], (dp, to))
            )
        return sends, pltpu.make_async_copy(src.at[sh], dst.at[sh], xlsem.at[which])

    x_sends, x_own = exchange(x_loc, xs, 0)
    c_sends, c_own = exchange(cot_loc, cots, 1)
    step(vector_copies, 0)
    x_own.start()
    c_own.start()
    for t in range(8):
        tick(t)
        if t in (1, 3, 5):
            step(vector_copies, (t + 1) // 2)
        if t == 0:
            for copy in x_sends:
                copy.start()
    step(vector_copies, 4)
    x_own.wait()
    for copy in x_sends:
        copy.wait_recv()
    used = lengths[sh]

    for g in range(8):
        total = jnp.zeros((16, 128), f32)
        for i in range(4):
            total = total + vg[g // 2, g % 2, i // 2, i % 2].astype(f32)
        vec[:, g * 128 : g * 128 + 128] = total
    for h in range(2):
        bias3[h] = vec[0:1, h * 512 : h * 512 + 512]
        bias3[2 + h] = jnp.zeros((1, 512), f32)
        bias3[4 + h] = vec[1:2, h * 512 : h * 512 + 512]
    for j in range(8):
        be3[j] = vec[8 + j // 2 : 9 + j // 2, (j % 2) * 512 : (j % 2) * 512 + 512]

    outs = []

    def put(src, dst):
        copy = pltpu.make_async_copy(src, dst, osem.at[len(outs)])
        copy.start()
        outs.append(copy)

    put(xs, x_o)

    @pl.loop(0, 6)
    def _(i):
        tick(8 + i)
        cols = pl.ds(pl.multiple_of(lax.rem(i, 2) * 512, 512), 512)
        got = dot(xs[...].reshape(512, D), w1[i].reshape(D, 512)) + bias3[i]
        qkv[lax.div(i, 2), :, cols] = got.astype(bf16)

    put(qkv, qkv_o)
    for copy in c_sends:
        copy.start()

    lane = lax.broadcasted_iota(jnp.int32, (1, 128), 1)
    key_ok = lax.broadcasted_iota(jnp.int32, (512, 1), 0) < used

    @pl.loop(0, 8)
    def _(i):
        tick(14 + i)
        cols = pl.ds(pl.multiple_of(i * 128, 128), 128)
        q2, k2, v2 = qkv[0, :, cols], qkv[1, :, cols], qkv[2, :, cols]
        v_t = v2.T
        for h in range(2):
            mine = (lane < 64) if h == 0 else (lane >= 64)
            qm = jnp.where(mine, q2, jnp.zeros_like(q2))
            for b in range(2):
                s = dot(k2, qm[b * 256 : b * 256 + 256], 1, 1)
                s = jnp.where(key_ok, s * (HD**-0.5), masked_score)
                peak = jnp.max(s, axis=0, keepdims=True)
                e = jnp.exp(s - peak)
                total = jnp.sum(e, axis=0, keepdims=True)
                shares = (e * (1.0 / total)).astype(bf16)
                lse_o[i, h : h + 1, b * 256 : b * 256 + 256] = peak + jnp.log(total)
                mixed = dot(v_t[h * 64 : h * 64 + 64], shares)
                bt[pl.ds(pl.multiple_of(i * 128, 128) + h * 64, 64), b * 256 : b * 256 + 256] = mixed.astype(bf16)
        bl[:, cols] = bt[pl.ds(pl.multiple_of(i * 128, 128), 128), :].T

    put(bt, bt_o)

    @pl.loop(0, 2)
    def _(h):
        cols = pl.ds(pl.multiple_of(h * 512, 512), 512)
        att[:, cols] = dot(bl[...], w1[6 + h].reshape(D, 512))

    @pl.loop(0, 8)
    def _(r):
        rows = pl.ds(pl.multiple_of(r * 64, 64), 64)
        whole = xs[...].reshape(512, D) if False else None
        inp = xs[lax.div(r, 2), pl.ds(pl.multiple_of(lax.rem(r, 2) * 64, 64), 64), :].astype(f32)
        t = inp + (att[rows, :] + vec[2:3, :])
        center = t - jnp.mean(t, axis=-1, keepdims=True)
        factor = lax.rsqrt(jnp.mean(center * center, axis=-1, keepdims=True) + norm_eps)
        normed = center * factor
        out = normed * vec[3:4, :] + vec[4:5, :]
        n1[rows, :] = normed
        f1_o[rows, :] = jnp.broadcast_to(factor, (64, 128))
        settled[rows, :] = out
        sl[rows, :] = out.astype(bf16)

    put(n1, n1_o)
    put(sl, sl_o)

    @pl.loop(0, 8)
    def _(j):
        tick(22 + j)
        cols = pl.ds(pl.multiple_of(j * 512, 512), 512)
        for r in range(2):
            rows = slice(r * 256, r * 256 + 256)
            got = dot(sl[rows, :], w1[8 + j].reshape(D, 512)) + be3[j]
            a, slope = gelu_parts(got)
            act[rows, cols] = a.astype(bf16)
            gp[rows, cols] = slope.astype(bf16)

    put(act, act_o)
    put(gp, gp_o)

    @pl.loop(0, 8)
    def _(j):
        tick(30 + j)
        cols = pl.ds(pl.multiple_of(j * 128, 128), 128)
        att[:, cols] = dot(act[...], w2[j].reshape(FF, 128))

    c_own.wait()
    for copy in c_sends:
        copy.wait_recv()
    small_o[...] = jnp.zeros((8, D), f32)

    @pl.loop(0, 8)
    def _(r):
        rows = pl.ds(pl.multiple_of(r * 64, 64), 64)
        t = settled[rows, :] + (att[rows, :] + vec[7:8, :])
        center = t - jnp.mean(t, axis=-1, keepdims=True)
        factor = lax.rsqrt(jnp.mean(center * center, axis=-1, keepdims=True) + norm_eps)
        normed = center * factor
        ok = (lax.broadcasted_iota(jnp.int32, (64, 1), 0) + r * 64) < used
        finished = jnp.where(ok, normed * vec[5:6, :] + vec[6:7, :], 0.0)
        bl[rows, :] = finished.astype(bf16)
        cot = cots[lax.div(r, 2), pl.ds(pl.multiple_of(lax.rem(r, 2) * 64, 64), 64), :].astype(f32)
        grad = jnp.where(ok, cot, 0.0)
        e = grad * vec[5:6, :]
        pull = jnp.mean(e, axis=-1, keepdims=True) + normed * jnp.mean(e * normed, axis=-1, keepdims=True)
        two = factor * (e - pull)
        settled[rows, :] = two
        small_o[5:6, :] += jnp.sum(grad * normed, axis=0, keepdims=True)
        small_o[6:7, :] += jnp.sum(grad, axis=0, keepdims=True)
        small_o[7:8, :] += jnp.sum(two.astype(bf16).astype(f32), axis=0, keepdims=True)

    put(settled, g2_o)
    put(bl, res_o)

    for copy in outs:
        copy.wait()
    for copy in x_sends + c_sends:
        copy.wait_send()
    for stage in range(4):

        def left(core, stage=stage):
            for copy in vector_copies(core, stage):
                copy.wait_send()

        by_core(stage, left)
    for kind, low, high in ((0, 0, 16), (1, 16, 24)):

        @pl.loop(low, high)
        def _(p):
            for stage in range(4):

                def left(core, stage=stage):
                    for copy in copies(kind, p, core, stage):
                        copy.wait_send()

                by_core(stage, left)
            keep(kind, p).wait()


def forward_pass(sa, sm, se, sr, vt, x_loc, cot_loc, lengths):
    V, S = pltpu.VMEM, jax.ShapeDtypeStruct
    anywhere, vmem = pl.BlockSpec(memory_space=pl.ANY), pl.BlockSpec(memory_space=pltpu.VMEM)
    blocks = (4, 2, 2, 2)
    outs = [
        (S((16, *blocks, 32, 512), bf16), anywhere),
        (S((8, *blocks, 128, 128), bf16), anywhere),
        (S((16, D), f32), vmem),
        (S((4, 128, D), bf16), anywhere),
        (S((3, 512, D), bf16), anywhere),
        (S((8, 2, 512), f32), vmem),
        (S((D, 512), bf16), anywhere),
        (S((512, D), f32), anywhere),
        (S((512, 128), f32), vmem),
        (S((512, D), bf16), anywhere),
        (S((512, FF), bf16), anywhere),
        (S((512, FF), bf16), anywhere),
        (S((512, D), f32), anywhere),
        (S((512, D), bf16), anywhere),
        (S((8, D), f32), vmem),
    ]
    dma = pltpu.SemaphoreType.DMA
    return pl.pallas_call(
        forward_kernel,
        out_shape=[o[0] for o in outs],
        out_specs=[o[1] for o in outs],
        in_specs=[vmem] * 5 + [anywhere] * 2 + [pl.BlockSpec(memory_space=pltpu.SMEM)],
        scratch_shapes=[
            V((16, *blocks, 32, 512), bf16),
            V((8, *blocks, 128, 128), bf16),
            V((*blocks, 16, 128), bf16),
            V((4, 128, D), bf16),
            V((4, 128, D), bf16),
            V((3, 512, D), bf16),
            V((D, 512), bf16),
            V((512, D), bf16),
            V((512, D), f32),
            V((512, D), f32),
            V((512, D), f32),
            V((512, D), bf16),
            V((512, FF), bf16),
            V((512, FF), bf16),
            V((6, 1, 512), f32),
            V((8, 1, 512), f32),
            dma((24, 6)),
            dma((24, 6)),
            dma((24,)),
            dma((6,)),
            dma((6,)),
            dma((2, 3)),
            dma((2, 3)),
            dma((2,)),
            dma((16,)),
        ],
        compiler_params=pltpu.CompilerParams(
            collective_id=1, has_side_effects=True, vmem_limit_bytes=62 * 1024 * 1024
        ),
        name="forward_pass",
    )(sa, sm, se, sr, vt, x_loc, cot_loc, lengths)


def product(left_side, right_side):
    return jnp.einsum("sri,ij->srj", left_side, right_side, preferred_element_type=f32)


def product_back(gradient, right_side):
    return jnp.einsum("srj,ij->sri", gradient, right_side, preferred_element_type=f32)


def outer_sum(left_side, gradient):
    return jnp.einsum("sri,srj->ij", left_side, gradient, preferred_element_type=f32)


def sum_rows(tensor):
    return jnp.sum(tensor.astype(f32), axis=(0, 1))


def split_heads(tensor):
    return tensor.reshape(tensor.shape[0], tensor.shape[1], -1, HD)


def norm_forward(tensor, gain, shift):
    center = tensor - jnp.mean(tensor, axis=-1, keepdims=True)
    spread = jnp.mean(center * center, axis=-1, keepdims=True)
    factor = lax.rsqrt(spread + norm_eps)
    normed = center * factor
    return (normed * gain + shift, normed, factor)


def norm_backward(gradient, normed, factor, gain):
    grad_normed = gradient * gain
    return factor * (
        grad_normed
        - jnp.mean(grad_normed, axis=-1, keepdims=True)
        - normed * jnp.mean(grad_normed * normed, axis=-1, keepdims=True)
    )


def attention_core(queries, keys, values, key_valid):
    score_scale = HD ** (-0.5)
    scores = (
        jnp.einsum("sqhd,skhd->shqk", split_heads(queries), split_heads(keys), preferred_element_type=f32)
        * score_scale
    )
    scores = jnp.where(key_valid[:, None, None, :], scores, masked_score)
    row_peak = jnp.max(scores, axis=-1, keepdims=True)
    row_sum = jnp.sum(jnp.exp(scores - row_peak), axis=-1, keepdims=True)
    shares = jnp.exp(scores - (row_peak + jnp.log(row_sum)))
    shares_low = shares.astype(bf16)
    blended = jnp.einsum("shqk,skhd->sqhd", shares_low, split_heads(values), preferred_element_type=f32)
    blended = blended.reshape(queries.shape).astype(bf16)
    return (blended, shares, shares_low)


def attention_back(grad_blended, queries, keys, values, shares, shares_low):
    score_scale = HD ** (-0.5)
    heads_grad = split_heads(grad_blended)
    grad_shares = jnp.einsum("sqhd,skhd->shqk", heads_grad, split_heads(values), preferred_element_type=f32)
    share_dot = jnp.sum(shares * grad_shares, axis=-1, keepdims=True)
    grad_scores = (shares * (grad_shares - share_dot)).astype(bf16)
    grad_query = (
        jnp.einsum("shqk,skhd->sqhd", grad_scores, split_heads(keys), preferred_element_type=f32) * score_scale
    )
    key_part = (
        jnp.einsum("shqk,sqhd->skhd", grad_scores, split_heads(queries), preferred_element_type=f32) * score_scale
    )
    value_part = jnp.einsum("shqk,sqhd->skhd", shares_low, heads_grad, preferred_element_type=f32)
    return (
        grad_query.reshape(queries.shape).astype(bf16),
        key_part.reshape(keys.shape).astype(bf16),
        value_part.reshape(values.shape).astype(bf16),
    )


def adam_update(weight, first, second, gradient, rate, decay):
    first_new = beta_one * first + (1.0 - beta_one) * gradient
    second_new = beta_two * second + (1.0 - beta_two) * gradient * gradient
    first_hat = first_new / (1.0 - beta_one**STEP)
    second_hat = second_new / (1.0 - beta_two**STEP)
    weight_new = weight - rate * (first_hat / (jnp.sqrt(second_hat) + adam_eps) + decay * weight)
    return (first_new, second_new, weight_new)


def finish(result, input_gradient, masters, firsts, seconds, reduced):
    updated = []
    for number in range(5):
        decay = matrix_decay if number < 4 else 0.0
        updated += adam_update(
            masters[number], firsts[number], seconds[number], reduced[number], rates[number], decay
        )
    return (result, input_gradient, *updated, reduced[4][2])


def local_fast(inputs, cotangent, lengths, *states):
    masters, firsts, seconds = states[0::3], states[1::3], states[2::3]
    mine = lax.rem(lax.axis_index("shard"), 4)
    tile = jnp.tile(jnp.pad(masters[4], ((0, 4), (0, 0))), (1, 4))
    tile = jnp.where(jnp.arange(128)[None, :] // 32 == mine, tile, 0.0).astype(bf16)
    (w1, w2, vec, block_in, qkv, lse, blended_t, normed_one, factor_one, settled_low, activated, slope, grad_two, result, small) = (
        forward_pass(*masters[:4], tile, inputs, cotangent, lengths)
    )
    w1 = w1.reshape(16, D, 512)
    attend_full = jnp.stack([jnp.concatenate([w1[2 * m], w1[2 * m + 1]], axis=1) for m in range(3)])
    mixing_full = jnp.concatenate([w1[6], w1[7]], axis=1)
    expand_full = jnp.concatenate([w1[8 + j] for j in range(8)], axis=1)
    w2 = w2.reshape(8, FF, 128)
    reduce_full = jnp.concatenate([w2[j] for j in range(8)], axis=1)
    block_in = block_in.reshape(1, 512, D)
    queries, keys, values = qkv[0][None], qkv[1][None], qkv[2][None]
    used = lax.dynamic_slice_in_dim(lengths, lax.axis_index("shard"), 1)
    valid = jnp.arange(512)[None, :] < used[:, None]
    _, shares, shares_low = attention_core(queries, keys, values, valid)
    blended = blended_t.T[None]
    settled_low, activated, grad_two, normed_one = [t[None] for t in (settled_low, activated, grad_two, normed_one)]
    factor_one = factor_one[None, :, :1]
    result = lax.all_to_all(result[None], "shard", split_axis=1, concat_axis=0, tiled=True)

    grad_contract = grad_two.astype(bf16)
    grad_reduce = outer_sum(activated, grad_contract)
    grad_active = product_back(grad_contract, reduce_full)
    grad_expanded = (grad_active * slope[None].astype(f32)).astype(bf16)
    grad_expand = outer_sum(settled_low, grad_expanded)
    bias_expand = sum_rows(grad_expanded)
    grad_settled = grad_two + product_back(grad_expanded, expand_full)
    gain_one = sum_rows(grad_settled * normed_one)
    shift_one = sum_rows(grad_settled)
    grad_one = norm_backward(grad_settled, normed_one, factor_one, vec[3])
    grad_attended = grad_one.astype(bf16)
    grad_mixing = outer_sum(blended, grad_attended)
    bias_mixing = sum_rows(grad_attended)
    grad_blended = product_back(grad_attended, mixing_full).astype(bf16)
    query_grad, key_grad, value_grad = attention_back(grad_blended, queries, keys, values, shares, shares_low)
    grad_attend = jnp.stack([outer_sum(block_in, g) for g in (query_grad, key_grad, value_grad)])
    input_gradient = (
        grad_one
        + product_back(query_grad, attend_full[0])
        + product_back(key_grad, attend_full[1])
        + product_back(value_grad, attend_full[2])
    )
    input_gradient = lax.all_to_all(input_gradient, "shard", split_axis=1, concat_axis=0, tiled=True)
    small_rows = [sum_rows(query_grad), sum_rows(value_grad), bias_mixing, gain_one, shift_one, *small[5:8]]
    grad_vectors = jnp.concatenate([jnp.stack(small_rows), bias_expand.reshape(NV - 8, D)], axis=0)
    reduced = scatter_gradients(*[g.astype(bf16) for g in (grad_attend, grad_mixing, grad_expand, grad_reduce)])
    reduced = (*reduced, lax.psum_scatter(grad_vectors, ("dp", "shard"), scatter_dimension=1, tiled=True))
    return finish(result, input_gradient, masters, firsts, seconds, reduced)


def local_any(inputs, cotangent, lengths, *states):
    masters, firsts, seconds = states[0::3], states[1::3], states[2::3]
    attend_low, mixing_low, expand_low, reduce_low = [w.astype(bf16) for w in masters[:4]]
    attend_full = lax.all_gather(attend_low, ("dp", "shard"), axis=1, tiled=True)
    mixing_full, expand_full, reduce_full = [
        lax.all_gather(w, ("dp", "shard"), axis=0, tiled=True) for w in (mixing_low, expand_low, reduce_low)
    ]
    vec = lax.all_gather(masters[4].astype(bf16), ("dp", "shard"), axis=1, tiled=True).astype(f32)

    block_in = lax.all_to_all(inputs, "shard", split_axis=0, concat_axis=1, tiled=True)
    block_cot = lax.all_to_all(cotangent, "shard", split_axis=0, concat_axis=1, tiled=True)
    count, length = block_in.shape[0], block_in.shape[1]
    used = lax.dynamic_slice_in_dim(lengths, lax.axis_index("shard") * count, count)
    valid = jnp.arange(length)[None, :] < used[:, None]
    row_valid = valid.astype(f32)

    queries = (product(block_in, attend_full[0]) + vec[0]).astype(bf16)
    keys = product(block_in, attend_full[1]).astype(bf16)
    values = (product(block_in, attend_full[2]) + vec[1]).astype(bf16)
    blended, shares, shares_low = attention_core(queries, keys, values, valid)
    attended = product(blended, mixing_full) + vec[2]
    settled, normed_one, factor_one = norm_forward(block_in.astype(f32) + attended, vec[3], vec[4])
    settled_low = settled.astype(bf16)
    expanded = product(settled_low, expand_full) + vec[8:].reshape(FF)
    activated = jax.nn.gelu(expanded, approximate=False).astype(bf16)
    contracted = product(activated, reduce_full) + vec[7]
    finished, normed_two, factor_two = norm_forward(settled + contracted, vec[5], vec[6])
    result = (finished * row_valid[:, :, None]).astype(bf16)
    result = lax.all_to_all(result, "shard", split_axis=1, concat_axis=0, tiled=True)

    grad_out = block_cot.astype(f32) * row_valid[:, :, None]
    gain_two = sum_rows(grad_out * normed_two)
    shift_two = sum_rows(grad_out)
    grad_two = norm_backward(grad_out, normed_two, factor_two, vec[5])
    grad_contract = grad_two.astype(bf16)
    grad_reduce = outer_sum(activated, grad_contract)
    bias_reduce = sum_rows(grad_contract)
    grad_active = product_back(grad_contract, reduce_full)
    gelu_pull = jax.vjp(functools.partial(jax.nn.gelu, approximate=False), expanded)[1]
    grad_expanded = gelu_pull(grad_active)[0].astype(bf16)
    grad_expand = outer_sum(settled_low, grad_expanded)
    bias_expand = sum_rows(grad_expanded)
    grad_settled = grad_two + product_back(grad_expanded, expand_full)
    gain_one = sum_rows(grad_settled * normed_one)
    shift_one = sum_rows(grad_settled)
    grad_one = norm_backward(grad_settled, normed_one, factor_one, vec[3])
    grad_attended = grad_one.astype(bf16)
    grad_mixing = outer_sum(blended, grad_attended)
    bias_mixing = sum_rows(grad_attended)
    grad_blended = product_back(grad_attended, mixing_full).astype(bf16)
    query_grad, key_grad, value_grad = attention_back(grad_blended, queries, keys, values, shares, shares_low)
    grad_attend = jnp.stack([outer_sum(block_in, g) for g in (query_grad, key_grad, value_grad)])
    input_gradient = (
        grad_one
        + product_back(query_grad, attend_full[0])
        + product_back(key_grad, attend_full[1])
        + product_back(value_grad, attend_full[2])
    )
    input_gradient = lax.all_to_all(input_gradient, "shard", split_axis=1, concat_axis=0, tiled=True)
    small_rows = [sum_rows(query_grad), sum_rows(value_grad), bias_mixing, gain_one, shift_one, gain_two, shift_two]
    small_rows = jnp.stack([*small_rows, bias_reduce])
    grad_vectors = jnp.concatenate([small_rows, bias_expand.reshape(NV - 8, D)], axis=0)

    reduced = [lax.psum_scatter(grad_attend, ("dp", "shard"), scatter_dimension=1, tiled=True)]
    for g in (grad_mixing, grad_expand, grad_reduce):
        reduced.append(lax.psum_scatter(g, ("dp", "shard"), scatter_dimension=0, tiled=True))
    reduced = (*reduced, lax.psum_scatter(grad_vectors, ("dp", "shard"), scatter_dimension=1, tiled=True))
    return finish(result, input_gradient, masters, firsts, seconds, reduced)


def solution(mesh):
    fast = mesh.shape["dp"] == 8 and mesh.shape["shard"] == 4
    rows = P("dp", "shard", None)
    both = ("dp", "shard")
    middle, first, last = P(None, both, None), P(both, None), P(None, both)
    states = [middle] * 3 + [first] * 9 + [last] * 3
    return jax.shard_map(
        local_fast if fast else local_any,
        mesh=mesh,
        in_specs=(rows, rows, P("dp"), *states),
        out_specs=(rows, rows, *states, P(both)),
        check_vma=False,
    )
```

```python
import functools

import jax
import jax.numpy as jnp
from jax import lax
from jax.experimental import pallas as pl
from jax.experimental.pallas import tpu as pltpu
from jax.sharding import PartitionSpec as P

D = 1024
HD = 64
FF = 4096
STEP = 10
NV = 12
MESH = pl.DeviceIdType.MESH
ALL = slice(None)

beta_one = 0.9
beta_two = 0.999
adam_eps = 1e-08
norm_eps = 1e-05
matrix_decay = 0.01
masked_score = -1e30
rates = (0.06, 1.0, 0.06, 0.03, 0.5)
bf16 = jnp.bfloat16
f32 = jnp.float32


def place():
    dp = lax.axis_index("dp")
    sh = lax.axis_index("shard")
    return lax.div(dp, 2), lax.rem(dp, 2), lax.div(sh, 2), lax.rem(sh, 2)


def device(z, y, x, c):
    return (z * 2 + y, x * 2 + c)


def meet(z, y, x, c):
    bar = pltpu.get_barrier_semaphore()
    others = [device(z, y, x, 1 - c), device(z, y, 1 - x, c), device(z, 1 - y, x, c)]
    others += [device(lax.rem(z + k, 4), y, x, c) for k in (1, 2, 3)]
    for other in others:
        pl.semaphore_signal(bar, inc=1, device_id=other, device_id_type=MESH)
    pl.semaphore_wait(bar, len(others))


GATHER_ORDER = ("zyx", "zxy")


def dot(a, b, left=1, right=0):
    return lax.dot_general(a, b, (((left,), (right,)), ((), ())), preferred_element_type=f32)


def when(cond, run):
    if isinstance(cond, bool):
        if cond:
            run()
    else:
        pl.when(cond)(run)


def within(p, low, high):
    if isinstance(p, int):
        return low <= p < high
    return jnp.logical_and(p >= low, p < high)


def gelu_parts(v):
    u = jnp.abs(v) * (0.5**0.5)
    t = 1.0 / (1.0 + 0.3275911 * u)
    bell = jnp.exp(-u * u)
    poly = ((((1.061405429 * t - 1.453152027) * t + 1.421413741) * t - 0.284496736) * t + 0.254829592) * t
    tail = 0.5 * poly * bell
    share = jnp.where(v < 0.0, tail, 1.0 - tail)
    return v * share, share + v * bell * 0.3989422804014327


def forward_kernel(
    sa, sm, se, sr, vt, x_loc, cot_loc, lengths,
    w1h, w2h, vec, xt_o, qkv_o, lse_o, bt_o, n1_o, f1_o, slt_o, act_o, gp_o, g2_o, res_o, small_o,
    w1, w2, vg, xs, cots, qkv, bt, bl, att, settled, n1, sl, act, gp, xt, slt, bias3, be3,
    ssem, rsem, wsem, vssem, vrsem, xssem, xrsem, xlsem, osem,
):
    z, y, x, c = place()
    sh = x * 2 + c
    dp = z * 2 + y

    for m in range(3):
        for h in range(2):
            w1[m * 2 + h, z, y, x, c] = sa[m, :, h * 512 : h * 512 + 512].astype(bf16)
    for h in range(2):
        w1[6 + h, z, y, x, c] = sm[:, h * 512 : h * 512 + 512].astype(bf16)
    for j in range(8):
        w1[8 + j, z, y, x, c] = se[:, j * 512 : j * 512 + 512].astype(bf16)
        w2[j, z, y, x, c] = sr[:, j * 128 : j * 128 + 128].astype(bf16)
    vg[z, y, x, c] = vt[...]

    def remote(src, dst, s, r, to):
        return pltpu.make_async_remote_copy(src, dst, s, r, device_id=to, device_id_type=MESH)

    def route(view, core, stage, s, r):
        if stage == 3:
            ref = view(ALL, ALL, ALL, c)
            return [remote(ref, ref, s(5), r(5), device(z, y, x, 1 - c))]
        order = GATHER_ORDER[core]
        done, axis = order[:stage], order[stage]
        here = dict(z=z, y=y, x=x)
        ref = view(*[ALL if a in done else here[a] for a in "zyx"], c)
        if axis == "z":
            up = [lax.rem(z + k, 4) for k in (1, 2, 3)]
            return [remote(ref, ref, s(k), r(k), device(up[k], y, x, c)) for k in range(3)]
        if axis == "y":
            return [remote(ref, ref, s(3), r(3), device(z, 1 - y, x, c))]
        return [remote(ref, ref, s(4), r(4), device(z, y, 1 - x, c))]

    def copies(kind, p, core, stage):
        buf = w1 if kind == 0 else w2
        q = p if kind == 0 else p - 16
        return route(lambda *i: buf.at[(q, *i)], core, stage, lambda k: ssem.at[p, k], lambda k: rsem.at[p, k])

    def vector_copies(core, stage):
        return route(lambda *i: vg.at[i], core, stage, lambda k: vssem.at[k], lambda k: vrsem.at[k])

    def keep(kind, p):
        if kind == 0:
            return pltpu.make_async_copy(w1.at[p], w1h.at[p], wsem.at[p])
        cols = pl.ds((p - 16) * 128 if isinstance(p, int) else pl.multiple_of((p - 16) * 128, 128), 128)
        return pltpu.make_async_copy(w2.at[p - 16], w2h.at[:, :, :, :, :, cols], wsem.at[p])

    def by_core(stage, run):
        if stage in (0, 3):
            run(0)
        else:
            pl.when(c == 0)(lambda: run(0))
            pl.when(c == 1)(lambda: run(1))

    def step(make, stage):
        def arrive(core):
            for copy in make(core, stage - 1):
                copy.wait_recv()

        def leave(core):
            for copy in make(core, stage):
                copy.start()

        if stage > 0:
            by_core(stage - 1, arrive)
        if stage < 4:
            by_core(stage, leave)

    def tick(t):
        for stage in (4, 3, 2, 1, 0):
            p = t - 2 * stage
            for kind, low, high in ((0, 0, 16), (1, 16, 24)):

                def run(kind=kind, p=p, stage=stage):
                    step(lambda core, s: copies(kind, p, core, s), stage)
                    if stage == 4:
                        keep(kind, p).start()

                when(within(p, low, high), run)

    bar = pltpu.get_barrier_semaphore()
    others = [device(z, y, x, 1 - c), device(z, y, 1 - x, c), device(z, y, 1 - x, 1 - c), device(z, 1 - y, x, c)]
    others += [device(lax.rem(z + k, 4), y, x, c) for k in (1, 2, 3)]
    for other in others:
        pl.semaphore_signal(bar, inc=1, device_id=other, device_id_type=MESH)
    pl.semaphore_wait(bar, len(others))

    def exchange(src, dst, which):
        sends = []
        for k in (1, 2, 3):
            to = lax.rem(sh + k, 4)
            sends.append(
                remote(src.at[to], dst.at[sh], xssem.at[which, k - 1], xrsem.at[which, k - 1], (dp, to))
            )
        return sends, pltpu.make_async_copy(src.at[sh], dst.at[sh], xlsem.at[which])

    x_sends, x_own = exchange(x_loc, xs, 0)
    c_sends, c_own = exchange(cot_loc, cots, 1)
    step(vector_copies, 0)
    x_own.start()
    c_own.start()
    for t in range(8):
        tick(t)
        if t in (1, 3, 5):
            step(vector_copies, (t + 1) // 2)
        if t == 0:
            for copy in x_sends:
                copy.start()
    step(vector_copies, 4)
    x_own.wait()
    for copy in x_sends:
        copy.wait_recv()
    used = lengths[sh]

    for g in range(8):
        total = jnp.zeros((16, 128), f32)
        for i in range(4):
            total = total + vg[g // 2, g % 2, i // 2, i % 2].astype(f32)
        vec[:, g * 128 : g * 128 + 128] = total
    for h in range(2):
        bias3[h] = vec[0:1, h * 512 : h * 512 + 512]
        bias3[2 + h] = jnp.zeros((1, 512), f32)
        bias3[4 + h] = vec[1:2, h * 512 : h * 512 + 512]
    for j in range(8):
        be3[j] = vec[8 + j // 2 : 9 + j // 2, (j % 2) * 512 : (j % 2) * 512 + 512]

    outs = []

    def put(src, dst):
        copy = pltpu.make_async_copy(src, dst, osem.at[len(outs)])
        copy.start()
        outs.append(copy)

    @pl.loop(0, 8)
    def _(i):
        cols = pl.ds(pl.multiple_of(i * 128, 128), 128)
        for b in range(4):
            xt[cols, b * 128 : b * 128 + 128] = xs[b, :, cols].T

    put(xt, xt_o)

    @pl.loop(0, 6)
    def _(i):
        tick(8 + i)
        cols = pl.ds(pl.multiple_of(lax.rem(i, 2) * 512, 512), 512)
        got = dot(xs[...].reshape(512, D), w1[i].reshape(D, 512)) + bias3[i]
        qkv[lax.div(i, 2), :, cols] = got.astype(bf16)

    put(qkv, qkv_o)
    for copy in c_sends:
        copy.start()

    lane = lax.broadcasted_iota(jnp.int32, (1, 128), 1)
    key_ok = lax.broadcasted_iota(jnp.int32, (512, 1), 0) < used

    @pl.loop(0, 8)
    def _(i):
        tick(14 + i)
        cols = pl.ds(pl.multiple_of(i * 128, 128), 128)
        q2, k2, v2 = qkv[0, :, cols], qkv[1, :, cols], qkv[2, :, cols]
        v_t = v2.T
        for h in range(2):
            mine = (lane < 64) if h == 0 else (lane >= 64)
            qm = jnp.where(mine, q2, jnp.zeros_like(q2))
            for b in range(2):
                s = dot(k2, qm[b * 256 : b * 256 + 256], 1, 1)
                s = jnp.where(key_ok, s * (HD**-0.5), masked_score)
                peak = jnp.max(s, axis=0, keepdims=True)
                e = jnp.exp(s - peak)
                total = jnp.sum(e, axis=0, keepdims=True)
                shares = (e * (1.0 / total)).astype(bf16)
                lse_o[i, h : h + 1, b * 256 : b * 256 + 256] = peak + jnp.log(total)
                mixed = dot(v_t[h * 64 : h * 64 + 64], shares)
                bt[pl.ds(pl.multiple_of(i * 128, 128) + h * 64, 64), b * 256 : b * 256 + 256] = mixed.astype(bf16)
        bl[:, cols] = bt[pl.ds(pl.multiple_of(i * 128, 128), 128), :].T

    put(bt, bt_o)

    @pl.loop(0, 2)
    def _(h):
        cols = pl.ds(pl.multiple_of(h * 512, 512), 512)
        att[:, cols] = dot(bl[...], w1[6 + h].reshape(D, 512))

    @pl.loop(0, 8)
    def _(r):
        rows = pl.ds(pl.multiple_of(r * 64, 64), 64)
        inp = xs[lax.div(r, 2), pl.ds(pl.multiple_of(lax.rem(r, 2) * 64, 64), 64), :].astype(f32)
        t = inp + (att[rows, :] + vec[2:3, :])
        center = t - jnp.mean(t, axis=-1, keepdims=True)
        factor = lax.rsqrt(jnp.mean(center * center, axis=-1, keepdims=True) + norm_eps)
        normed = center * factor
        out = normed * vec[3:4, :] + vec[4:5, :]
        n1[rows, :] = normed
        f1_o[rows, :] = jnp.broadcast_to(factor, (64, 128))
        settled[rows, :] = out
        sl[rows, :] = out.astype(bf16)

    put(n1, n1_o)

    @pl.loop(0, 8)
    def _(i):
        cols = pl.ds(pl.multiple_of(i * 128, 128), 128)
        slt[cols, :] = sl[:, cols].T

    put(slt, slt_o)

    @pl.loop(0, 8)
    def _(j):
        tick(22 + j)
        cols = pl.ds(pl.multiple_of(j * 512, 512), 512)
        for r in range(2):
            rows = slice(r * 256, r * 256 + 256)
            got = dot(sl[rows, :], w1[8 + j].reshape(D, 512)) + be3[j]
            a, slope = gelu_parts(got)
            act[rows, cols] = a.astype(bf16)
            gp[rows, cols] = slope.astype(bf16)

    put(act, act_o)
    put(gp, gp_o)

    @pl.loop(0, 8)
    def _(j):
        tick(30 + j)
        cols = pl.ds(pl.multiple_of(j * 128, 128), 128)
        att[:, cols] = dot(act[...], w2[j].reshape(FF, 128))

    c_own.wait()
    for copy in c_sends:
        copy.wait_recv()
    small_o[...] = jnp.zeros((8, D), f32)

    @pl.loop(0, 8)
    def _(r):
        rows = pl.ds(pl.multiple_of(r * 64, 64), 64)
        t = settled[rows, :] + (att[rows, :] + vec[7:8, :])
        center = t - jnp.mean(t, axis=-1, keepdims=True)
        factor = lax.rsqrt(jnp.mean(center * center, axis=-1, keepdims=True) + norm_eps)
        normed = center * factor
        ok = (lax.broadcasted_iota(jnp.int32, (64, 1), 0) + r * 64) < used
        finished = jnp.where(ok, normed * vec[5:6, :] + vec[6:7, :], 0.0)
        bl[rows, :] = finished.astype(bf16)
        cot = cots[lax.div(r, 2), pl.ds(pl.multiple_of(lax.rem(r, 2) * 64, 64), 64), :].astype(f32)
        grad = jnp.where(ok, cot, 0.0)
        e = grad * vec[5:6, :]
        pull = jnp.mean(e, axis=-1, keepdims=True) + normed * jnp.mean(e * normed, axis=-1, keepdims=True)
        two = factor * (e - pull)
        settled[rows, :] = two
        small_o[5:6, :] += jnp.sum(grad * normed, axis=0, keepdims=True)
        small_o[6:7, :] += jnp.sum(grad, axis=0, keepdims=True)
        small_o[7:8, :] += jnp.sum(two.astype(bf16).astype(f32), axis=0, keepdims=True)

    put(settled, g2_o)
    put(bl, res_o)

    for copy in outs:
        copy.wait()
    for copy in x_sends + c_sends:
        copy.wait_send()
    for stage in range(4):

        def left(core, stage=stage):
            for copy in vector_copies(core, stage):
                copy.wait_send()

        by_core(stage, left)
    for kind, low, high in ((0, 0, 16), (1, 16, 24)):

        @pl.loop(low, high)
        def _(p):
            for stage in range(4):

                def left(core, stage=stage):
                    for copy in copies(kind, p, core, stage):
                        copy.wait_send()

                by_core(stage, left)
            keep(kind, p).wait()


def forward_pass(sa, sm, se, sr, vt, x_loc, cot_loc, lengths):
    V, S = pltpu.VMEM, jax.ShapeDtypeStruct
    anywhere, vmem = pl.BlockSpec(memory_space=pl.ANY), pl.BlockSpec(memory_space=pltpu.VMEM)
    blocks = (4, 2, 2, 2)
    outs = [
        (S((16, *blocks, 32, 512), bf16), anywhere),
        (S((*blocks, 128, D), bf16), anywhere),
        (S((16, D), f32), vmem),
        (S((D, 512), bf16), anywhere),
        (S((3, 512, D), bf16), anywhere),
        (S((8, 2, 512), f32), vmem),
        (S((D, 512), bf16), anywhere),
        (S((512, D), f32), anywhere),
        (S((512, 128), f32), vmem),
        (S((D, 512), bf16), anywhere),
        (S((512, FF), bf16), anywhere),
        (S((512, FF), bf16), anywhere),
        (S((512, D), f32), anywhere),
        (S((512, D), bf16), anywhere),
        (S((8, D), f32), vmem),
    ]
    dma = pltpu.SemaphoreType.DMA
    return pl.pallas_call(
        forward_kernel,
        out_shape=[o[0] for o in outs],
        out_specs=[o[1] for o in outs],
        in_specs=[vmem] * 5 + [anywhere] * 2 + [pl.BlockSpec(memory_space=pltpu.SMEM)],
        scratch_shapes=[
            V((16, *blocks, 32, 512), bf16),
            V((8, *blocks, 128, 128), bf16),
            V((*blocks, 16, 128), bf16),
            V((4, 128, D), bf16),
            V((4, 128, D), bf16),
            V((3, 512, D), bf16),
            V((D, 512), bf16),
            V((512, D), bf16),
            V((512, D), f32),
            V((512, D), f32),
            V((512, D), f32),
            V((512, D), bf16),
            V((512, FF), bf16),
            V((512, FF), bf16),
            V((D, 512), bf16),
            V((D, 512), bf16),
            V((6, 1, 512), f32),
            V((8, 1, 512), f32),
            dma((24, 6)),
            dma((24, 6)),
            dma((24,)),
            dma((6,)),
            dma((6,)),
            dma((2, 3)),
            dma((2, 3)),
            dma((2,)),
            dma((16,)),
        ],
        compiler_params=pltpu.CompilerParams(
            collective_id=1, has_side_effects=True, vmem_limit_bytes=62 * 1024 * 1024
        ),
        name="forward_pass",
    )(sa, sm, se, sr, vt, x_loc, cot_loc, lengths)


SCATTER_LAGS = (0, 1, 3, 5, 7)
RING = 10


def backward_kernel(
    w1h, w2h, vec, xt_i, qkv_i, lse, bt_i, n1_i, f1, slt_i, act_i, gp_i, g2_i, res_i, small, lengths,
    aw_i, am_i, au_i, mw_i, mm_i, mu_i, ew_i, em_i, eu_i, rw_i, rm_i, ru_i,
    res_o, ig_o, am_o, au_o, aw_o, mm_o, mu_o, mw_o, em_o, eu_o, ew_o, rm_o, ru_o, rw_o, vg_o,
    act, gp, gc, gct, slt, xt, bt, qkv, gs, n1, wr, we, wm, wa,
    gh, r1, r2, r3, r4, h2, h3, aw, am, au, mw, mm, mu, ew, em, eu, rw, rm, ru,
    vg, bg, v1, v2, v3, v4, vh,
    lsem, wrsem, wesem, ssem, rsem, stsem, vssem, vrsem, xssem, xrsem, xlsem,
):
    z, y, x, c = place()
    sh = x * 2 + c
    dp = z * 2 + y
    up = [lax.rem(z + k, 4) for k in (1, 2, 3)]

    loads = []

    def load(src, dst):
        copy = pltpu.make_async_copy(src, dst, lsem.at[len(loads)])
        copy.start()
        loads.append(copy)
        return copy

    got_two, got_act = load(g2_i, gs), load(act_i, act)

    def wr_load(j):
        slot = lax.rem(j, 2) if not isinstance(j, int) else j % 2
        a, b = (lax.div(j, 2), lax.rem(j, 2)) if not isinstance(j, int) else (j // 2, j % 2)
        return pltpu.make_async_copy(w2h.at[a, b], wr.at[slot], wrsem.at[slot])

    def we_load(j):
        slot = lax.rem(j, 2) if not isinstance(j, int) else j % 2
        return pltpu.make_async_copy(w1h.at[8 + j], we.at[slot], wesem.at[slot])

    wr_load(0).start()
    we_load(0).start()
    got_gp, got_sl = load(gp_i, gp), load(slt_i, slt)
    got_n1, got_bt, got_wm = load(n1_i, n1), load(bt_i, bt), load(w1h.at[pl.ds(6, 2)], wm)
    got_qkv, got_xt, got_wa = load(qkv_i, qkv), load(xt_i, xt), load(w1h.at[pl.ds(0, 6)], wa)
    states = [(aw_i, aw), (am_i, am), (au_i, au), (mw_i, mw), (mm_i, mm), (mu_i, mu), (ew_i, ew), (em_i, em), (eu_i, eu)]
    states += [(rw_i, rw), (rm_i, rm), (ru_i, ru)]
    got_states = [load(a, b) for a, b in states]

    def remote(src, dst, s, r, to):
        return pltpu.make_async_remote_copy(src, dst, s, r, device_id=to, device_id_type=MESH)

    bar = pltpu.get_barrier_semaphore()
    others = [device(z, y, x, 1 - c), device(z, y, 1 - x, c), device(z, y, 1 - x, 1 - c), device(z, 1 - y, x, c)]
    others += [device(up[k], y, x, c) for k in range(3)]
    for other in others:
        pl.semaphore_signal(bar, inc=1, device_id=other, device_id_type=MESH)
    pl.semaphore_wait(bar, len(others))

    def mod(p, n):
        return p % n if isinstance(p, int) else lax.rem(p, n)

    def copies(p, core, stage):
        own = gh.at[mod(p, RING)]
        R1, R2, R3, R4 = r1.at[mod(p, 8)], r2.at[mod(p, 8)], r3.at[mod(p, 8)], r4.at[mod(p, 8)]
        H2, H3 = h2.at[mod(p, 4)], h3.at[mod(p, 4)]

        def send(slot, a, b, to):
            return remote(a, b, ssem.at[p, slot], rsem.at[p, slot], to)

        if stage == 0:
            return [send(0, own.at[:, :, :, 1 - c], R1, device(z, y, x, 1 - c))]
        if core == 0:
            if stage == 1:
                return [send(1, own.at[:, :, 1 - x, c], R2, device(z, y, 1 - x, c))]
            if stage == 2:
                return [send(2, H2.at[:, 1 - y], R3.at[pl.ds(0, 4)], device(z, 1 - y, x, c))]
            return [send(3 + k, H3.at[up[k]], R4.at[k], device(up[k], y, x, c)) for k in range(3)]
        if stage == 1:
            return [send(1, own.at[:, 1 - y, :, c], R2, device(z, 1 - y, x, c))]
        if stage == 2:
            return [send(3 + k, H2.at[up[k]], R3.at[pl.ds(2 * k, 2)], device(up[k], y, x, c)) for k in range(3)]
        return [send(2, H3.at[1 - x], R4.at[0], device(z, y, 1 - x, c))]

    def wide(v):
        return v.astype(f32)

    def adam(w, m, u, index, g, rate):
        first = beta_one * m[index] + (1.0 - beta_one) * g
        second = beta_two * u[index] + (1.0 - beta_two) * g * g
        m[index] = first
        u[index] = second
        root = jnp.sqrt(second * (1.0 / (1.0 - beta_two**STEP))) + adam_eps
        old = w[index]
        w[index] = old - rate * (first * (1.0 / (1.0 - beta_one**STEP)) / root + matrix_decay * old)

    def stores(p, kind):
        def at(n, width):
            return pl.ds(pl.multiple_of(n * width, width), width)

        if kind == 0:
            refs, index = [(rm, rm_o), (ru, ru_o), (rw, rw_o)], (ALL, at(p, 128))
        elif kind == 1:
            refs, index = [(em, em_o), (eu, eu_o), (ew, ew_o)], (ALL, at(p - 8, 512))
        elif kind == 2:
            refs, index = [(mm, mm_o), (mu, mu_o), (mw, mw_o)], (ALL, at(p - 16, 512))
        else:
            m, h = (p - 18) // 2, (p - 18) % 2
            refs, index = [(am, am_o), (au, au_o), (aw, aw_o)], (m, ALL, at(h, 512))
        return index, [pltpu.make_async_copy(a.at[index], b.at[index], stsem.at[p, n]) for n, (a, b) in enumerate(refs)]

    kinds = ((0, 0, 8), (1, 8, 16), (2, 16, 18), (3, 18, 24))

    def close(p, g):
        for kind, low, high in kinds:

            def run(kind=kind):
                index, out = stores(p, kind)
                if kind == 0:
                    tall = jnp.concatenate([g[:, n * 128 : n * 128 + 128] for n in range(4)], axis=0)
                    adam(rw, rm, ru, index, tall.T, rates[3])
                elif kind == 1:
                    adam(ew, em, eu, index, g, rates[2])
                elif kind == 2:
                    adam(mw, mm, mu, index, g, rates[1])
                else:
                    adam(aw, am, au, index, g, rates[0])
                for copy in out:
                    copy.start()

            when(within(p, low, high), run)

    def arrive(p, core, stage):
        GH = gh.at[mod(p, RING)]
        R1, R2, R3, R4 = r1.at[mod(p, 8)], r2.at[mod(p, 8)], r3.at[mod(p, 8)], r4.at[mod(p, 8)]
        H2, H3 = h2.at[mod(p, 4)], h3.at[mod(p, 4)]
        if stage > 0:
            for copy in copies(p, core, stage - 1):
                copy.wait()
        if stage == 1:

            @pl.loop(0, 16)
            def _(i):
                a, b, d = i // 4, (i // 2) % 2, i % 2
                GH[a, b, d, c] = (wide(GH[a, b, d, c]) + wide(R1[a, b, d])).astype(bf16)

        elif stage == 2:

            @pl.loop(0, 8)
            def _(i):
                a, b = i // 2, i % 2
                mine = GH[a, b, x, c] if core == 0 else GH[a, y, b, c]
                H2[a, b] = (wide(mine) + wide(R2[a, b])).astype(bf16)

        elif stage == 3 and core == 0:

            @pl.loop(0, 4)
            def _(a):
                H3[a] = (wide(H2[a, y]) + wide(R3[a])).astype(bf16)

        elif stage == 3:

            @pl.loop(0, 2)
            def _(a):
                H3[a] = (wide(H2[z, a]) + wide(R3[a]) + wide(R3[2 + a]) + wide(R3[4 + a])).astype(bf16)

        elif stage == 4 and core == 0:
            close(p, wide(H3[z]) + wide(R4[0]) + wide(R4[1]) + wide(R4[2]))
        elif stage == 4:
            close(p, wide(H3[x]) + wide(R4[0]))
        if stage < 4:
            for copy in copies(p, core, stage):
                copy.start()

    def tick(t):
        for stage in (4, 3, 2, 1, 0):
            p = t - SCATTER_LAGS[stage]

            def run(p=p, stage=stage):
                if stage == 0:
                    arrive(p, 0, 0)
                else:
                    pl.when(c == 0)(lambda: arrive(p, 0, stage))
                    pl.when(c == 1)(lambda: arrive(p, 1, stage))

            when(within(p, 0, 24), run)

    def exchange(src, dst, which):
        sends = []
        for k in (1, 2, 3):
            to = lax.rem(sh + k, 4)
            rows = pl.ds(pl.multiple_of(to * 128, 128), 128)
            sends.append(
                remote(src.at[rows], dst.at[sh], xssem.at[which, k - 1], xrsem.at[which, k - 1], (dp, to))
            )
        rows = pl.ds(pl.multiple_of(sh * 128, 128), 128)
        sends_own = pltpu.make_async_copy(src.at[rows], dst.at[sh], xlsem.at[which])
        for copy in [*sends, sends_own]:
            copy.start()
        return [*sends, sends_own]

    used = lengths[sh]
    moved = exchange(res_i, res_o, 0)

    got_two.wait()

    @pl.loop(0, 8)
    def _(i):
        cols = pl.ds(pl.multiple_of(i * 128, 128), 128)
        low = gs[:, cols].astype(bf16)
        gc[:, cols] = low
        gct[cols, :] = low.T

    got_act.wait()
    for half in range(2):

        @pl.loop(0, 8)
        def _(j):
            cols = pl.ds(pl.multiple_of(j * 512, 512), 512)
            got = dot(gct[half * 512 : half * 512 + 512, :], act[:, cols]).astype(bf16)
            for n in range(4):
                for k in range(4):
                    for g in range(4):
                        row = n * 128 + g * 32
                        gh[half * 4 + n, lax.div(j, 2), lax.rem(j, 2), k // 2, k % 2, :, g * 128 : g * 128 + 128] = got[
                            row : row + 32, k * 128 : k * 128 + 128
                        ]

        tick(half * 2)
        tick(half * 2 + 1)

    got_gp.wait()
    got_sl.wait()
    for copy in got_states:
        copy.wait()

    def produce(p, left, right):
        got = dot(left, right).astype(bf16)
        gh[mod(p, RING)] = got.reshape(4, 2, 2, 2, 32, 512)

    @pl.loop(0, 8)
    def _(j):
        @pl.when(j < 7)
        def _():
            wr_load(j + 1).start()
            we_load(j + 1).start()

        cols = pl.ds(pl.multiple_of(j * 512, 512), 512)
        slot = lax.rem(j, 2)
        wr_load(j).wait()
        got = dot(gc[...], wr[slot].reshape(512, D), 1, 1) * gp[:, cols].astype(f32)
        low = got.astype(bf16)
        gp[:, cols] = low
        bg[j] = jnp.sum(low.astype(f32), axis=0, keepdims=True)
        produce(8 + j, slt[...], gp[:, cols])
        we_load(j).wait()
        gs[...] += dot(gp[:, cols], we[slot].reshape(D, 512), 1, 1)
        tick(4 + j)

    vg[...] = jnp.zeros((16, D), f32)
    vg[5:8, :] = small[5:8, :]
    for j in range(8):
        vg[8 + j // 2 : 9 + j // 2, (j % 2) * 512 : (j % 2) * 512 + 512] = bg[j]
    got_n1.wait()

    @pl.loop(0, 8)
    def _(r):
        rows = pl.ds(pl.multiple_of(r * 64, 64), 64)
        grad, normed = gs[rows, :], n1[rows, :]
        vg[3:4, :] += jnp.sum(grad * normed, axis=0, keepdims=True)
        vg[4:5, :] += jnp.sum(grad, axis=0, keepdims=True)
        e = grad * vec[3:4, :]
        pull = jnp.mean(e, axis=-1, keepdims=True) + normed * jnp.mean(e * normed, axis=-1, keepdims=True)
        one = f1[rows, 0:1] * (e - pull)
        gs[rows, :] = one
        low = one.astype(bf16)
        gc[rows, :] = low
        vg[2:3, :] += jnp.sum(low.astype(f32), axis=0, keepdims=True)

    got_bt.wait()
    got_wm.wait()
    for h in range(2):
        produce(16 + h, bt[...], gc[:, h * 512 : h * 512 + 512])
    for h in range(2):
        rows = slice(h * 256, h * 256 + 256)
        back = dot(gc[rows, 0:512], wm[0].reshape(D, 512), 1, 1) + dot(gc[rows, 512:D], wm[1].reshape(D, 512), 1, 1)
        act[rows, 3 * D : 4 * D] = back.astype(bf16)

    got_qkv.wait()
    lane = lax.broadcasted_iota(jnp.int32, (1, 128), 1)
    key_ok = lax.broadcasted_iota(jnp.int32, (512, 1), 0) < used

    @pl.loop(0, 8)
    def _(i):
        @pl.when(i < 6)
        def _():
            tick(12 + i)

        start = pl.multiple_of(i * 128, 128)
        cols = pl.ds(start, 128)
        q2, k2, v2 = qkv[0, :, cols], qkv[1, :, cols], qkv[2, :, cols]
        db = act[:, pl.ds(pl.multiple_of(3 * D + i * 128, 128), 128)]
        k_t = k2.T
        dk = jnp.zeros((512, 128), f32)
        dv = jnp.zeros((512, 128), f32)
        turned = []
        for h in range(2):
            mine = (lane < 64) if h == 0 else (lane >= 64)
            qm = jnp.where(mine, q2, jnp.zeros_like(q2))
            dm = jnp.where(mine, db, jnp.zeros_like(db))
            parts = []
            for b in range(2):
                qb, gb = qm[b * 256 : b * 256 + 256], dm[b * 256 : b * 256 + 256]
                s = jnp.where(key_ok, dot(k2, qb, 1, 1) * (HD**-0.5), masked_score)
                share = jnp.exp(s - lse[i, h : h + 1, b * 256 : b * 256 + 256])
                gshare = dot(v2, gb, 1, 1)
                inner = jnp.sum(share * gshare, axis=0, keepdims=True)
                gscore = (share * (gshare - inner)).astype(bf16)
                dv = dv + dot(share.astype(bf16), gb)
                dk = dk + dot(gscore, qb)
                parts.append(dot(k_t[h * 64 : h * 64 + 64], gscore))
            turned.append(jnp.concatenate(parts, axis=1))
        dq = jnp.concatenate(turned, axis=0).T
        for n, (value, scale) in enumerate(((dq, HD**-0.5), (dk, HD**-0.5), (dv, 1.0))):
            low = (value * scale).astype(bf16)
            act[:, pl.ds(pl.multiple_of(n * D + i * 128, 128), 128)] = low
            if n != 1:
                vg[n // 2 : n // 2 + 1, cols] = jnp.sum(low.astype(f32), axis=0, keepdims=True)

    got_xt.wait()
    got_wa.wait()

    def vector_copies(stage):
        if stage == 0:
            return [remote(vg, v1, vssem.at[0], vrsem.at[0], device(z, y, x, 1 - c))]
        if stage == 1:
            return [remote(vg, v2, vssem.at[1], vrsem.at[1], device(z, y, 1 - x, c))]
        if stage == 2:
            return [remote(vh.at[:, 1 - y], v3, vssem.at[2], vrsem.at[2], device(z, 1 - y, x, c))]
        return [
            remote(vh.at[up[k], y], v4.at[k], vssem.at[3 + k], vrsem.at[3 + k], device(up[k], y, x, c))
            for k in range(3)
        ]

    def vector_step(stage):
        if stage > 0:
            for copy in vector_copies(stage - 1):
                copy.wait()
        if stage == 1:
            vg[...] += v1[...]
        elif stage == 2:
            vg[...] += v2[...]
            for g in range(8):
                vh[g // 2, g % 2] = vg[:, g * 128 : g * 128 + 128]
        elif stage == 3:
            for a in range(4):
                vh[a, y] += v3[a]
        elif stage == 4:
            vg_o[...] = vh[z, y] + v4[0] + v4[1] + v4[2]
        if stage < 4:
            for copy in vector_copies(stage):
                copy.start()

    vector_step(0)

    @pl.loop(0, 6)
    def _(i):
        cols = pl.ds(pl.multiple_of(i * 512, 512), 512)
        produce(18 + i, xt[...], act[:, cols])
        gs[...] += dot(act[:, cols], wa[i].reshape(D, 512), 1, 1)
        tick(18 + i)

    moved += exchange(gs, ig_o, 1)
    for t in range(24, 24 + 7):
        if t in (24, 25, 26, 27):
            vector_step(t - 23)
        tick(t)

    for copy in moved:
        copy.wait()

    for kind, low, high in kinds:

        @pl.loop(low, high)
        def _(p):
            for copy in stores(p, kind)[1]:
                copy.wait()


def backward_pass(kept, lengths, states):
    V, S = pltpu.VMEM, jax.ShapeDtypeStruct
    anywhere, vmem = pl.BlockSpec(memory_space=pl.ANY), pl.BlockSpec(memory_space=pltpu.VMEM)
    dma = pltpu.SemaphoreType.DMA
    shapes = [(3, 32, D), (32, D), (32, FF), (128, D)]
    weights = [V(s, f32) for s in shapes for _ in range(3)]
    near = [2, 5, 8, 14]
    return pl.pallas_call(
        backward_kernel,
        out_shape=[S((4, 128, D), bf16), S((4, 128, D), f32)]
        + [S(s, f32) for s in shapes for _ in range(3)]
        + [S((16, 128), f32)],
        out_specs=[anywhere] * 14 + [vmem],
        in_specs=[vmem if n in near else anywhere for n in range(15)]
        + [pl.BlockSpec(memory_space=pltpu.SMEM)]
        + [anywhere] * 12,
        scratch_shapes=[
            V((512, FF), bf16),
            V((512, FF), bf16),
            V((512, D), bf16),
            V((D, 512), bf16),
            V((D, 512), bf16),
            V((D, 512), bf16),
            V((D, 512), bf16),
            V((3, 512, D), bf16),
            V((512, D), f32),
            V((512, D), f32),
            V((2, 2, 2, 128, D), bf16),
            V((2, 4, 2, 2, 2, 32, 512), bf16),
            V((2, 4, 2, 2, 2, 32, 512), bf16),
            V((6, 4, 2, 2, 2, 32, 512), bf16),
            V((RING, 4, 2, 2, 2, 32, 512), bf16),
            V((8, 4, 2, 2, 32, 512), bf16),
            V((8, 4, 2, 32, 512), bf16),
            V((8, 6, 32, 512), bf16),
            V((8, 3, 32, 512), bf16),
            V((4, 4, 2, 32, 512), bf16),
            V((4, 4, 32, 512), bf16),
            *weights,
            V((16, D), f32),
            V((8, 1, 512), f32),
            V((16, D), f32),
            V((16, D), f32),
            V((4, 16, 128), f32),
            V((3, 16, 128), f32),
            V((4, 2, 16, 128), f32),
            dma((24,)),
            dma((2,)),
            dma((2,)),
            dma((24, 6)),
            dma((24, 6)),
            dma((24, 3)),
            dma((6,)),
            dma((6,)),
            dma((2, 3)),
            dma((2, 3)),
            dma((2,)),
        ],
        compiler_params=pltpu.CompilerParams(
            collective_id=2, has_side_effects=True, vmem_limit_bytes=62 * 1024 * 1024
        ),
        name="backward_pass",
    )(*kept, lengths, *states)


def product(left_side, right_side):
    return jnp.einsum("sri,ij->srj", left_side, right_side, preferred_element_type=f32)


def product_back(gradient, right_side):
    return jnp.einsum("srj,ij->sri", gradient, right_side, preferred_element_type=f32)


def outer_sum(left_side, gradient):
    return jnp.einsum("sri,srj->ij", left_side, gradient, preferred_element_type=f32)


def sum_rows(tensor):
    return jnp.sum(tensor.astype(f32), axis=(0, 1))


def split_heads(tensor):
    return tensor.reshape(tensor.shape[0], tensor.shape[1], -1, HD)


def norm_forward(tensor, gain, shift):
    center = tensor - jnp.mean(tensor, axis=-1, keepdims=True)
    spread = jnp.mean(center * center, axis=-1, keepdims=True)
    factor = lax.rsqrt(spread + norm_eps)
    normed = center * factor
    return (normed * gain + shift, normed, factor)


def norm_backward(gradient, normed, factor, gain):
    grad_normed = gradient * gain
    return factor * (
        grad_normed
        - jnp.mean(grad_normed, axis=-1, keepdims=True)
        - normed * jnp.mean(grad_normed * normed, axis=-1, keepdims=True)
    )


def attention_core(queries, keys, values, key_valid):
    score_scale = HD ** (-0.5)
    scores = (
        jnp.einsum("sqhd,skhd->shqk", split_heads(queries), split_heads(keys), preferred_element_type=f32)
        * score_scale
    )
    scores = jnp.where(key_valid[:, None, None, :], scores, masked_score)
    row_peak = jnp.max(scores, axis=-1, keepdims=True)
    row_sum = jnp.sum(jnp.exp(scores - row_peak), axis=-1, keepdims=True)
    shares = jnp.exp(scores - (row_peak + jnp.log(row_sum)))
    shares_low = shares.astype(bf16)
    blended = jnp.einsum("shqk,skhd->sqhd", shares_low, split_heads(values), preferred_element_type=f32)
    blended = blended.reshape(queries.shape).astype(bf16)
    return (blended, shares, shares_low)


def attention_back(grad_blended, queries, keys, values, shares, shares_low):
    score_scale = HD ** (-0.5)
    heads_grad = split_heads(grad_blended)
    grad_shares = jnp.einsum("sqhd,skhd->shqk", heads_grad, split_heads(values), preferred_element_type=f32)
    share_dot = jnp.sum(shares * grad_shares, axis=-1, keepdims=True)
    grad_scores = (shares * (grad_shares - share_dot)).astype(bf16)
    grad_query = (
        jnp.einsum("shqk,skhd->sqhd", grad_scores, split_heads(keys), preferred_element_type=f32) * score_scale
    )
    key_part = (
        jnp.einsum("shqk,sqhd->skhd", grad_scores, split_heads(queries), preferred_element_type=f32) * score_scale
    )
    value_part = jnp.einsum("shqk,sqhd->skhd", shares_low, heads_grad, preferred_element_type=f32)
    return (
        grad_query.reshape(queries.shape).astype(bf16),
        key_part.reshape(keys.shape).astype(bf16),
        value_part.reshape(values.shape).astype(bf16),
    )


def adam_update(weight, first, second, gradient, rate, decay):
    first_new = beta_one * first + (1.0 - beta_one) * gradient
    second_new = beta_two * second + (1.0 - beta_two) * gradient * gradient
    first_hat = first_new / (1.0 - beta_one**STEP)
    second_hat = second_new / (1.0 - beta_two**STEP)
    weight_new = weight - rate * (first_hat / (jnp.sqrt(second_hat) + adam_eps) + decay * weight)
    return (first_new, second_new, weight_new)


def finish(result, input_gradient, masters, firsts, seconds, reduced):
    updated = []
    for number in range(5):
        decay = matrix_decay if number < 4 else 0.0
        updated += adam_update(
            masters[number], firsts[number], seconds[number], reduced[number], rates[number], decay
        )
    return (result, input_gradient, *updated, reduced[4][2])


def local_fast(inputs, cotangent, lengths, *states):
    masters, firsts, seconds = states[0::3], states[1::3], states[2::3]
    mine = lax.rem(lax.axis_index("shard"), 4)
    tile = jnp.tile(jnp.pad(masters[4], ((0, 4), (0, 0))), (1, 4))
    tile = jnp.where(jnp.arange(128)[None, :] // 32 == mine, tile, 0.0).astype(bf16)
    kept = forward_pass(*masters[:4], tile, inputs, cotangent, lengths)
    states = [t[n] for n in range(4) for t in (masters, firsts, seconds)]
    result, input_gradient, *updated, grad = backward_pass(kept, lengths, states)
    grad = lax.dynamic_slice(grad, (0, mine * 32), (NV, 32))
    updated += adam_update(masters[4], firsts[4], seconds[4], grad, rates[4], 0.0)
    return (result, input_gradient, *updated, grad[2])


def local_any(inputs, cotangent, lengths, *states):
    masters, firsts, seconds = states[0::3], states[1::3], states[2::3]
    attend_low, mixing_low, expand_low, reduce_low = [w.astype(bf16) for w in masters[:4]]
    attend_full = lax.all_gather(attend_low, ("dp", "shard"), axis=1, tiled=True)
    mixing_full, expand_full, reduce_full = [
        lax.all_gather(w, ("dp", "shard"), axis=0, tiled=True) for w in (mixing_low, expand_low, reduce_low)
    ]
    vec = lax.all_gather(masters[4].astype(bf16), ("dp", "shard"), axis=1, tiled=True).astype(f32)

    block_in = lax.all_to_all(inputs, "shard", split_axis=0, concat_axis=1, tiled=True)
    block_cot = lax.all_to_all(cotangent, "shard", split_axis=0, concat_axis=1, tiled=True)
    count, length = block_in.shape[0], block_in.shape[1]
    used = lax.dynamic_slice_in_dim(lengths, lax.axis_index("shard") * count, count)
    valid = jnp.arange(length)[None, :] < used[:, None]
    row_valid = valid.astype(f32)

    queries = (product(block_in, attend_full[0]) + vec[0]).astype(bf16)
    keys = product(block_in, attend_full[1]).astype(bf16)
    values = (product(block_in, attend_full[2]) + vec[1]).astype(bf16)
    blended, shares, shares_low = attention_core(queries, keys, values, valid)
    attended = product(blended, mixing_full) + vec[2]
    settled, normed_one, factor_one = norm_forward(block_in.astype(f32) + attended, vec[3], vec[4])
    settled_low = settled.astype(bf16)
    expanded = product(settled_low, expand_full) + vec[8:].reshape(FF)
    activated = jax.nn.gelu(expanded, approximate=False).astype(bf16)
    contracted = product(activated, reduce_full) + vec[7]
    finished, normed_two, factor_two = norm_forward(settled + contracted, vec[5], vec[6])
    result = (finished * row_valid[:, :, None]).astype(bf16)
    result = lax.all_to_all(result, "shard", split_axis=1, concat_axis=0, tiled=True)

    grad_out = block_cot.astype(f32) * row_valid[:, :, None]
    gain_two = sum_rows(grad_out * normed_two)
    shift_two = sum_rows(grad_out)
    grad_two = norm_backward(grad_out, normed_two, factor_two, vec[5])
    grad_contract = grad_two.astype(bf16)
    grad_reduce = outer_sum(activated, grad_contract)
    bias_reduce = sum_rows(grad_contract)
    grad_active = product_back(grad_contract, reduce_full)
    gelu_pull = jax.vjp(functools.partial(jax.nn.gelu, approximate=False), expanded)[1]
    grad_expanded = gelu_pull(grad_active)[0].astype(bf16)
    grad_expand = outer_sum(settled_low, grad_expanded)
    bias_expand = sum_rows(grad_expanded)
    grad_settled = grad_two + product_back(grad_expanded, expand_full)
    gain_one = sum_rows(grad_settled * normed_one)
    shift_one = sum_rows(grad_settled)
    grad_one = norm_backward(grad_settled, normed_one, factor_one, vec[3])
    grad_attended = grad_one.astype(bf16)
    grad_mixing = outer_sum(blended, grad_attended)
    bias_mixing = sum_rows(grad_attended)
    grad_blended = product_back(grad_attended, mixing_full).astype(bf16)
    query_grad, key_grad, value_grad = attention_back(grad_blended, queries, keys, values, shares, shares_low)
    grad_attend = jnp.stack([outer_sum(block_in, g) for g in (query_grad, key_grad, value_grad)])
    input_gradient = (
        grad_one
        + product_back(query_grad, attend_full[0])
        + product_back(key_grad, attend_full[1])
        + product_back(value_grad, attend_full[2])
    )
    input_gradient = lax.all_to_all(input_gradient, "shard", split_axis=1, concat_axis=0, tiled=True)
    small_rows = [sum_rows(query_grad), sum_rows(value_grad), bias_mixing, gain_one, shift_one, gain_two, shift_two]
    small_rows = jnp.stack([*small_rows, bias_reduce])
    grad_vectors = jnp.concatenate([small_rows, bias_expand.reshape(NV - 8, D)], axis=0)

    reduced = [lax.psum_scatter(grad_attend, ("dp", "shard"), scatter_dimension=1, tiled=True)]
    for g in (grad_mixing, grad_expand, grad_reduce):
        reduced.append(lax.psum_scatter(g, ("dp", "shard"), scatter_dimension=0, tiled=True))
    reduced = (*reduced, lax.psum_scatter(grad_vectors, ("dp", "shard"), scatter_dimension=1, tiled=True))
    return finish(result, input_gradient, masters, firsts, seconds, reduced)


def solution(mesh):
    fast = mesh.shape["dp"] == 8 and mesh.shape["shard"] == 4
    rows = P("dp", "shard", None)
    both = ("dp", "shard")
    middle, first, last = P(None, both, None), P(both, None), P(None, both)
    states = [middle] * 3 + [first] * 9 + [last] * 3
    return jax.shard_map(
        local_fast if fast else local_any,
        mesh=mesh,
        in_specs=(rows, rows, P("dp"), *states),
        out_specs=(rows, rows, *states, P(both)),
        check_vma=False,
    )
```

```python
import functools

import jax
import jax.numpy as jnp
from jax import lax
from jax.experimental import pallas as pl
from jax.experimental.pallas import tpu as pltpu
from jax.sharding import PartitionSpec as P

D = 1024
HD = 64
FF = 4096
STEP = 10
NV = 12
MESH = pl.DeviceIdType.MESH
ALL = slice(None)

beta_one = 0.9
beta_two = 0.999
adam_eps = 1e-08
norm_eps = 1e-05
matrix_decay = 0.01
masked_score = -1e30
rates = (0.06, 1.0, 0.06, 0.03, 0.5)
bf16 = jnp.bfloat16
f32 = jnp.float32


def place():
    dp = lax.axis_index("dp")
    sh = lax.axis_index("shard")
    return lax.div(dp, 2), lax.rem(dp, 2), lax.div(sh, 2), lax.rem(sh, 2)


def device(z, y, x, c):
    return (z * 2 + y, x * 2 + c)


def meet(z, y, x, c):
    bar = pltpu.get_barrier_semaphore()
    others = [device(z, y, x, 1 - c), device(z, y, 1 - x, c), device(z, 1 - y, x, c)]
    others += [device(lax.rem(z + k, 4), y, x, c) for k in (1, 2, 3)]
    for other in others:
        pl.semaphore_signal(bar, inc=1, device_id=other, device_id_type=MESH)
    pl.semaphore_wait(bar, len(others))


GATHER_ORDER = ("zyx", "xzy")
EARLY_ORDER = ("zyx", "yzx")


def dot(a, b, left=1, right=0):
    return lax.dot_general(a, b, (((left,), (right,)), ((), ())), preferred_element_type=f32)


def when(cond, run):
    if isinstance(cond, bool):
        if cond:
            run()
    else:
        pl.when(cond)(run)


def within(p, low, high):
    if isinstance(p, int):
        return low <= p < high
    return jnp.logical_and(p >= low, p < high)


def gelu_parts(v):
    u = jnp.abs(v) * (0.5**0.5)
    t = 1.0 / (1.0 + 0.3275911 * u)
    bell = jnp.exp(-u * u)
    poly = ((((1.061405429 * t - 1.453152027) * t + 1.421413741) * t - 0.284496736) * t + 0.254829592) * t
    tail = 0.5 * poly * bell
    share = jnp.where(v < 0.0, tail, 1.0 - tail)
    return v * share, share + v * bell * 0.3989422804014327


def forward_kernel(
    sa, sm, se, sr, vs, x_loc, cot_loc, lengths,
    w1h, w2h, vec, xt_o, qkv_o, lse_o, bt_o, n1_o, f1_o, slt_o, act_o, gp_o, g2_o, res_o, gc_o, gct_o, small_o,
    w1, w2, vg, xs, cots, qkv, bt, bl, att, settled, n1, sl, act, gp, xt, slt, gct, bias3, be3,
    ssem, rsem, wsem, vssem, vrsem, xssem, xrsem, xlsem, osem, rowsem,
):
    z, y, x, c = place()
    sh = x * 2 + c
    dp = z * 2 + y

    bar = pltpu.get_barrier_semaphore()
    others = [device(z, y, x, 1 - c), device(z, y, 1 - x, c), device(z, y, 1 - x, 1 - c), device(z, 1 - y, x, c)]
    others += [device(lax.rem(z + k, 4), y, x, c) for k in (1, 2, 3)]
    for other in others:
        pl.semaphore_signal(bar, inc=1, device_id=other, device_id_type=MESH)

    for m in range(3):
        for h in range(2):
            w1[m * 2 + h, z, y, x, c] = sa[m, :, h * 512 : h * 512 + 512].astype(bf16)
    for h in range(2):
        w1[6 + h, z, y, x, c] = sm[:, h * 512 : h * 512 + 512].astype(bf16)
    for j in range(8):
        w1[8 + j, z, y, x, c] = se[:, j * 512 : j * 512 + 512].astype(bf16)
        w2[j, z, y, x, c] = sr[:, j * 128 : j * 128 + 128].astype(bf16)
    vec[...] = jnp.zeros((16, D), f32)
    vec[0:12, 0:32] = vs[...]
    vg[z, y, x, c] = pltpu.roll(vec[:, 0:128], sh * 32, 1).astype(bf16)

    def remote(src, dst, s, r, to):
        return pltpu.make_async_remote_copy(src, dst, s, r, device_id=to, device_id_type=MESH)

    def route(view, core, stage, s, r, early=None):
        if stage == 3:
            ref = view(ALL, ALL, ALL, c)
            return [remote(ref, ref, s(5), r(5), device(z, y, x, 1 - c))]
        order = (early if early else GATHER_ORDER)[core]
        done, axis = order[:stage], order[stage]
        here = dict(z=z, y=y, x=x)
        ref = view(*[ALL if a in done else here[a] for a in "zyx"], c)
        if axis == "z":
            up = [lax.rem(z + k, 4) for k in (1, 2, 3)]
            return [remote(ref, ref, s(k), r(k), device(up[k], y, x, c)) for k in range(3)]
        if axis == "y":
            return [remote(ref, ref, s(3), r(3), device(z, 1 - y, x, c))]
        return [remote(ref, ref, s(4), r(4), device(z, y, 1 - x, c))]

    def copies(kind, p, core, stage):
        buf = w1 if kind == 0 else w2
        q = p if kind == 0 else p - 16
        early = EARLY_ORDER if isinstance(p, int) and p < 2 else None
        return route(lambda *i: buf.at[(q, *i)], core, stage, lambda k: ssem.at[p, k], lambda k: rsem.at[p, k], early)

    def vector_copies(core, stage):
        return route(lambda *i: vg.at[i], core, stage, lambda k: vssem.at[k], lambda k: vrsem.at[k])

    def keep(kind, p):
        if kind == 0:
            return pltpu.make_async_copy(w1.at[p], w1h.at[p], wsem.at[p])
        cols = pl.ds((p - 16) * 128 if isinstance(p, int) else pl.multiple_of((p - 16) * 128, 128), 128)
        return pltpu.make_async_copy(w2.at[p - 16], w2h.at[:, :, :, :, :, cols], wsem.at[p])

    def by_core(stage, run):
        if stage == 3:
            run(0)
        else:
            pl.when(c == 0)(lambda: run(0))
            pl.when(c == 1)(lambda: run(1))

    def step(make, stage):
        def arrive(core):
            for copy in make(core, stage - 1):
                copy.wait()

        def leave(core):
            for copy in make(core, stage):
                copy.start()

        if stage > 0:
            by_core(stage - 1, arrive)
        if stage < 4:
            by_core(stage, leave)

    def tick(t):
        for stage in (4, 3, 2, 1, 0):
            p = t - 2 * stage
            for kind, low, high in ((0, 0, 16), (1, 16, 24)):

                def run(kind=kind, p=p, stage=stage):
                    step(lambda core, s: copies(kind, p, core, s), stage)
                    if stage == 4:
                        keep(kind, p).start()

                when(within(p, low, high), run)

    pl.semaphore_wait(bar, len(others))

    def exchange(src, dst, which):
        sends = []
        for k in (1, 2, 3):
            to = lax.rem(sh + k, 4)
            sends.append(
                remote(src.at[to], dst.at[sh], xssem.at[which, k - 1], xrsem.at[which, k - 1], (dp, to))
            )
        return sends, pltpu.make_async_copy(src.at[sh], dst.at[sh], xlsem.at[which])

    x_sends, x_own = exchange(x_loc, xs, 0)
    c_sends, c_own = exchange(cot_loc, cots, 1)
    step(vector_copies, 0)
    x_own.start()
    c_own.start()
    for t in range(8):
        tick(t)
        if t in (2, 4, 6):
            step(vector_copies, (2, 4, 6).index(t) + 1)
        if t == 0:
            for copy in x_sends:
                copy.start()
    x_own.wait()
    for copy in x_sends:
        copy.wait_recv()
    used = lengths[sh]
    step(vector_copies, 4)

    for g in range(8):
        total = jnp.zeros((16, 128), f32)
        for i in range(4):
            total = total + vg[g // 2, g % 2, i // 2, i % 2].astype(f32)
        vec[:, g * 128 : g * 128 + 128] = total
    for h in range(2):
        bias3[h] = vec[0:1, h * 512 : h * 512 + 512]
        bias3[2 + h] = jnp.zeros((1, 512), f32)
        bias3[4 + h] = vec[1:2, h * 512 : h * 512 + 512]
    for j in range(8):
        be3[j] = vec[8 + j // 2 : 9 + j // 2, (j % 2) * 512 : (j % 2) * 512 + 512]

    outs = []

    def put(src, dst):
        copy = pltpu.make_async_copy(src, dst, osem.at[len(outs)])
        copy.start()
        outs.append(copy)

    @pl.loop(0, 8)
    def _(i):
        cols = pl.ds(pl.multiple_of(i * 128, 128), 128)
        for b in range(4):
            xt[cols, b * 128 : b * 128 + 128] = xs[b, :, cols].T

    put(xt, xt_o)

    @pl.loop(0, 6)
    def _(i):
        tick(8 + i)
        cols = pl.ds(pl.multiple_of(lax.rem(i, 2) * 512, 512), 512)
        got = dot(xs[...].reshape(512, D), w1[i].reshape(D, 512)) + bias3[i]
        qkv[lax.div(i, 2), :, cols] = got.astype(bf16)

    put(qkv, qkv_o)
    for copy in c_sends:
        copy.start()

    lane = lax.broadcasted_iota(jnp.int32, (1, 128), 1)
    key_ok = lax.broadcasted_iota(jnp.int32, (512, 1), 0) < used

    @pl.loop(0, 8)
    def _(i):
        @pl.when(lax.rem(i, 2) == 0)
        def _():
            tick(14 + lax.div(i, 2))

        cols = pl.ds(pl.multiple_of(i * 128, 128), 128)
        q2, k2, v2 = qkv[0, :, cols], qkv[1, :, cols], qkv[2, :, cols]
        v_t = v2.T
        for h in range(2):
            mine = (lane < 64) if h == 0 else (lane >= 64)
            qm = jnp.where(mine, q2, jnp.zeros_like(q2))
            for b in range(2):
                s = dot(k2, qm[b * 256 : b * 256 + 256], 1, 1)
                s = jnp.where(key_ok, s * (HD**-0.5), masked_score)
                peak = jnp.max(s, axis=0, keepdims=True)
                e = jnp.exp(s - peak)
                total = jnp.sum(e, axis=0, keepdims=True)
                shares = (e * (1.0 / total)).astype(bf16)
                lse_o[i, h : h + 1, b * 256 : b * 256 + 256] = peak + jnp.log(total)
                mixed = dot(v_t[h * 64 : h * 64 + 64], shares)
                bt[pl.ds(pl.multiple_of(i * 128, 128) + h * 64, 64), b * 256 : b * 256 + 256] = mixed.astype(bf16)
        bl[:, cols] = bt[pl.ds(pl.multiple_of(i * 128, 128), 128), :].T

    put(bt, bt_o)

    @pl.loop(0, 2)
    def _(h):
        cols = pl.ds(pl.multiple_of(h * 512, 512), 512)
        att[:, cols] = dot(bl[...], w1[6 + h].reshape(D, 512))

    tick(18)

    @pl.loop(0, 8)
    def _(r):
        rows = pl.ds(pl.multiple_of(r * 64, 64), 64)
        inp = xs[lax.div(r, 2), pl.ds(pl.multiple_of(lax.rem(r, 2) * 64, 64), 64), :].astype(f32)
        t = inp + (att[rows, :] + vec[2:3, :])
        center = t - jnp.mean(t, axis=-1, keepdims=True)
        factor = lax.rsqrt(jnp.mean(center * center, axis=-1, keepdims=True) + norm_eps)
        normed = center * factor
        out = normed * vec[3:4, :] + vec[4:5, :]
        n1[rows, :] = normed
        f1_o[rows, :] = jnp.broadcast_to(factor, (64, 128))
        settled[rows, :] = out
        sl[rows, :] = out.astype(bf16)

    tick(19)

    put(n1, n1_o)

    @pl.loop(0, 8)
    def _(i):
        cols = pl.ds(pl.multiple_of(i * 128, 128), 128)
        slt[cols, :] = sl[:, cols].T

    put(slt, slt_o)

    @pl.loop(0, 8)
    def _(j):
        @pl.when(lax.rem(j, 2) == 0)
        def _():
            tick(20 + lax.div(j, 2))

        cols = pl.ds(pl.multiple_of(j * 512, 512), 512)
        for r in range(2):
            rows = slice(r * 256, r * 256 + 256)
            got = dot(sl[rows, :], w1[8 + j].reshape(D, 512)) + be3[j]
            a, slope = gelu_parts(got)
            act[rows, cols] = a.astype(bf16)
            gp[rows, cols] = slope.astype(bf16)

    put(act, act_o)
    put(gp, gp_o)

    @pl.loop(0, 8)
    def _(j):
        tick(24 + j)
        cols = pl.ds(pl.multiple_of(j * 128, 128), 128)
        att[:, cols] = dot(act[...], w2[j].reshape(FF, 128))

    c_own.wait()
    for copy in c_sends:
        copy.wait_recv()
    small_o[...] = jnp.zeros((8, D), f32)

    def row_stores(rows, r):
        pairs = ((settled, g2_o), (bl, res_o), (sl, gc_o))
        return [pltpu.make_async_copy(a.at[rows], b.at[rows], rowsem.at[r, n]) for n, (a, b) in enumerate(pairs)]

    @pl.loop(0, 8)
    def _(r):
        rows = pl.ds(pl.multiple_of(r * 64, 64), 64)
        t = settled[rows, :] + (att[rows, :] + vec[7:8, :])
        center = t - jnp.mean(t, axis=-1, keepdims=True)
        factor = lax.rsqrt(jnp.mean(center * center, axis=-1, keepdims=True) + norm_eps)
        normed = center * factor
        ok = (lax.broadcasted_iota(jnp.int32, (64, 1), 0) + r * 64) < used
        finished = jnp.where(ok, normed * vec[5:6, :] + vec[6:7, :], 0.0)
        bl[rows, :] = finished.astype(bf16)
        cot = cots[lax.div(r, 2), pl.ds(pl.multiple_of(lax.rem(r, 2) * 64, 64), 64), :].astype(f32)
        grad = jnp.where(ok, cot, 0.0)
        e = grad * vec[5:6, :]
        pull = jnp.mean(e, axis=-1, keepdims=True) + normed * jnp.mean(e * normed, axis=-1, keepdims=True)
        two = factor * (e - pull)
        settled[rows, :] = two
        sl[rows, :] = two.astype(bf16)
        for copy in row_stores(rows, r):
            copy.start()
        small_o[5:6, :] += jnp.sum(grad * normed, axis=0, keepdims=True)
        small_o[6:7, :] += jnp.sum(grad, axis=0, keepdims=True)
        small_o[7:8, :] += jnp.sum(two.astype(bf16).astype(f32), axis=0, keepdims=True)

    @pl.loop(0, 8)
    def _(i):
        cols = pl.ds(pl.multiple_of(i * 128, 128), 128)
        gct[cols, :] = sl[:, cols].T

    put(gct, gct_o)

    @pl.loop(0, 8)
    def _(r):
        for copy in row_stores(pl.ds(pl.multiple_of(r * 64, 64), 64), r):
            copy.wait()

    for copy in outs:
        copy.wait()
    for copy in x_sends + c_sends:
        copy.wait_send()

    @pl.loop(0, 16)
    def _(p):
        keep(0, p).wait()

    @pl.loop(16, 24)
    def _(p):
        keep(1, p).wait()


def forward_pass(sa, sm, se, sr, vs, x_loc, cot_loc, lengths):
    V, S = pltpu.VMEM, jax.ShapeDtypeStruct
    anywhere, vmem = pl.BlockSpec(memory_space=pl.ANY), pl.BlockSpec(memory_space=pltpu.VMEM)
    blocks = (4, 2, 2, 2)
    outs = [
        (S((16, *blocks, 32, 512), bf16), anywhere),
        (S((*blocks, 128, D), bf16), anywhere),
        (S((16, D), f32), vmem),
        (S((D, 512), bf16), anywhere),
        (S((3, 512, D), bf16), anywhere),
        (S((8, 2, 512), f32), vmem),
        (S((D, 512), bf16), anywhere),
        (S((512, D), f32), anywhere),
        (S((512, 128), f32), vmem),
        (S((D, 512), bf16), anywhere),
        (S((512, FF), bf16), anywhere),
        (S((512, FF), bf16), anywhere),
        (S((512, D), f32), anywhere),
        (S((512, D), bf16), anywhere),
        (S((512, D), bf16), anywhere),
        (S((D, 512), bf16), anywhere),
        (S((8, D), f32), vmem),
    ]
    dma = pltpu.SemaphoreType.DMA
    return pl.pallas_call(
        forward_kernel,
        out_shape=[o[0] for o in outs],
        out_specs=[o[1] for o in outs],
        in_specs=[vmem] * 5 + [anywhere] * 2 + [pl.BlockSpec(memory_space=pltpu.SMEM)],
        scratch_shapes=[
            V((16, *blocks, 32, 512), bf16),
            V((8, *blocks, 128, 128), bf16),
            V((*blocks, 16, 128), bf16),
            V((4, 128, D), bf16),
            V((4, 128, D), bf16),
            V((3, 512, D), bf16),
            V((D, 512), bf16),
            V((512, D), bf16),
            V((512, D), f32),
            V((512, D), f32),
            V((512, D), f32),
            V((512, D), bf16),
            V((512, FF), bf16),
            V((512, FF), bf16),
            V((D, 512), bf16),
            V((D, 512), bf16),
            V((D, 512), bf16),
            V((6, 1, 512), f32),
            V((8, 1, 512), f32),
            dma((24, 6)),
            dma((24, 6)),
            dma((24,)),
            dma((6,)),
            dma((6,)),
            dma((2, 3)),
            dma((2, 3)),
            dma((2,)),
            dma((16,)),
            dma((8, 3)),
        ],
        compiler_params=pltpu.CompilerParams(
            collective_id=1, has_side_effects=True, vmem_limit_bytes=62 * 1024 * 1024
        ),
        name="forward_pass",
    )(sa, sm, se, sr, vs, x_loc, cot_loc, lengths)


SCATTER_LAGS = (0, 1, 3, 5, 7)
RING = 10


def backward_kernel(
    w1h, w2h, vec, xt_i, qkv_i, lse, bt_i, n1_i, f1, slt_i, act_i, gp_i, g2_i, res_i, gc_i, gct_i, small, lengths,
    res_o, ig_o, ga_o, gm_o, ge_o, gr_o, vg_o,
    act, gp, gc, gct, slt, xt, bt, qkv, gs, n1, wr, we, wm, wa,
    gh, r1, r2, r3, r4, h2, h3, ga, gm, ge, gr,
    vg, bg, v1, v2, v3, v4, vh,
    lsem, wrsem, wesem, ssem, rsem, stsem, vssem, vrsem, xssem, xrsem, xlsem,
):
    z, y, x, c = place()
    sh = x * 2 + c
    dp = z * 2 + y
    up = [lax.rem(z + k, 4) for k in (1, 2, 3)]

    loads = []

    def load(src, dst):
        copy = pltpu.make_async_copy(src, dst, lsem.at[len(loads)])
        copy.start()
        loads.append(copy)
        return copy

    got_gct, got_act = load(gct_i, gct), load(act_i, act)

    def wr_load(j):
        slot = lax.rem(j, 2) if not isinstance(j, int) else j % 2
        a, b = (lax.div(j, 2), lax.rem(j, 2)) if not isinstance(j, int) else (j // 2, j % 2)
        return pltpu.make_async_copy(w2h.at[a, b], wr.at[slot], wrsem.at[slot])

    def we_load(j):
        slot = lax.rem(j, 2) if not isinstance(j, int) else j % 2
        return pltpu.make_async_copy(w1h.at[8 + j], we.at[slot], wesem.at[slot])

    def remote(src, dst, s, r, to):
        return pltpu.make_async_remote_copy(src, dst, s, r, device_id=to, device_id_type=MESH)

    bar = pltpu.get_barrier_semaphore()
    others = [device(z, y, x, 1 - c), device(z, y, 1 - x, c), device(z, y, 1 - x, 1 - c), device(z, 1 - y, x, c)]
    others += [device(up[k], y, x, c) for k in range(3)]
    for other in others:
        pl.semaphore_signal(bar, inc=1, device_id=other, device_id_type=MESH)

    def mod(p, n):
        return p % n if isinstance(p, int) else lax.rem(p, n)

    def copies(p, core, stage):
        own = gh.at[mod(p, RING)]
        R1, R2, R3, R4 = r1.at[mod(p, 8)], r2.at[mod(p, 8)], r3.at[mod(p, 8)], r4.at[mod(p, 8)]
        H2, H3 = h2.at[mod(p, 4)], h3.at[mod(p, 4)]

        def send(slot, a, b, to):
            return remote(a, b, ssem.at[p, slot], rsem.at[p, slot], to)

        if stage == 0:
            return [send(0, own.at[:, :, :, 1 - c], R1, device(z, y, x, 1 - c))]
        if core == 0:
            if stage == 1:
                return [send(1, own.at[:, :, 1 - x, c], R2, device(z, y, 1 - x, c))]
            if stage == 2:
                return [send(2, H2.at[:, 1 - y], R3.at[pl.ds(0, 4)], device(z, 1 - y, x, c))]
            return [send(3 + k, H3.at[up[k]], R4.at[k], device(up[k], y, x, c)) for k in range(3)]
        if stage == 1:
            return [send(1, own.at[:, 1 - y, :, c], R2, device(z, 1 - y, x, c))]
        if stage == 2:
            return [send(3 + k, H2.at[up[k]], R3.at[pl.ds(2 * k, 2)], device(up[k], y, x, c)) for k in range(3)]
        return [send(2, H3.at[1 - x], R4.at[0], device(z, y, 1 - x, c))]

    def wide(v):
        return v.astype(f32)

    def store(p, kind):
        def at(n, width):
            return pl.ds(pl.multiple_of(n * width, width), width)

        if kind == 0:
            ref, out, index = gr, gr_o, (ALL, at(p, 128))
        elif kind == 1:
            ref, out, index = ge, ge_o, (ALL, at(p - 8, 512))
        elif kind == 2:
            ref, out, index = gm, gm_o, (ALL, at(p - 16, 512))
        else:
            ref, out, index = ga, ga_o, ((p - 18) // 2, ALL, at((p - 18) % 2, 512))
        return ref, index, pltpu.make_async_copy(ref.at[index], out.at[index], stsem.at[p])

    kinds = ((0, 0, 8), (1, 8, 16), (2, 16, 18), (3, 18, 24))

    def close(p, g):
        for kind, low, high in kinds:

            def run(kind=kind):
                ref, index, out = store(p, kind)
                if kind == 0:
                    tall = jnp.concatenate([g[:, n * 128 : n * 128 + 128] for n in range(4)], axis=0)
                    ref[index] = tall.T
                else:
                    ref[index] = g
                out.start()

            when(within(p, low, high), run)

    def arrive(p, core, stage):
        GH = gh.at[mod(p, RING)]
        R1, R2, R3, R4 = r1.at[mod(p, 8)], r2.at[mod(p, 8)], r3.at[mod(p, 8)], r4.at[mod(p, 8)]
        H2, H3 = h2.at[mod(p, 4)], h3.at[mod(p, 4)]
        if stage > 0:
            for copy in copies(p, core, stage - 1):
                copy.wait()
        if stage == 1:

            @pl.loop(0, 4)
            def _(a):
                GH[a, :, :, c] = GH[a, :, :, c] + R1[a]

        elif stage == 2:

            @pl.loop(0, 4)
            def _(a):
                mine = GH[a, :, x, c] if core == 0 else GH[a, y, :, c]
                H2[a] = mine + R2[a]

        elif stage == 3 and core == 0:

            H3[...] = H2[:, y] + R3[0:4]

        elif stage == 3:

            @pl.loop(0, 2)
            def _(a):
                H3[a] = (wide(H2[z, a]) + wide(R3[a]) + wide(R3[2 + a]) + wide(R3[4 + a])).astype(bf16)

        elif stage == 4 and core == 0:
            close(p, wide(H3[z]) + wide(R4[0]) + wide(R4[1]) + wide(R4[2]))
        elif stage == 4:
            close(p, wide(H3[x]) + wide(R4[0]))
        if stage < 4:
            for copy in copies(p, core, stage):
                copy.start()

    def tick(t):
        for stage in (4, 3, 2, 1, 0):
            p = t - SCATTER_LAGS[stage]

            def run(p=p, stage=stage):
                if stage == 0:
                    arrive(p, 0, 0)
                else:
                    pl.when(c == 0)(lambda: arrive(p, 0, stage))
                    pl.when(c == 1)(lambda: arrive(p, 1, stage))

            when(within(p, 0, 24), run)

    def exchange(src, dst, which):
        sends = []
        for k in (1, 2, 3):
            to = lax.rem(sh + k, 4)
            rows = pl.ds(pl.multiple_of(to * 128, 128), 128)
            sends.append(
                remote(src.at[rows], dst.at[sh], xssem.at[which, k - 1], xrsem.at[which, k - 1], (dp, to))
            )
        rows = pl.ds(pl.multiple_of(sh * 128, 128), 128)
        sends_own = pltpu.make_async_copy(src.at[rows], dst.at[sh], xlsem.at[which])
        for copy in [*sends, sends_own]:
            copy.start()
        return [*sends, sends_own]

    used = lengths[sh]

    got_two, got_gc = load(g2_i, gs), load(gc_i, gc)
    wr_load(0).start()
    we_load(0).start()
    got_gp, got_sl = load(gp_i, gp), load(slt_i, slt)
    got_gct.wait()
    got_act.wait()
    for part in range(4):

        @pl.loop(0, 8)
        def _(j):
            cols = pl.ds(pl.multiple_of(j * 512, 512), 512)
            got = dot(gct[part * 256 : part * 256 + 256, :], act[:, cols]).astype(bf16)
            for n in range(2):
                for k in range(4):
                    for g in range(4):
                        row = n * 128 + g * 32
                        gh[part * 2 + n, lax.div(j, 2), lax.rem(j, 2), k // 2, k % 2, :, g * 128 : g * 128 + 128] = got[
                            row : row + 32, k * 128 : k * 128 + 128
                        ]

        if part == 0:
            pl.semaphore_wait(bar, len(others))
        tick(part)

    got_two.wait()
    got_gc.wait()
    got_gp.wait()
    got_sl.wait()
    got_n1, got_bt, got_wm = load(n1_i, n1), load(bt_i, bt), load(w1h.at[pl.ds(6, 2)], wm)
    got_qkv, got_xt, got_wa = load(qkv_i, qkv), load(xt_i, xt), load(w1h.at[pl.ds(0, 6)], wa)

    def produce(p, left, right):
        got = dot(left, right).astype(bf16)
        gh[mod(p, RING)] = got.reshape(4, 2, 2, 2, 32, 512)

    @pl.loop(0, 8)
    def _(j):
        @pl.when(j < 7)
        def _():
            wr_load(j + 1).start()
            we_load(j + 1).start()

        cols = pl.ds(pl.multiple_of(j * 512, 512), 512)
        slot = lax.rem(j, 2)
        wr_load(j).wait()
        got = dot(gc[...], wr[slot].reshape(512, D), 1, 1) * gp[:, cols].astype(f32)
        low = got.astype(bf16)
        gp[:, cols] = low
        bg[j] = jnp.sum(low.astype(f32), axis=0, keepdims=True)
        produce(8 + j, slt[...], gp[:, cols])
        we_load(j).wait()
        gs[...] += dot(gp[:, cols], we[slot].reshape(D, 512), 1, 1)
        tick(4 + j)

    moved = exchange(res_i, res_o, 0)

    vg[...] = jnp.zeros((16, D), f32)
    vg[5:8, :] = small[5:8, :]
    for j in range(8):
        vg[8 + j // 2 : 9 + j // 2, (j % 2) * 512 : (j % 2) * 512 + 512] = bg[j]
    got_n1.wait()

    @pl.loop(0, 8)
    def _(r):
        rows = pl.ds(pl.multiple_of(r * 64, 64), 64)
        grad, normed = gs[rows, :], n1[rows, :]
        vg[3:4, :] += jnp.sum(grad * normed, axis=0, keepdims=True)
        vg[4:5, :] += jnp.sum(grad, axis=0, keepdims=True)
        e = grad * vec[3:4, :]
        pull = jnp.mean(e, axis=-1, keepdims=True) + normed * jnp.mean(e * normed, axis=-1, keepdims=True)
        one = f1[rows, 0:1] * (e - pull)
        gs[rows, :] = one
        low = one.astype(bf16)
        gc[rows, :] = low
        vg[2:3, :] += jnp.sum(low.astype(f32), axis=0, keepdims=True)

    tick(12)
    got_bt.wait()
    got_wm.wait()
    for h in range(2):
        produce(16 + h, bt[...], gc[:, h * 512 : h * 512 + 512])
    for h in range(2):
        rows = slice(h * 256, h * 256 + 256)
        back = dot(gc[rows, 0:512], wm[0].reshape(D, 512), 1, 1) + dot(gc[rows, 512:D], wm[1].reshape(D, 512), 1, 1)
        act[rows, 3 * D : 4 * D] = back.astype(bf16)

    got_qkv.wait()
    lane = lax.broadcasted_iota(jnp.int32, (1, 128), 1)
    key_ok = lax.broadcasted_iota(jnp.int32, (512, 1), 0) < used

    @pl.loop(0, 8)
    def _(i):
        @pl.when(lax.rem(i, 2) == 0)
        def _():
            tick(13 + lax.div(i, 2))

        start = pl.multiple_of(i * 128, 128)
        cols = pl.ds(start, 128)
        q2, k2, v2 = qkv[0, :, cols], qkv[1, :, cols], qkv[2, :, cols]
        db = act[:, pl.ds(pl.multiple_of(3 * D + i * 128, 128), 128)]
        k_t = k2.T
        dk = jnp.zeros((512, 128), f32)
        dv = jnp.zeros((512, 128), f32)
        turned = []
        for h in range(2):
            mine = (lane < 64) if h == 0 else (lane >= 64)
            qm = jnp.where(mine, q2, jnp.zeros_like(q2))
            dm = jnp.where(mine, db, jnp.zeros_like(db))
            parts = []
            for b in range(2):
                qb, gb = qm[b * 256 : b * 256 + 256], dm[b * 256 : b * 256 + 256]
                s = jnp.where(key_ok, dot(k2, qb, 1, 1) * (HD**-0.5), masked_score)
                share = jnp.exp(s - lse[i, h : h + 1, b * 256 : b * 256 + 256])
                gshare = dot(v2, gb, 1, 1)
                inner = jnp.sum(share * gshare, axis=0, keepdims=True)
                gscore = (share * (gshare - inner)).astype(bf16)
                dv = dv + dot(share.astype(bf16), gb)
                dk = dk + dot(gscore, qb)
                parts.append(dot(k_t[h * 64 : h * 64 + 64], gscore))
            turned.append(jnp.concatenate(parts, axis=1))
        dq = jnp.concatenate(turned, axis=0).T
        for n, (value, scale) in enumerate(((dq, HD**-0.5), (dk, HD**-0.5), (dv, 1.0))):
            low = (value * scale).astype(bf16)
            act[:, pl.ds(pl.multiple_of(n * D + i * 128, 128), 128)] = low
            if n != 1:
                vg[n // 2 : n // 2 + 1, cols] = jnp.sum(low.astype(f32), axis=0, keepdims=True)

    got_xt.wait()
    got_wa.wait()

    def vector_copies(stage):
        if stage == 0:
            return [remote(vg, v1, vssem.at[0], vrsem.at[0], device(z, y, x, 1 - c))]
        if stage == 1:
            return [remote(vg, v2, vssem.at[1], vrsem.at[1], device(z, y, 1 - x, c))]
        if stage == 2:
            return [remote(vh.at[:, 1 - y], v3, vssem.at[2], vrsem.at[2], device(z, 1 - y, x, c))]
        return [
            remote(vh.at[up[k], y], v4.at[k], vssem.at[3 + k], vrsem.at[3 + k], device(up[k], y, x, c))
            for k in range(3)
        ]

    def vector_step(stage):
        if stage > 0:
            for copy in vector_copies(stage - 1):
                copy.wait()
        if stage == 1:
            vg[...] += v1[...]
        elif stage == 2:
            vg[...] += v2[...]
            for g in range(8):
                vh[g // 2, g % 2] = vg[:, g * 128 : g * 128 + 128]
        elif stage == 3:
            for a in range(4):
                vh[a, y] += v3[a]
        elif stage == 4:
            vg_o[...] = vh[z, y] + v4[0] + v4[1] + v4[2]
        if stage < 4:
            for copy in vector_copies(stage):
                copy.start()

    vector_step(0)
    tick(17)

    @pl.loop(0, 6)
    def _(i):
        cols = pl.ds(pl.multiple_of(i * 512, 512), 512)
        gs[...] += dot(act[:, cols], wa[i].reshape(D, 512), 1, 1)

    gc[...] = gs[...].astype(bf16)
    moved += exchange(gc, ig_o, 1)

    @pl.loop(0, 6)
    def _(i):
        cols = pl.ds(pl.multiple_of(i * 512, 512), 512)
        produce(18 + i, xt[...], act[:, cols])
        tick(18 + i)

    for t in range(24, 24 + SCATTER_LAGS[4]):
        if t in (24, 25, 26, 27):
            vector_step(t - 23)
        tick(t)

    for copy in moved:
        copy.wait()

    for kind, low, high in kinds:

        @pl.loop(low, high)
        def _(p):
            store(p, kind)[2].wait()


def backward_pass(kept, lengths):
    V, S = pltpu.VMEM, jax.ShapeDtypeStruct
    anywhere, vmem = pl.BlockSpec(memory_space=pl.ANY), pl.BlockSpec(memory_space=pltpu.VMEM)
    dma = pltpu.SemaphoreType.DMA
    shapes = [(3, 32, D), (32, D), (32, FF), (128, D)]
    near = [2, 5, 8, 16]
    return pl.pallas_call(
        backward_kernel,
        out_shape=[S((4, 128, D), bf16), S((4, 128, D), bf16)]
        + [S(s, f32) for s in shapes]
        + [S((16, 128), f32)],
        out_specs=[anywhere] * 6 + [vmem],
        in_specs=[vmem if n in near else anywhere for n in range(17)]
        + [pl.BlockSpec(memory_space=pltpu.SMEM)],
        scratch_shapes=[
            V((512, FF), bf16),
            V((512, FF), bf16),
            V((512, D), bf16),
            V((D, 512), bf16),
            V((D, 512), bf16),
            V((D, 512), bf16),
            V((D, 512), bf16),
            V((3, 512, D), bf16),
            V((512, D), f32),
            V((512, D), f32),
            V((2, 2, 2, 128, D), bf16),
            V((2, 4, 2, 2, 2, 32, 512), bf16),
            V((2, 4, 2, 2, 2, 32, 512), bf16),
            V((6, 4, 2, 2, 2, 32, 512), bf16),
            V((RING, 4, 2, 2, 2, 32, 512), bf16),
            V((8, 4, 2, 2, 32, 512), bf16),
            V((8, 4, 2, 32, 512), bf16),
            V((8, 6, 32, 512), bf16),
            V((8, 3, 32, 512), bf16),
            V((4, 4, 2, 32, 512), bf16),
            V((4, 4, 32, 512), bf16),
            *[V(s, f32) for s in shapes],
            V((16, D), f32),
            V((8, 1, 512), f32),
            V((16, D), f32),
            V((16, D), f32),
            V((4, 16, 128), f32),
            V((3, 16, 128), f32),
            V((4, 2, 16, 128), f32),
            dma((24,)),
            dma((2,)),
            dma((2,)),
            dma((24, 6)),
            dma((24, 6)),
            dma((24,)),
            dma((6,)),
            dma((6,)),
            dma((2, 3)),
            dma((2, 3)),
            dma((2,)),
        ],
        compiler_params=pltpu.CompilerParams(
            collective_id=2, has_side_effects=True, vmem_limit_bytes=62 * 1024 * 1024
        ),
        name="backward_pass",
    )(*kept, lengths)


def finish_kernel(*refs):
    ins, outs, held, wide, sems = refs[:22], refs[22:40], refs[40:58], refs[58], refs[59:]
    vg, mine, small = ins[0], lax.axis_index("shard"), ins[1:4]
    gains, big = ins[4:8], ins[8:20]
    moved = ins[20:22]
    isem, osem = sems

    def load(n, src):
        copy = pltpu.make_async_copy(src, held[n], isem.at[n])
        copy.start()
        return copy

    def save(n, dst):
        copy = pltpu.make_async_copy(held[n], dst, osem.at[n])
        copy.start()
        return copy

    order = (1, 0, 2, 3)
    loads = {}
    for k in order:
        loads[k] = [load(k, gains[k])] + [load(4 + 3 * k + n, big[3 * k + n]) for n in range(3)]
    passed = [load(16 + n, moved[n]) for n in range(2)]
    saves = []

    def adam(w, m, u, g, rate, decay):
        first = beta_one * m + (1.0 - beta_one) * g
        second = beta_two * u + (1.0 - beta_two) * g * g
        root = jnp.sqrt(second * (1.0 / (1.0 - beta_two**STEP))) + adam_eps
        return first, second, w - rate * (first * (1.0 / (1.0 - beta_one**STEP)) / root + decay * w)

    for k in order:
        for copy in loads[k]:
            copy.wait()
        w, m, u = held[4 + 3 * k : 7 + 3 * k]
        new = adam(w[...], m[...], u[...], held[k][...], rates[k], matrix_decay)
        m[...], u[...], w[...] = new
        saves += [save(5 + 3 * k, outs[2 + 3 * k]), save(6 + 3 * k, outs[3 + 3 * k]), save(4 + 3 * k, outs[4 + 3 * k])]
    passed[0].wait()
    saves.append(save(16, outs[0]))
    passed[1].wait()
    wide[...] = held[17][...].astype(f32)
    saves.append(pltpu.make_async_copy(wide, outs[1], osem.at[17]))
    saves[-1].start()
    grad = pltpu.roll(vg[...], lax.rem(4 - mine, 4) * 32, 1)[0:NV, 0:32]
    outs[14][...], outs[15][...], outs[16][...] = adam(small[0][...], small[1][...], small[2][...], grad, rates[4], 0.0)
    outs[17][...] = grad[2:3, :]
    for copy in saves:
        copy.wait()


def finish_step(masters, firsts, seconds, result, input_gradient, gradients, vector_gradient):
    V, S = pltpu.VMEM, jax.ShapeDtypeStruct
    anywhere, vmem = pl.BlockSpec(memory_space=pl.ANY), pl.BlockSpec(memory_space=pltpu.VMEM)
    big = [t[n] for n in range(4) for t in (masters, firsts, seconds)]
    moved = [S(t.shape, t.dtype) for t in (result, input_gradient)]
    outs = [moved[0], S(moved[1].shape, f32)] + [S(t.shape, f32) for t in big] + [S((NV, 32), f32)] * 3 + [S((1, 32), f32)]
    dma = pltpu.SemaphoreType.DMA
    *done, bias = pl.pallas_call(
        finish_kernel,
        out_shape=outs,
        out_specs=[anywhere] * 14 + [vmem] * 4,
        in_specs=[vmem] * 4 + [anywhere] * 18,
        scratch_shapes=[V(t.shape, f32) for t in gradients]
        + [V(t.shape, f32) for t in big]
        + [V(t.shape, t.dtype) for t in moved]
        + [V(moved[1].shape, f32)]
        + [dma((18,)), dma((18,))],
        compiler_params=pltpu.CompilerParams(vmem_limit_bytes=62 * 1024 * 1024),
        name="finish_step",
    )(vector_gradient, masters[4], firsts[4], seconds[4], *gradients, *big, result, input_gradient)
    return (*done, bias[0])


def product(left_side, right_side):
    return jnp.einsum("sri,ij->srj", left_side, right_side, preferred_element_type=f32)


def product_back(gradient, right_side):
    return jnp.einsum("srj,ij->sri", gradient, right_side, preferred_element_type=f32)


def outer_sum(left_side, gradient):
    return jnp.einsum("sri,srj->ij", left_side, gradient, preferred_element_type=f32)


def sum_rows(tensor):
    return jnp.sum(tensor.astype(f32), axis=(0, 1))


def split_heads(tensor):
    return tensor.reshape(tensor.shape[0], tensor.shape[1], -1, HD)


def norm_forward(tensor, gain, shift):
    center = tensor - jnp.mean(tensor, axis=-1, keepdims=True)
    spread = jnp.mean(center * center, axis=-1, keepdims=True)
    factor = lax.rsqrt(spread + norm_eps)
    normed = center * factor
    return (normed * gain + shift, normed, factor)


def norm_backward(gradient, normed, factor, gain):
    grad_normed = gradient * gain
    return factor * (
        grad_normed
        - jnp.mean(grad_normed, axis=-1, keepdims=True)
        - normed * jnp.mean(grad_normed * normed, axis=-1, keepdims=True)
    )


def attention_core(queries, keys, values, key_valid):
    score_scale = HD ** (-0.5)
    scores = (
        jnp.einsum("sqhd,skhd->shqk", split_heads(queries), split_heads(keys), preferred_element_type=f32)
        * score_scale
    )
    scores = jnp.where(key_valid[:, None, None, :], scores, masked_score)
    row_peak = jnp.max(scores, axis=-1, keepdims=True)
    row_sum = jnp.sum(jnp.exp(scores - row_peak), axis=-1, keepdims=True)
    shares = jnp.exp(scores - (row_peak + jnp.log(row_sum)))
    shares_low = shares.astype(bf16)
    blended = jnp.einsum("shqk,skhd->sqhd", shares_low, split_heads(values), preferred_element_type=f32)
    blended = blended.reshape(queries.shape).astype(bf16)
    return (blended, shares, shares_low)


def attention_back(grad_blended, queries, keys, values, shares, shares_low):
    score_scale = HD ** (-0.5)
    heads_grad = split_heads(grad_blended)
    grad_shares = jnp.einsum("sqhd,skhd->shqk", heads_grad, split_heads(values), preferred_element_type=f32)
    share_dot = jnp.sum(shares * grad_shares, axis=-1, keepdims=True)
    grad_scores = (shares * (grad_shares - share_dot)).astype(bf16)
    grad_query = (
        jnp.einsum("shqk,skhd->sqhd", grad_scores, split_heads(keys), preferred_element_type=f32) * score_scale
    )
    key_part = (
        jnp.einsum("shqk,sqhd->skhd", grad_scores, split_heads(queries), preferred_element_type=f32) * score_scale
    )
    value_part = jnp.einsum("shqk,sqhd->skhd", shares_low, heads_grad, preferred_element_type=f32)
    return (
        grad_query.reshape(queries.shape).astype(bf16),
        key_part.reshape(keys.shape).astype(bf16),
        value_part.reshape(values.shape).astype(bf16),
    )


def adam_update(weight, first, second, gradient, rate, decay):
    first_new = beta_one * first + (1.0 - beta_one) * gradient
    second_new = beta_two * second + (1.0 - beta_two) * gradient * gradient
    first_hat = first_new / (1.0 - beta_one**STEP)
    second_hat = second_new / (1.0 - beta_two**STEP)
    weight_new = weight - rate * (first_hat / (jnp.sqrt(second_hat) + adam_eps) + decay * weight)
    return (first_new, second_new, weight_new)


def finish(result, input_gradient, masters, firsts, seconds, reduced):
    updated = []
    for number in range(5):
        decay = matrix_decay if number < 4 else 0.0
        updated += adam_update(
            masters[number], firsts[number], seconds[number], reduced[number], rates[number], decay
        )
    return (result, input_gradient, *updated, reduced[4][2])


def local_fast(inputs, cotangent, lengths, *states):
    masters, firsts, seconds = states[0::3], states[1::3], states[2::3]
    kept = forward_pass(*masters, inputs, cotangent, lengths)
    result, input_gradient, *gradients, vector_gradient = backward_pass(kept, lengths)
    return finish_step(masters, firsts, seconds, result, input_gradient, gradients, vector_gradient)


def local_any(inputs, cotangent, lengths, *states):
    masters, firsts, seconds = states[0::3], states[1::3], states[2::3]
    attend_low, mixing_low, expand_low, reduce_low = [w.astype(bf16) for w in masters[:4]]
    attend_full = lax.all_gather(attend_low, ("dp", "shard"), axis=1, tiled=True)
    mixing_full, expand_full, reduce_full = [
        lax.all_gather(w, ("dp", "shard"), axis=0, tiled=True) for w in (mixing_low, expand_low, reduce_low)
    ]
    vec = lax.all_gather(masters[4].astype(bf16), ("dp", "shard"), axis=1, tiled=True).astype(f32)

    block_in = lax.all_to_all(inputs, "shard", split_axis=0, concat_axis=1, tiled=True)
    block_cot = lax.all_to_all(cotangent, "shard", split_axis=0, concat_axis=1, tiled=True)
    count, length = block_in.shape[0], block_in.shape[1]
    used = lax.dynamic_slice_in_dim(lengths, lax.axis_index("shard") * count, count)
    valid = jnp.arange(length)[None, :] < used[:, None]
    row_valid = valid.astype(f32)

    queries = (product(block_in, attend_full[0]) + vec[0]).astype(bf16)
    keys = product(block_in, attend_full[1]).astype(bf16)
    values = (product(block_in, attend_full[2]) + vec[1]).astype(bf16)
    blended, shares, shares_low = attention_core(queries, keys, values, valid)
    attended = product(blended, mixing_full) + vec[2]
    settled, normed_one, factor_one = norm_forward(block_in.astype(f32) + attended, vec[3], vec[4])
    settled_low = settled.astype(bf16)
    expanded = product(settled_low, expand_full) + vec[8:].reshape(FF)
    activated = jax.nn.gelu(expanded, approximate=False).astype(bf16)
    contracted = product(activated, reduce_full) + vec[7]
    finished, normed_two, factor_two = norm_forward(settled + contracted, vec[5], vec[6])
    result = (finished * row_valid[:, :, None]).astype(bf16)
    result = lax.all_to_all(result, "shard", split_axis=1, concat_axis=0, tiled=True)

    grad_out = block_cot.astype(f32) * row_valid[:, :, None]
    gain_two = sum_rows(grad_out * normed_two)
    shift_two = sum_rows(grad_out)
    grad_two = norm_backward(grad_out, normed_two, factor_two, vec[5])
    grad_contract = grad_two.astype(bf16)
    grad_reduce = outer_sum(activated, grad_contract)
    bias_reduce = sum_rows(grad_contract)
    grad_active = product_back(grad_contract, reduce_full)
    gelu_pull = jax.vjp(functools.partial(jax.nn.gelu, approximate=False), expanded)[1]
    grad_expanded = gelu_pull(grad_active)[0].astype(bf16)
    grad_expand = outer_sum(settled_low, grad_expanded)
    bias_expand = sum_rows(grad_expanded)
    grad_settled = grad_two + product_back(grad_expanded, expand_full)
    gain_one = sum_rows(grad_settled * normed_one)
    shift_one = sum_rows(grad_settled)
    grad_one = norm_backward(grad_settled, normed_one, factor_one, vec[3])
    grad_attended = grad_one.astype(bf16)
    grad_mixing = outer_sum(blended, grad_attended)
    bias_mixing = sum_rows(grad_attended)
    grad_blended = product_back(grad_attended, mixing_full).astype(bf16)
    query_grad, key_grad, value_grad = attention_back(grad_blended, queries, keys, values, shares, shares_low)
    grad_attend = jnp.stack([outer_sum(block_in, g) for g in (query_grad, key_grad, value_grad)])
    input_gradient = (
        grad_one
        + product_back(query_grad, attend_full[0])
        + product_back(key_grad, attend_full[1])
        + product_back(value_grad, attend_full[2])
    )
    input_gradient = lax.all_to_all(input_gradient, "shard", split_axis=1, concat_axis=0, tiled=True)
    small_rows = [sum_rows(query_grad), sum_rows(value_grad), bias_mixing, gain_one, shift_one, gain_two, shift_two]
    small_rows = jnp.stack([*small_rows, bias_reduce])
    grad_vectors = jnp.concatenate([small_rows, bias_expand.reshape(NV - 8, D)], axis=0)

    reduced = [lax.psum_scatter(grad_attend, ("dp", "shard"), scatter_dimension=1, tiled=True)]
    for g in (grad_mixing, grad_expand, grad_reduce):
        reduced.append(lax.psum_scatter(g, ("dp", "shard"), scatter_dimension=0, tiled=True))
    reduced = (*reduced, lax.psum_scatter(grad_vectors, ("dp", "shard"), scatter_dimension=1, tiled=True))
    return finish(result, input_gradient, masters, firsts, seconds, reduced)


def solution(mesh):
    fast = mesh.shape["dp"] == 8 and mesh.shape["shard"] == 4
    rows = P("dp", "shard", None)
    both = ("dp", "shard")
    middle, first, last = P(None, both, None), P(both, None), P(None, both)
    states = [middle] * 3 + [first] * 9 + [last] * 3
    return jax.shard_map(
        local_fast if fast else local_any,
        mesh=mesh,
        in_specs=(rows, rows, P("dp"), *states),
        out_specs=(rows, rows, *states, P(both)),
        check_vma=False,
    )
```

```python
import functools

import jax
import jax.numpy as jnp
from jax import lax
from jax.experimental import pallas as pl
from jax.experimental.pallas import tpu as pltpu
from jax.sharding import PartitionSpec as P

D = 1024
HD = 64
FF = 4096
STEP = 10
NV = 12
MESH = pl.DeviceIdType.MESH
ALL = slice(None)

beta_one = 0.9
beta_two = 0.999
adam_eps = 1e-08
norm_eps = 1e-05
matrix_decay = 0.01
masked_score = -1e30
rates = (0.06, 1.0, 0.06, 0.03, 0.5)
bf16 = jnp.bfloat16
f32 = jnp.float32


def place():
    dp = lax.axis_index("dp")
    sh = lax.axis_index("shard")
    return lax.div(dp, 2), lax.rem(dp, 2), lax.div(sh, 2), lax.rem(sh, 2)


def device(z, y, x, c):
    return (z * 2 + y, x * 2 + c)


GATHER_ORDER = ("zyx", "xzy")
EARLY_ORDER = ("zyx", "yzx")
EARLY = 2


def orders(p, c):
    early = isinstance(p, int) and p < EARLY
    return [(c == core, (EARLY_ORDER if early else GATHER_ORDER)[core]) for core in range(2)]


def dot(a, b, left=1, right=0):
    return lax.dot_general(a, b, (((left,), (right,)), ((), ())), preferred_element_type=f32)


def when(cond, run):
    if isinstance(cond, bool):
        if cond:
            run()
    else:
        pl.when(cond)(run)


def within(p, low, high):
    if isinstance(p, int):
        return low <= p < high
    return jnp.logical_and(p >= low, p < high)


def gelu_parts(v):
    u = jnp.abs(v) * (0.5**0.5)
    t = 1.0 / (1.0 + 0.3275911 * u)
    bell = jnp.exp(-u * u)
    poly = ((((1.061405429 * t - 1.453152027) * t + 1.421413741) * t - 0.284496736) * t + 0.254829592) * t
    tail = 0.5 * poly * bell
    share = jnp.where(v < 0.0, tail, 1.0 - tail)
    return v * share, share + v * bell * 0.3989422804014327


def forward_kernel(
    sa, sm, se, sr, vs, x_loc, cot_loc, lengths,
    w1h, w2h, vec, xt_o, qkv_o, lse_o, bt_o, n1_o, f1_o, slt_o, act_o, gp_o, g2_o, res_o, gc_o, gct_o, small_o,
    w1, w2, vg, xs, cots, qkv, bt, bl, att, settled, n1, sl, act, gp, xt, slt, gct, bias3, be3,
    ssem, rsem, wsem, vssem, vrsem, xssem, xrsem, xlsem, osem, rowsem,
):
    z, y, x, c = place()
    sh = x * 2 + c
    dp = z * 2 + y

    bar = pltpu.get_barrier_semaphore()
    others = [device(z, y, x, 1 - c), device(z, y, 1 - x, c), device(z, y, 1 - x, 1 - c), device(z, 1 - y, x, c)]
    others += [device(lax.rem(z + k, 4), y, x, c) for k in (1, 2, 3)]
    for other in others:
        pl.semaphore_signal(bar, inc=1, device_id=other, device_id_type=MESH)

    for m in range(3):
        for h in range(2):
            w1[m * 2 + h, z, y, x, c] = sa[m, :, h * 512 : h * 512 + 512].astype(bf16)
    for h in range(2):
        w1[6 + h, z, y, x, c] = sm[:, h * 512 : h * 512 + 512].astype(bf16)
    for j in range(8):
        w1[8 + j, z, y, x, c] = se[:, j * 512 : j * 512 + 512].astype(bf16)
        w2[j, z, y, x, c] = sr[:, j * 128 : j * 128 + 128].astype(bf16)
    vec[...] = jnp.zeros((16, D), f32)
    vec[0:12, 0:32] = vs[...]
    vg[z, y, x, c] = pltpu.roll(vec[:, 0:128], sh * 32, 1).astype(bf16)

    def remote(src, dst, s, r, to):
        return pltpu.make_async_remote_copy(src, dst, s, r, device_id=to, device_id_type=MESH)

    inner = jnp.logical_or(z == 1, z == 2)
    up = [lax.rem(z + k, 4) for k in (1, 2, 3)]

    def route(view, order, stage, s, r):
        if stage == 3:
            ref = view(ALL, ALL, ALL, c)
            return [remote(ref, ref, s(5), r(5), device(z, y, x, 1 - c))], "c"
        done, axis = order[:stage], order[stage]
        here = dict(z=z, y=y, x=x)
        ref = view(*[ALL if a in done else here[a] for a in "zyx"], c)
        if axis == "z":
            return [remote(ref, ref, s(k), r(k), device(up[k], y, x, c)) for k in range(3)], axis
        if axis == "y":
            return [remote(ref, ref, s(3), r(3), device(z, 1 - y, x, c))], axis
        return [remote(ref, ref, s(4), r(4), device(z, y, 1 - x, c))], axis

    def relay(view, order, s, r):
        done = order[: order.index("z")]
        here = dict(z=3 - z, y=y, x=x)
        ref = view(*[ALL if a in done else here[a] for a in "zyx"], c)
        remote(ref, ref, s(4 - 2 * z), r(4 - 2 * z), device(z, y, x, c)).wait_recv()
        remote(ref, ref, s(1), r(1), device(3 * (z - 1), y, x, c)).start()

    def leave(made, whole):
        copies, axis = made
        for k, copy in enumerate(copies):
            if axis == "z" and k == 1 and not whole:
                pl.when(jnp.logical_not(inner))(copy.start)
            else:
                copy.start()

    def arrive(made, whole):
        copies, axis = made
        for k, copy in enumerate(copies):
            copy.wait_send()
            if axis == "z" and k != 1 and not whole:
                pl.when(z != 2 - k // 2)(copy.wait_recv)
            else:
                copy.wait_recv()

    def place_of(kind, p):
        buf = w1 if kind == 0 else w2
        q = p if kind == 0 else p - 16
        return lambda *i: buf.at[(q, *i)], lambda k: ssem.at[p, k], lambda k: rsem.at[p, k]

    def step(p, parts, stage, whole=False):
        view, sends, receives = parts
        for cond, order in orders(p, c):

            def run(order=order):
                if stage > 0:
                    arrive(route(view, order, stage - 1, sends, receives), whole)
                if stage < 4:
                    leave(route(view, order, stage, sends, receives), whole)

            if stage == 4:
                run()
                break
            pl.when(cond)(run)

    def keep(kind, p):
        if kind == 0:
            return pltpu.make_async_copy(w1.at[p], w1h.at[p], wsem.at[p])
        cols = pl.ds((p - 16) * 128 if isinstance(p, int) else pl.multiple_of((p - 16) * 128, 128), 128)
        return pltpu.make_async_copy(w2.at[p - 16], w2h.at[:, :, :, :, :, cols], wsem.at[p])

    def tick(t):
        for stage in (4, 3, 2, 1, 0):
            p = t - 2 * stage
            for kind, low, high in ((0, 0, 16), (1, 16, 24)):

                def run(kind=kind, p=p, stage=stage):
                    step(p, place_of(kind, p), stage)
                    if stage == 4:
                        keep(kind, p).start()

                when(within(p, low, high), run)
        for stage in (2, 1, 0):
            p = t - 2 * stage - 1
            for kind, low, high in ((0, 0, 16), (1, 16, 24)):

                def run(kind=kind, p=p, stage=stage):
                    for cond, order in orders(p, c):
                        if order.index("z") == stage:
                            pl.when(jnp.logical_and(cond, inner))(lambda order=order: relay(place_of(kind, p)[0], order, *place_of(kind, p)[1:]))

                when(within(p, low, high), run)

    vectors_place = (lambda *i: vg.at[i], lambda k: vssem.at[k], lambda k: vrsem.at[k])

    def vector_step(stage):
        step(None, vectors_place, stage, whole=True)

    pl.semaphore_wait(bar, len(others))

    def exchange(src, dst, which):
        sends = []
        for k in (1, 2, 3):
            to = lax.rem(sh + k, 4)
            sends.append(
                remote(src.at[to], dst.at[sh], xssem.at[which, k - 1], xrsem.at[which, k - 1], (dp, to))
            )
        return sends, pltpu.make_async_copy(src.at[sh], dst.at[sh], xlsem.at[which])

    x_sends, x_own = exchange(x_loc, xs, 0)
    c_sends, c_own = exchange(cot_loc, cots, 1)
    vector_step(0)
    x_own.start()
    c_own.start()
    for t in range(8):
        tick(t)
        if t in (2, 4, 6):
            vector_step((2, 4, 6).index(t) + 1)
        if t in (0, 2, 4):
            x_sends[(0, 2, 4).index(t)].start()
    x_own.wait()
    for copy in x_sends:
        copy.wait_recv()
    used = lengths[sh]
    vector_step(4)

    for g in range(8):
        total = jnp.zeros((16, 128), f32)
        for i in range(4):
            total = total + vg[g // 2, g % 2, i // 2, i % 2].astype(f32)
        vec[:, g * 128 : g * 128 + 128] = total
    for h in range(2):
        bias3[h] = vec[0:1, h * 512 : h * 512 + 512]
        bias3[2 + h] = jnp.zeros((1, 512), f32)
        bias3[4 + h] = vec[1:2, h * 512 : h * 512 + 512]
    for j in range(8):
        be3[j] = vec[8 + j // 2 : 9 + j // 2, (j % 2) * 512 : (j % 2) * 512 + 512]

    outs = []

    def put(src, dst):
        copy = pltpu.make_async_copy(src, dst, osem.at[len(outs)])
        copy.start()
        outs.append(copy)

    @pl.loop(0, 8)
    def _(i):
        cols = pl.ds(pl.multiple_of(i * 128, 128), 128)
        for b in range(4):
            xt[cols, b * 128 : b * 128 + 128] = xs[b, :, cols].T

    put(xt, xt_o)

    for i in range(6):
        tick(8 + i)
        if i == 5:
            c_sends[1].start()
        if i == 3:
            c_sends[0].start()
        got = dot(xs[...].reshape(512, D), w1[i].reshape(D, 512)) + bias3[i]
        qkv[i // 2, :, (i % 2) * 512 : (i % 2) * 512 + 512] = got.astype(bf16)

    put(qkv, qkv_o)

    lane = lax.broadcasted_iota(jnp.int32, (1, 128), 1)
    key_ok = lax.broadcasted_iota(jnp.int32, (512, 1), 0) < used

    @pl.loop(0, 8)
    def _(i):
        @pl.when(lax.rem(i, 2) == 0)
        def _():
            tick(14 + lax.div(i, 2))

        cols = pl.ds(pl.multiple_of(i * 128, 128), 128)
        q2, k2, v2 = qkv[0, :, cols], qkv[1, :, cols], qkv[2, :, cols]
        v_t = v2.T
        for h in range(2):
            mine = (lane < 64) if h == 0 else (lane >= 64)
            qm = jnp.where(mine, q2, jnp.zeros_like(q2))
            for b in range(2):
                s = dot(k2, qm[b * 256 : b * 256 + 256], 1, 1)
                s = jnp.where(key_ok, s * (HD**-0.5), masked_score)
                peak = jnp.max(s, axis=0, keepdims=True)
                e = jnp.exp(s - peak)
                total = jnp.sum(e, axis=0, keepdims=True)
                shares = (e * (1.0 / total)).astype(bf16)
                lse_o[i, h : h + 1, b * 256 : b * 256 + 256] = peak + jnp.log(total)
                mixed = dot(v_t[h * 64 : h * 64 + 64], shares)
                bt[pl.ds(pl.multiple_of(i * 128, 128) + h * 64, 64), b * 256 : b * 256 + 256] = mixed.astype(bf16)
        bl[:, cols] = bt[pl.ds(pl.multiple_of(i * 128, 128), 128), :].T

    put(bt, bt_o)
    c_sends[2].start()

    @pl.loop(0, 2)
    def _(h):
        cols = pl.ds(pl.multiple_of(h * 512, 512), 512)
        att[:, cols] = dot(bl[...], w1[6 + h].reshape(D, 512))

    tick(18)

    @pl.loop(0, 8)
    def _(r):
        rows = pl.ds(pl.multiple_of(r * 64, 64), 64)
        inp = xs[lax.div(r, 2), pl.ds(pl.multiple_of(lax.rem(r, 2) * 64, 64), 64), :].astype(f32)
        t = inp + (att[rows, :] + vec[2:3, :])
        center = t - jnp.mean(t, axis=-1, keepdims=True)
        factor = lax.rsqrt(jnp.mean(center * center, axis=-1, keepdims=True) + norm_eps)
        normed = center * factor
        out = normed * vec[3:4, :] + vec[4:5, :]
        n1[rows, :] = normed
        f1_o[rows, :] = jnp.broadcast_to(factor, (64, 128))
        settled[rows, :] = out
        sl[rows, :] = out.astype(bf16)

    tick(19)

    put(n1, n1_o)

    @pl.loop(0, 8)
    def _(i):
        cols = pl.ds(pl.multiple_of(i * 128, 128), 128)
        slt[cols, :] = sl[:, cols].T

    put(slt, slt_o)

    @pl.loop(0, 8)
    def _(j):
        @pl.when(lax.rem(j, 2) == 0)
        def _():
            tick(20 + lax.div(j, 2))

        cols = pl.ds(pl.multiple_of(j * 512, 512), 512)
        for r in range(2):
            rows = slice(r * 256, r * 256 + 256)
            got = dot(sl[rows, :], w1[8 + j].reshape(D, 512)) + be3[j]
            a, slope = gelu_parts(got)
            act[rows, cols] = a.astype(bf16)
            gp[rows, cols] = slope.astype(bf16)

    put(act, act_o)
    put(gp, gp_o)

    @pl.loop(0, 8)
    def _(j):
        tick(24 + j)
        cols = pl.ds(pl.multiple_of(j * 128, 128), 128)
        att[:, cols] = dot(act[...], w2[j].reshape(FF, 128))

    c_own.wait()
    for copy in c_sends:
        copy.wait_recv()
    small_o[...] = jnp.zeros((8, D), f32)

    def row_stores(rows, r):
        pairs = ((settled, g2_o), (bl, res_o), (sl, gc_o))
        return [pltpu.make_async_copy(a.at[rows], b.at[rows], rowsem.at[r, n]) for n, (a, b) in enumerate(pairs)]

    @pl.loop(0, 8)
    def _(r):
        rows = pl.ds(pl.multiple_of(r * 64, 64), 64)
        t = settled[rows, :] + (att[rows, :] + vec[7:8, :])
        center = t - jnp.mean(t, axis=-1, keepdims=True)
        factor = lax.rsqrt(jnp.mean(center * center, axis=-1, keepdims=True) + norm_eps)
        normed = center * factor
        ok = (lax.broadcasted_iota(jnp.int32, (64, 1), 0) + r * 64) < used
        finished = jnp.where(ok, normed * vec[5:6, :] + vec[6:7, :], 0.0)
        bl[rows, :] = finished.astype(bf16)
        cot = cots[lax.div(r, 2), pl.ds(pl.multiple_of(lax.rem(r, 2) * 64, 64), 64), :].astype(f32)
        grad = jnp.where(ok, cot, 0.0)
        e = grad * vec[5:6, :]
        pull = jnp.mean(e, axis=-1, keepdims=True) + normed * jnp.mean(e * normed, axis=-1, keepdims=True)
        two = factor * (e - pull)
        settled[rows, :] = two
        sl[rows, :] = two.astype(bf16)
        for copy in row_stores(rows, r):
            copy.start()
        small_o[5:6, :] += jnp.sum(grad * normed, axis=0, keepdims=True)
        small_o[6:7, :] += jnp.sum(grad, axis=0, keepdims=True)
        small_o[7:8, :] += jnp.sum(two.astype(bf16).astype(f32), axis=0, keepdims=True)

    @pl.loop(0, 8)
    def _(i):
        cols = pl.ds(pl.multiple_of(i * 128, 128), 128)
        gct[cols, :] = sl[:, cols].T

    put(gct, gct_o)

    @pl.loop(0, 8)
    def _(r):
        for copy in row_stores(pl.ds(pl.multiple_of(r * 64, 64), 64), r):
            copy.wait()

    for copy in outs:
        copy.wait()
    for copy in x_sends + c_sends:
        copy.wait_send()

    @pl.loop(0, 16)
    def _(p):
        keep(0, p).wait()

    @pl.loop(16, 24)
    def _(p):
        keep(1, p).wait()


def forward_pass(sa, sm, se, sr, vs, x_loc, cot_loc, lengths):
    V, S = pltpu.VMEM, jax.ShapeDtypeStruct
    anywhere, vmem = pl.BlockSpec(memory_space=pl.ANY), pl.BlockSpec(memory_space=pltpu.VMEM)
    blocks = (4, 2, 2, 2)
    outs = [
        (S((16, *blocks, 32, 512), bf16), anywhere),
        (S((*blocks, 128, D), bf16), anywhere),
        (S((16, D), f32), vmem),
        (S((D, 512), bf16), anywhere),
        (S((3, 512, D), bf16), anywhere),
        (S((8, 2, 512), f32), vmem),
        (S((D, 512), bf16), anywhere),
        (S((512, D), f32), anywhere),
        (S((512, 128), f32), vmem),
        (S((D, 512), bf16), anywhere),
        (S((512, FF), bf16), anywhere),
        (S((512, FF), bf16), anywhere),
        (S((512, D), f32), anywhere),
        (S((512, D), bf16), anywhere),
        (S((512, D), bf16), anywhere),
        (S((D, 512), bf16), anywhere),
        (S((8, D), f32), vmem),
    ]
    dma = pltpu.SemaphoreType.DMA
    return pl.pallas_call(
        forward_kernel,
        out_shape=[o[0] for o in outs],
        out_specs=[o[1] for o in outs],
        in_specs=[vmem] * 5 + [anywhere] * 2 + [pl.BlockSpec(memory_space=pltpu.SMEM)],
        scratch_shapes=[
            V((16, *blocks, 32, 512), bf16),
            V((8, *blocks, 128, 128), bf16),
            V((*blocks, 16, 128), bf16),
            V((4, 128, D), bf16),
            V((4, 128, D), bf16),
            V((3, 512, D), bf16),
            V((D, 512), bf16),
            V((512, D), bf16),
            V((512, D), f32),
            V((512, D), f32),
            V((512, D), f32),
            V((512, D), bf16),
            V((512, FF), bf16),
            V((512, FF), bf16),
            V((D, 512), bf16),
            V((D, 512), bf16),
            V((D, 512), bf16),
            V((6, 1, 512), f32),
            V((8, 1, 512), f32),
            dma((24, 6)),
            dma((24, 6)),
            dma((24,)),
            dma((6,)),
            dma((6,)),
            dma((2, 3)),
            dma((2, 3)),
            dma((2,)),
            dma((16,)),
            dma((8, 3)),
        ],
        compiler_params=pltpu.CompilerParams(
            collective_id=1, has_side_effects=True, vmem_limit_bytes=62 * 1024 * 1024
        ),
        name="forward_pass",
    )(sa, sm, se, sr, vs, x_loc, cot_loc, lengths)


SCATTER_LAGS = (0, 1, 3, 5, 7)
RING = 10


def backward_kernel(
    w1h, w2h, vec, xt_i, qkv_i, lse, bt_i, n1_i, f1, slt_i, act_i, gp_i, g2_i, res_i, gc_i, gct_i, small, lengths,
    res_o, ig_o, ga_o, gm_o, ge_o, gr_o, vg_o,
    act, gp, gc, gct, slt, xt, bt, qkv, gs, n1, wr, we, wm, wa,
    gh, r1, r2, r3, r4, h2, h3, ga, gm, ge, gr,
    vg, bg, v1, v2, v3, v4, vh,
    lsem, wrsem, wesem, ssem, rsem, stsem, vssem, vrsem, xssem, xrsem, xlsem,
):
    z, y, x, c = place()
    sh = x * 2 + c
    dp = z * 2 + y
    up = [lax.rem(z + k, 4) for k in (1, 2, 3)]

    loads = []

    def load(src, dst):
        copy = pltpu.make_async_copy(src, dst, lsem.at[len(loads)])
        copy.start()
        loads.append(copy)
        return copy

    got_gct, got_act = load(gct_i, gct), load(act_i, act)

    def wr_load(j):
        slot = lax.rem(j, 2) if not isinstance(j, int) else j % 2
        a, b = (lax.div(j, 2), lax.rem(j, 2)) if not isinstance(j, int) else (j // 2, j % 2)
        return pltpu.make_async_copy(w2h.at[a, b], wr.at[slot], wrsem.at[slot])

    def we_load(j):
        slot = lax.rem(j, 2) if not isinstance(j, int) else j % 2
        return pltpu.make_async_copy(w1h.at[8 + j], we.at[slot], wesem.at[slot])

    def remote(src, dst, s, r, to):
        return pltpu.make_async_remote_copy(src, dst, s, r, device_id=to, device_id_type=MESH)

    bar = pltpu.get_barrier_semaphore()
    others = [device(z, y, x, 1 - c), device(z, y, 1 - x, c), device(z, y, 1 - x, 1 - c), device(z, 1 - y, x, c)]
    others += [device(up[k], y, x, c) for k in range(3)]
    for other in others:
        pl.semaphore_signal(bar, inc=1, device_id=other, device_id_type=MESH)

    def mod(p, n):
        return p % n if isinstance(p, int) else lax.rem(p, n)

    def copies(p, core, stage):
        own = gh.at[mod(p, RING)]
        R1, R2, R3, R4 = r1.at[mod(p, 8)], r2.at[mod(p, 8)], r3.at[mod(p, 8)], r4.at[mod(p, 8)]
        H2, H3 = h2.at[mod(p, 4)], h3.at[mod(p, 4)]

        def send(slot, a, b, to):
            return remote(a, b, ssem.at[p, slot], rsem.at[p, slot], to)

        if stage == 0:
            return [send(0, own.at[:, :, :, 1 - c], R1, device(z, y, x, 1 - c))]
        if core == 0:
            if stage == 1:
                return [send(1, own.at[:, :, 1 - x, c], R2, device(z, y, 1 - x, c))]
            if stage == 2:
                return [send(2, H2.at[:, 1 - y], R3.at[pl.ds(0, 4)], device(z, 1 - y, x, c))]
            return [send(3 + k, H3.at[up[k]], R4.at[k], device(up[k], y, x, c)) for k in range(3)]
        if stage == 1:
            return [send(1, own.at[:, 1 - y, :, c], R2, device(z, 1 - y, x, c))]
        if stage == 2:
            return [send(3 + k, H2.at[up[k]], R3.at[pl.ds(2 * k, 2)], device(up[k], y, x, c)) for k in range(3)]
        return [send(2, H3.at[1 - x], R4.at[0], device(z, y, 1 - x, c))]

    def wide(v):
        return v.astype(f32)

    def store(p, kind):
        def at(n, width):
            return pl.ds(pl.multiple_of(n * width, width), width)

        if kind == 0:
            ref, out, index = gr, gr_o, (ALL, at(p, 128))
        elif kind == 1:
            ref, out, index = ge, ge_o, (ALL, at(p - 8, 512))
        elif kind == 2:
            ref, out, index = gm, gm_o, (ALL, at(p - 16, 512))
        else:
            ref, out, index = ga, ga_o, ((p - 18) // 2, ALL, at((p - 18) % 2, 512))
        return ref, index, pltpu.make_async_copy(ref.at[index], out.at[index], stsem.at[p])

    kinds = ((0, 0, 8), (1, 8, 16), (2, 16, 18), (3, 18, 24))

    def close(p, g):
        for kind, low, high in kinds:

            def run(kind=kind):
                ref, index, out = store(p, kind)
                if kind == 0:
                    tall = jnp.concatenate([g[:, n * 128 : n * 128 + 128] for n in range(4)], axis=0)
                    ref[index] = tall.T
                else:
                    ref[index] = g
                out.start()

            when(within(p, low, high), run)

    def arrive(p, core, stage):
        GH = gh.at[mod(p, RING)]
        R1, R2, R3, R4 = r1.at[mod(p, 8)], r2.at[mod(p, 8)], r3.at[mod(p, 8)], r4.at[mod(p, 8)]
        H2, H3 = h2.at[mod(p, 4)], h3.at[mod(p, 4)]
        if stage > 0:
            for copy in copies(p, core, stage - 1):
                copy.wait()
        if stage == 1:

            @pl.loop(0, 4)
            def _(a):
                GH[a, :, :, c] = GH[a, :, :, c] + R1[a]

        elif stage == 2:

            @pl.loop(0, 4)
            def _(a):
                mine = GH[a, :, x, c] if core == 0 else GH[a, y, :, c]
                H2[a] = mine + R2[a]

        elif stage == 3 and core == 0:

            H3[...] = H2[:, y] + R3[0:4]

        elif stage == 3:

            @pl.loop(0, 2)
            def _(a):
                H3[a] = (wide(H2[z, a]) + wide(R3[a]) + wide(R3[2 + a]) + wide(R3[4 + a])).astype(bf16)

        elif stage == 4 and core == 0:
            close(p, wide(H3[z]) + wide(R4[0]) + wide(R4[1]) + wide(R4[2]))
        elif stage == 4:
            close(p, wide(H3[x]) + wide(R4[0]))
        if stage < 4:
            for copy in copies(p, core, stage):
                copy.start()

    def tick(t):
        for stage in (4, 3, 2, 1, 0):
            p = t - SCATTER_LAGS[stage]

            def run(p=p, stage=stage):
                if stage == 0:
                    arrive(p, 0, 0)
                else:
                    pl.when(c == 0)(lambda: arrive(p, 0, stage))
                    pl.when(c == 1)(lambda: arrive(p, 1, stage))

            when(within(p, 0, 24), run)

    def exchange(src, dst, which):
        sends = []
        for k in (1, 2, 3):
            to = lax.rem(sh + k, 4)
            rows = pl.ds(pl.multiple_of(to * 128, 128), 128)
            sends.append(
                remote(src.at[rows], dst.at[sh], xssem.at[which, k - 1], xrsem.at[which, k - 1], (dp, to))
            )
        rows = pl.ds(pl.multiple_of(sh * 128, 128), 128)
        sends_own = pltpu.make_async_copy(src.at[rows], dst.at[sh], xlsem.at[which])
        sends_own.start()
        return [*sends, sends_own]

    used = lengths[sh]
    moved = []

    got_two, got_gc = load(g2_i, gs), load(gc_i, gc)
    wr_load(0).start()
    we_load(0).start()
    got_gp, got_sl = load(gp_i, gp), load(slt_i, slt)
    got_gct.wait()
    got_act.wait()
    for part in range(4):

        @pl.loop(0, 8)
        def _(j):
            cols = pl.ds(pl.multiple_of(j * 512, 512), 512)
            got = dot(gct[part * 256 : part * 256 + 256, :], act[:, cols]).astype(bf16)
            for n in range(2):
                for k in range(4):
                    for g in range(4):
                        row = n * 128 + g * 32
                        gh[part * 2 + n, lax.div(j, 2), lax.rem(j, 2), k // 2, k % 2, :, g * 128 : g * 128 + 128] = got[
                            row : row + 32, k * 128 : k * 128 + 128
                        ]

        if part == 0:
            pl.semaphore_wait(bar, len(others))
            moved += exchange(res_i, res_o, 0)
        tick(part)
        if part == 3:
            moved[0].start()

    got_two.wait()
    got_gc.wait()
    got_gp.wait()
    got_sl.wait()
    got_n1, got_bt, got_wm = load(n1_i, n1), load(bt_i, bt), load(w1h.at[pl.ds(6, 2)], wm)
    got_qkv, got_xt, got_wa = load(qkv_i, qkv), load(xt_i, xt), load(w1h.at[pl.ds(0, 6)], wa)

    def produce(p, left, right):
        got = dot(left, right).astype(bf16)
        gh[mod(p, RING)] = got.reshape(4, 2, 2, 2, 32, 512)

    @pl.loop(0, 8)
    def _(j):
        @pl.when(j < 7)
        def _():
            wr_load(j + 1).start()
            we_load(j + 1).start()

        cols = pl.ds(pl.multiple_of(j * 512, 512), 512)
        slot = lax.rem(j, 2)
        wr_load(j).wait()
        got = dot(gc[...], wr[slot].reshape(512, D), 1, 1) * gp[:, cols].astype(f32)
        low = got.astype(bf16)
        gp[:, cols] = low
        bg[j] = jnp.sum(low.astype(f32), axis=0, keepdims=True)
        produce(8 + j, slt[...], gp[:, cols])
        we_load(j).wait()
        gs[...] += dot(gp[:, cols], we[slot].reshape(D, 512), 1, 1)
        tick(4 + j)


    vg[...] = jnp.zeros((16, D), f32)
    moved[1].start()
    vg[5:8, :] = small[5:8, :]
    for j in range(8):
        vg[8 + j // 2 : 9 + j // 2, (j % 2) * 512 : (j % 2) * 512 + 512] = bg[j]
    got_n1.wait()

    @pl.loop(0, 8)
    def _(r):
        rows = pl.ds(pl.multiple_of(r * 64, 64), 64)
        grad, normed = gs[rows, :], n1[rows, :]
        vg[3:4, :] += jnp.sum(grad * normed, axis=0, keepdims=True)
        vg[4:5, :] += jnp.sum(grad, axis=0, keepdims=True)
        e = grad * vec[3:4, :]
        pull = jnp.mean(e, axis=-1, keepdims=True) + normed * jnp.mean(e * normed, axis=-1, keepdims=True)
        one = f1[rows, 0:1] * (e - pull)
        gs[rows, :] = one
        low = one.astype(bf16)
        gc[rows, :] = low
        vg[2:3, :] += jnp.sum(low.astype(f32), axis=0, keepdims=True)

    tick(12)
    got_bt.wait()
    got_wm.wait()
    for h in range(2):
        produce(16 + h, bt[...], gc[:, h * 512 : h * 512 + 512])
    for h in range(2):
        rows = slice(h * 256, h * 256 + 256)
        back = dot(gc[rows, 0:512], wm[0].reshape(D, 512), 1, 1) + dot(gc[rows, 512:D], wm[1].reshape(D, 512), 1, 1)
        act[rows, 3 * D : 4 * D] = back.astype(bf16)

    got_qkv.wait()
    lane = lax.broadcasted_iota(jnp.int32, (1, 128), 1)
    key_ok = lax.broadcasted_iota(jnp.int32, (512, 1), 0) < used

    @pl.loop(0, 8)
    def _(i):
        @pl.when(lax.rem(i, 2) == 0)
        def _():
            tick(13 + lax.div(i, 2))

        start = pl.multiple_of(i * 128, 128)
        cols = pl.ds(start, 128)
        q2, k2, v2 = qkv[0, :, cols], qkv[1, :, cols], qkv[2, :, cols]
        db = act[:, pl.ds(pl.multiple_of(3 * D + i * 128, 128), 128)]
        k_t = k2.T
        dk = jnp.zeros((512, 128), f32)
        dv = jnp.zeros((512, 128), f32)
        turned = []
        for h in range(2):
            mine = (lane < 64) if h == 0 else (lane >= 64)
            qm = jnp.where(mine, q2, jnp.zeros_like(q2))
            dm = jnp.where(mine, db, jnp.zeros_like(db))
            parts = []
            for b in range(2):
                qb, gb = qm[b * 256 : b * 256 + 256], dm[b * 256 : b * 256 + 256]
                s = jnp.where(key_ok, dot(k2, qb, 1, 1) * (HD**-0.5), masked_score)
                share = jnp.exp(s - lse[i, h : h + 1, b * 256 : b * 256 + 256])
                gshare = dot(v2, gb, 1, 1)
                inner = jnp.sum(share * gshare, axis=0, keepdims=True)
                gscore = (share * (gshare - inner)).astype(bf16)
                dv = dv + dot(share.astype(bf16), gb)
                dk = dk + dot(gscore, qb)
                parts.append(dot(k_t[h * 64 : h * 64 + 64], gscore))
            turned.append(jnp.concatenate(parts, axis=1))
        dq = jnp.concatenate(turned, axis=0).T
        for n, (value, scale) in enumerate(((dq, HD**-0.5), (dk, HD**-0.5), (dv, 1.0))):
            low = (value * scale).astype(bf16)
            act[:, pl.ds(pl.multiple_of(n * D + i * 128, 128), 128)] = low
            if n != 1:
                vg[n // 2 : n // 2 + 1, cols] = jnp.sum(low.astype(f32), axis=0, keepdims=True)

    got_xt.wait()
    got_wa.wait()

    def vector_copies(stage):
        if stage == 0:
            return [remote(vg, v1, vssem.at[0], vrsem.at[0], device(z, y, x, 1 - c))]
        if stage == 1:
            return [remote(vg, v2, vssem.at[1], vrsem.at[1], device(z, y, 1 - x, c))]
        if stage == 2:
            return [remote(vh.at[:, 1 - y], v3, vssem.at[2], vrsem.at[2], device(z, 1 - y, x, c))]
        return [
            remote(vh.at[up[k], y], v4.at[k], vssem.at[3 + k], vrsem.at[3 + k], device(up[k], y, x, c))
            for k in range(3)
        ]

    def vector_step(stage):
        if stage > 0:
            for copy in vector_copies(stage - 1):
                copy.wait()
        if stage == 1:
            vg[...] += v1[...]
        elif stage == 2:
            vg[...] += v2[...]
            for g in range(8):
                vh[g // 2, g % 2] = vg[:, g * 128 : g * 128 + 128]
        elif stage == 3:
            for a in range(4):
                vh[a, y] += v3[a]
        elif stage == 4:
            vg_o[...] = vh[z, y] + v4[0] + v4[1] + v4[2]
        if stage < 4:
            for copy in vector_copies(stage):
                copy.start()

    vector_step(0)
    tick(17)
    moved[2].start()

    @pl.loop(0, 6)
    def _(i):
        cols = pl.ds(pl.multiple_of(i * 512, 512), 512)
        gs[...] += dot(act[:, cols], wa[i].reshape(D, 512), 1, 1)

    gc[...] = gs[...].astype(bf16)
    moved += exchange(gc, ig_o, 1)

    for i in range(6):
        produce(18 + i, xt[...], act[:, i * 512 : i * 512 + 512])
        tick(18 + i)
        if 18 + i in (20, 22, 24):
            moved[4 + (20, 22, 24).index(18 + i)].start()
        if i % 2:
            vector_step((i + 1) // 2)

    for t in range(24, 24 + SCATTER_LAGS[4]):
        tick(t)
        if t in (20, 22, 24):
            moved[4 + (20, 22, 24).index(t)].start()
        if t == 25:
            vector_step(4)

    for copy in moved:
        copy.wait()

    for kind, low, high in kinds:

        @pl.loop(low, high)
        def _(p):
            store(p, kind)[2].wait()


def backward_pass(kept, lengths):
    V, S = pltpu.VMEM, jax.ShapeDtypeStruct
    anywhere, vmem = pl.BlockSpec(memory_space=pl.ANY), pl.BlockSpec(memory_space=pltpu.VMEM)
    dma = pltpu.SemaphoreType.DMA
    shapes = [(3, 32, D), (32, D), (32, FF), (128, D)]
    near = [2, 5, 8, 16]
    return pl.pallas_call(
        backward_kernel,
        out_shape=[S((4, 128, D), bf16), S((4, 128, D), bf16)]
        + [S(s, f32) for s in shapes]
        + [S((16, 128), f32)],
        out_specs=[anywhere] * 6 + [vmem],
        in_specs=[vmem if n in near else anywhere for n in range(17)]
        + [pl.BlockSpec(memory_space=pltpu.SMEM)],
        scratch_shapes=[
            V((512, FF), bf16),
            V((512, FF), bf16),
            V((512, D), bf16),
            V((D, 512), bf16),
            V((D, 512), bf16),
            V((D, 512), bf16),
            V((D, 512), bf16),
            V((3, 512, D), bf16),
            V((512, D), f32),
            V((512, D), f32),
            V((2, 2, 2, 128, D), bf16),
            V((2, 4, 2, 2, 2, 32, 512), bf16),
            V((2, 4, 2, 2, 2, 32, 512), bf16),
            V((6, 4, 2, 2, 2, 32, 512), bf16),
            V((RING, 4, 2, 2, 2, 32, 512), bf16),
            V((8, 4, 2, 2, 32, 512), bf16),
            V((8, 4, 2, 32, 512), bf16),
            V((8, 6, 32, 512), bf16),
            V((8, 3, 32, 512), bf16),
            V((4, 4, 2, 32, 512), bf16),
            V((4, 4, 32, 512), bf16),
            *[V(s, f32) for s in shapes],
            V((16, D), f32),
            V((8, 1, 512), f32),
            V((16, D), f32),
            V((16, D), f32),
            V((4, 16, 128), f32),
            V((3, 16, 128), f32),
            V((4, 2, 16, 128), f32),
            dma((24,)),
            dma((2,)),
            dma((2,)),
            dma((24, 6)),
            dma((24, 6)),
            dma((24,)),
            dma((6,)),
            dma((6,)),
            dma((2, 3)),
            dma((2, 3)),
            dma((2,)),
        ],
        compiler_params=pltpu.CompilerParams(
            collective_id=2, has_side_effects=True, vmem_limit_bytes=62 * 1024 * 1024
        ),
        name="backward_pass",
    )(*kept, lengths)


def finish_kernel(*refs):
    ins, outs, held, wide, sems = refs[:22], refs[22:40], refs[40:58], refs[58], refs[59:]
    vg, mine, small = ins[0], lax.axis_index("shard"), ins[1:4]
    gains, big = ins[4:8], ins[8:20]
    moved = ins[20:22]
    isem, osem = sems

    def load(n, src):
        copy = pltpu.make_async_copy(src, held[n], isem.at[n])
        copy.start()
        return copy

    def save(n, dst):
        copy = pltpu.make_async_copy(held[n], dst, osem.at[n])
        copy.start()
        return copy

    order = (1, 0, 2, 3)
    loads = {}
    for k in order:
        loads[k] = [load(k, gains[k])] + [load(4 + 3 * k + n, big[3 * k + n]) for n in range(3)]
    passed = [load(16 + n, moved[n]) for n in range(2)]
    saves = []

    def adam(w, m, u, g, rate, decay):
        first = beta_one * m + (1.0 - beta_one) * g
        second = beta_two * u + (1.0 - beta_two) * g * g
        root = jnp.sqrt(second * (1.0 / (1.0 - beta_two**STEP))) + adam_eps
        return first, second, w - rate * (first * (1.0 / (1.0 - beta_one**STEP)) / root + decay * w)

    for k in order:
        for copy in loads[k]:
            copy.wait()
        w, m, u = held[4 + 3 * k : 7 + 3 * k]
        new = adam(w[...], m[...], u[...], held[k][...], rates[k], matrix_decay)
        m[...], u[...], w[...] = new
        saves += [save(5 + 3 * k, outs[2 + 3 * k]), save(6 + 3 * k, outs[3 + 3 * k]), save(4 + 3 * k, outs[4 + 3 * k])]
    passed[0].wait()
    saves.append(save(16, outs[0]))
    passed[1].wait()
    wide[...] = held[17][...].astype(f32)
    saves.append(pltpu.make_async_copy(wide, outs[1], osem.at[17]))
    saves[-1].start()
    grad = pltpu.roll(vg[...], lax.rem(4 - mine, 4) * 32, 1)[0:NV, 0:32]
    outs[14][...], outs[15][...], outs[16][...] = adam(small[0][...], small[1][...], small[2][...], grad, rates[4], 0.0)
    outs[17][...] = grad[2:3, :]
    for copy in saves:
        copy.wait()


def finish_step(masters, firsts, seconds, result, input_gradient, gradients, vector_gradient):
    V, S = pltpu.VMEM, jax.ShapeDtypeStruct
    anywhere, vmem = pl.BlockSpec(memory_space=pl.ANY), pl.BlockSpec(memory_space=pltpu.VMEM)
    big = [t[n] for n in range(4) for t in (masters, firsts, seconds)]
    moved = [S(t.shape, t.dtype) for t in (result, input_gradient)]
    outs = [moved[0], S(moved[1].shape, f32)] + [S(t.shape, f32) for t in big] + [S((NV, 32), f32)] * 3 + [S((1, 32), f32)]
    dma = pltpu.SemaphoreType.DMA
    *done, bias = pl.pallas_call(
        finish_kernel,
        out_shape=outs,
        out_specs=[anywhere] * 14 + [vmem] * 4,
        in_specs=[vmem] * 4 + [anywhere] * 18,
        scratch_shapes=[V(t.shape, f32) for t in gradients]
        + [V(t.shape, f32) for t in big]
        + [V(t.shape, t.dtype) for t in moved]
        + [V(moved[1].shape, f32)]
        + [dma((18,)), dma((18,))],
        compiler_params=pltpu.CompilerParams(vmem_limit_bytes=62 * 1024 * 1024),
        name="finish_step",
    )(vector_gradient, masters[4], firsts[4], seconds[4], *gradients, *big, result, input_gradient)
    return (*done, bias[0])


def product(left_side, right_side):
    return jnp.einsum("sri,ij->srj", left_side, right_side, preferred_element_type=f32)


def product_back(gradient, right_side):
    return jnp.einsum("srj,ij->sri", gradient, right_side, preferred_element_type=f32)


def outer_sum(left_side, gradient):
    return jnp.einsum("sri,srj->ij", left_side, gradient, preferred_element_type=f32)


def sum_rows(tensor):
    return jnp.sum(tensor.astype(f32), axis=(0, 1))


def split_heads(tensor):
    return tensor.reshape(tensor.shape[0], tensor.shape[1], -1, HD)


def norm_forward(tensor, gain, shift):
    center = tensor - jnp.mean(tensor, axis=-1, keepdims=True)
    spread = jnp.mean(center * center, axis=-1, keepdims=True)
    factor = lax.rsqrt(spread + norm_eps)
    normed = center * factor
    return (normed * gain + shift, normed, factor)


def norm_backward(gradient, normed, factor, gain):
    grad_normed = gradient * gain
    return factor * (
        grad_normed
        - jnp.mean(grad_normed, axis=-1, keepdims=True)
        - normed * jnp.mean(grad_normed * normed, axis=-1, keepdims=True)
    )


def attention_core(queries, keys, values, key_valid):
    score_scale = HD ** (-0.5)
    scores = (
        jnp.einsum("sqhd,skhd->shqk", split_heads(queries), split_heads(keys), preferred_element_type=f32)
        * score_scale
    )
    scores = jnp.where(key_valid[:, None, None, :], scores, masked_score)
    row_peak = jnp.max(scores, axis=-1, keepdims=True)
    row_sum = jnp.sum(jnp.exp(scores - row_peak), axis=-1, keepdims=True)
    shares = jnp.exp(scores - (row_peak + jnp.log(row_sum)))
    shares_low = shares.astype(bf16)
    blended = jnp.einsum("shqk,skhd->sqhd", shares_low, split_heads(values), preferred_element_type=f32)
    blended = blended.reshape(queries.shape).astype(bf16)
    return (blended, shares, shares_low)


def attention_back(grad_blended, queries, keys, values, shares, shares_low):
    score_scale = HD ** (-0.5)
    heads_grad = split_heads(grad_blended)
    grad_shares = jnp.einsum("sqhd,skhd->shqk", heads_grad, split_heads(values), preferred_element_type=f32)
    share_dot = jnp.sum(shares * grad_shares, axis=-1, keepdims=True)
    grad_scores = (shares * (grad_shares - share_dot)).astype(bf16)
    grad_query = (
        jnp.einsum("shqk,skhd->sqhd", grad_scores, split_heads(keys), preferred_element_type=f32) * score_scale
    )
    key_part = (
        jnp.einsum("shqk,sqhd->skhd", grad_scores, split_heads(queries), preferred_element_type=f32) * score_scale
    )
    value_part = jnp.einsum("shqk,sqhd->skhd", shares_low, heads_grad, preferred_element_type=f32)
    return (
        grad_query.reshape(queries.shape).astype(bf16),
        key_part.reshape(keys.shape).astype(bf16),
        value_part.reshape(values.shape).astype(bf16),
    )


def adam_update(weight, first, second, gradient, rate, decay):
    first_new = beta_one * first + (1.0 - beta_one) * gradient
    second_new = beta_two * second + (1.0 - beta_two) * gradient * gradient
    first_hat = first_new / (1.0 - beta_one**STEP)
    second_hat = second_new / (1.0 - beta_two**STEP)
    weight_new = weight - rate * (first_hat / (jnp.sqrt(second_hat) + adam_eps) + decay * weight)
    return (first_new, second_new, weight_new)


def finish(result, input_gradient, masters, firsts, seconds, reduced):
    updated = []
    for number in range(5):
        decay = matrix_decay if number < 4 else 0.0
        updated += adam_update(
            masters[number], firsts[number], seconds[number], reduced[number], rates[number], decay
        )
    return (result, input_gradient, *updated, reduced[4][2])


def local_fast(inputs, cotangent, lengths, *states):
    masters, firsts, seconds = states[0::3], states[1::3], states[2::3]
    kept = forward_pass(*masters, inputs, cotangent, lengths)
    result, input_gradient, *gradients, vector_gradient = backward_pass(kept, lengths)
    return finish_step(masters, firsts, seconds, result, input_gradient, gradients, vector_gradient)


def local_any(inputs, cotangent, lengths, *states):
    masters, firsts, seconds = states[0::3], states[1::3], states[2::3]
    attend_low, mixing_low, expand_low, reduce_low = [w.astype(bf16) for w in masters[:4]]
    attend_full = lax.all_gather(attend_low, ("dp", "shard"), axis=1, tiled=True)
    mixing_full, expand_full, reduce_full = [
        lax.all_gather(w, ("dp", "shard"), axis=0, tiled=True) for w in (mixing_low, expand_low, reduce_low)
    ]
    vec = lax.all_gather(masters[4].astype(bf16), ("dp", "shard"), axis=1, tiled=True).astype(f32)

    block_in = lax.all_to_all(inputs, "shard", split_axis=0, concat_axis=1, tiled=True)
    block_cot = lax.all_to_all(cotangent, "shard", split_axis=0, concat_axis=1, tiled=True)
    count, length = block_in.shape[0], block_in.shape[1]
    used = lax.dynamic_slice_in_dim(lengths, lax.axis_index("shard") * count, count)
    valid = jnp.arange(length)[None, :] < used[:, None]
    row_valid = valid.astype(f32)

    queries = (product(block_in, attend_full[0]) + vec[0]).astype(bf16)
    keys = product(block_in, attend_full[1]).astype(bf16)
    values = (product(block_in, attend_full[2]) + vec[1]).astype(bf16)
    blended, shares, shares_low = attention_core(queries, keys, values, valid)
    attended = product(blended, mixing_full) + vec[2]
    settled, normed_one, factor_one = norm_forward(block_in.astype(f32) + attended, vec[3], vec[4])
    settled_low = settled.astype(bf16)
    expanded = product(settled_low, expand_full) + vec[8:].reshape(FF)
    activated = jax.nn.gelu(expanded, approximate=False).astype(bf16)
    contracted = product(activated, reduce_full) + vec[7]
    finished, normed_two, factor_two = norm_forward(settled + contracted, vec[5], vec[6])
    result = (finished * row_valid[:, :, None]).astype(bf16)
    result = lax.all_to_all(result, "shard", split_axis=1, concat_axis=0, tiled=True)

    grad_out = block_cot.astype(f32) * row_valid[:, :, None]
    gain_two = sum_rows(grad_out * normed_two)
    shift_two = sum_rows(grad_out)
    grad_two = norm_backward(grad_out, normed_two, factor_two, vec[5])
    grad_contract = grad_two.astype(bf16)
    grad_reduce = outer_sum(activated, grad_contract)
    bias_reduce = sum_rows(grad_contract)
    grad_active = product_back(grad_contract, reduce_full)
    gelu_pull = jax.vjp(functools.partial(jax.nn.gelu, approximate=False), expanded)[1]
    grad_expanded = gelu_pull(grad_active)[0].astype(bf16)
    grad_expand = outer_sum(settled_low, grad_expanded)
    bias_expand = sum_rows(grad_expanded)
    grad_settled = grad_two + product_back(grad_expanded, expand_full)
    gain_one = sum_rows(grad_settled * normed_one)
    shift_one = sum_rows(grad_settled)
    grad_one = norm_backward(grad_settled, normed_one, factor_one, vec[3])
    grad_attended = grad_one.astype(bf16)
    grad_mixing = outer_sum(blended, grad_attended)
    bias_mixing = sum_rows(grad_attended)
    grad_blended = product_back(grad_attended, mixing_full).astype(bf16)
    query_grad, key_grad, value_grad = attention_back(grad_blended, queries, keys, values, shares, shares_low)
    grad_attend = jnp.stack([outer_sum(block_in, g) for g in (query_grad, key_grad, value_grad)])
    input_gradient = (
        grad_one
        + product_back(query_grad, attend_full[0])
        + product_back(key_grad, attend_full[1])
        + product_back(value_grad, attend_full[2])
    )
    input_gradient = lax.all_to_all(input_gradient, "shard", split_axis=1, concat_axis=0, tiled=True)
    small_rows = [sum_rows(query_grad), sum_rows(value_grad), bias_mixing, gain_one, shift_one, gain_two, shift_two]
    small_rows = jnp.stack([*small_rows, bias_reduce])
    grad_vectors = jnp.concatenate([small_rows, bias_expand.reshape(NV - 8, D)], axis=0)

    reduced = [lax.psum_scatter(grad_attend, ("dp", "shard"), scatter_dimension=1, tiled=True)]
    for g in (grad_mixing, grad_expand, grad_reduce):
        reduced.append(lax.psum_scatter(g, ("dp", "shard"), scatter_dimension=0, tiled=True))
    reduced = (*reduced, lax.psum_scatter(grad_vectors, ("dp", "shard"), scatter_dimension=1, tiled=True))
    return finish(result, input_gradient, masters, firsts, seconds, reduced)


def solution(mesh):
    fast = mesh.shape["dp"] == 8 and mesh.shape["shard"] == 4
    rows = P("dp", "shard", None)
    both = ("dp", "shard")
    middle, first, last = P(None, both, None), P(both, None), P(None, both)
    states = [middle] * 3 + [first] * 9 + [last] * 3
    return jax.shard_map(
        local_fast if fast else local_any,
        mesh=mesh,
        in_specs=(rows, rows, P("dp"), *states),
        out_specs=(rows, rows, *states, P(both)),
        check_vma=False,
    )
```

```python
import functools

import jax
import jax.numpy as jnp
from jax import lax
from jax.experimental import pallas as pl
from jax.experimental.pallas import tpu as pltpu
from jax.sharding import PartitionSpec as P

D = 1024
HD = 64
FF = 4096
STEP = 10
NV = 12
MESH = pl.DeviceIdType.MESH
ALL = slice(None)

beta_one = 0.9
beta_two = 0.999
adam_eps = 1e-08
norm_eps = 1e-05
matrix_decay = 0.01
masked_score = -1e30
rates = (0.06, 1.0, 0.06, 0.03, 0.5)
bf16 = jnp.bfloat16
f32 = jnp.float32


def place():
    dp = lax.axis_index("dp")
    sh = lax.axis_index("shard")
    return lax.div(dp, 2), lax.rem(dp, 2), lax.div(sh, 2), lax.rem(sh, 2)


def device(z, y, x, c):
    return (z * 2 + y, x * 2 + c)


GATHER_ORDER = ("zyx", "xzy")
EARLY_ORDER = ("zyx", "yzx")
EARLY = 2


def orders(p, c):
    early = isinstance(p, int) and p < EARLY
    return [(c == core, (EARLY_ORDER if early else GATHER_ORDER)[core]) for core in range(2)]


def dot(a, b, left=1, right=0):
    return lax.dot_general(a, b, (((left,), (right,)), ((), ())), preferred_element_type=f32)


def when(cond, run):
    if isinstance(cond, bool):
        if cond:
            run()
    else:
        pl.when(cond)(run)


def within(p, low, high):
    if isinstance(p, int):
        return low <= p < high
    return jnp.logical_and(p >= low, p < high)


def gelu_parts(v):
    u = jnp.abs(v) * (0.5**0.5)
    t = 1.0 / (1.0 + 0.3275911 * u)
    bell = jnp.exp(-u * u)
    poly = ((((1.061405429 * t - 1.453152027) * t + 1.421413741) * t - 0.284496736) * t + 0.254829592) * t
    tail = 0.5 * poly * bell
    share = jnp.where(v < 0.0, tail, 1.0 - tail)
    return v * share, share + v * bell * 0.3989422804014327


def forward_kernel(
    sa, sm, se, sr, vs, x_loc, cot_loc, lengths,
    w1h, w2h, vec, xt_o, qkv_o, lse_o, bt_o, n1_o, f1_o, slt_o, act_o, gp_o, g2_o, res_o, gc_o, gct_o, small_o,
    w1, w2, vg, xs, cots, qkv, bt, bl, att, settled, n1, sl, act, gp, xt, slt, gct, bias3, be3,
    ssem, rsem, wsem, vssem, vrsem, xssem, xrsem, xlsem, osem, rowsem,
):
    z, y, x, c = place()
    sh = x * 2 + c
    dp = z * 2 + y

    bar = pltpu.get_barrier_semaphore()
    others = [device(z, y, x, 1 - c), device(z, y, 1 - x, c), device(z, y, 1 - x, 1 - c), device(z, 1 - y, x, c)]
    others += [device(lax.rem(z + k, 4), y, x, c) for k in (1, 2, 3)]
    for other in others:
        pl.semaphore_signal(bar, inc=1, device_id=other, device_id_type=MESH)

    for m in range(3):
        for h in range(2):
            w1[m * 2 + h, z, y, x, c] = sa[m, :, h * 512 : h * 512 + 512].astype(bf16)
    for h in range(2):
        w1[6 + h, z, y, x, c] = sm[:, h * 512 : h * 512 + 512].astype(bf16)
    for j in range(8):
        w1[8 + j, z, y, x, c] = se[:, j * 512 : j * 512 + 512].astype(bf16)
        w2[j, z, y, x, c] = sr[:, j * 128 : j * 128 + 128].astype(bf16)
    vec[...] = jnp.zeros((16, D), f32)
    vec[0:12, 0:32] = vs[...]
    vg[z, y, x, c] = pltpu.roll(vec[:, 0:128], sh * 32, 1).astype(bf16)

    def remote(src, dst, s, r, to):
        return pltpu.make_async_remote_copy(src, dst, s, r, device_id=to, device_id_type=MESH)

    inner = jnp.logical_or(z == 1, z == 2)
    up = [lax.rem(z + k, 4) for k in (1, 2, 3)]

    def route(view, order, stage, s, r):
        if stage == 3:
            ref = view(ALL, ALL, ALL, c)
            return [remote(ref, ref, s(5), r(5), device(z, y, x, 1 - c))], "c"
        done, axis = order[:stage], order[stage]
        here = dict(z=z, y=y, x=x)
        ref = view(*[ALL if a in done else here[a] for a in "zyx"], c)
        if axis == "z":
            return [remote(ref, ref, s(k), r(k), device(up[k], y, x, c)) for k in range(3)], axis
        if axis == "y":
            return [remote(ref, ref, s(3), r(3), device(z, 1 - y, x, c))], axis
        return [remote(ref, ref, s(4), r(4), device(z, y, 1 - x, c))], axis

    def relay(view, order, s, r):
        done = order[: order.index("z")]
        here = dict(z=3 - z, y=y, x=x)
        ref = view(*[ALL if a in done else here[a] for a in "zyx"], c)
        remote(ref, ref, s(4 - 2 * z), r(4 - 2 * z), device(z, y, x, c)).wait_recv()
        remote(ref, ref, s(1), r(1), device(3 * (z - 1), y, x, c)).start()

    def leave(made, whole):
        copies, axis = made
        for k, copy in enumerate(copies):
            if axis == "z" and k == 1 and not whole:
                pl.when(jnp.logical_not(inner))(copy.start)
            else:
                copy.start()

    def arrive(made, whole):
        copies, axis = made
        for k, copy in enumerate(copies):
            copy.wait_send()
            if axis == "z" and k != 1 and not whole:
                pl.when(z != 2 - k // 2)(copy.wait_recv)
            else:
                copy.wait_recv()

    def place_of(kind, p):
        buf = w1 if kind == 0 else w2
        q = p if kind == 0 else p - 16
        return lambda *i: buf.at[(q, *i)], lambda k: ssem.at[p, k], lambda k: rsem.at[p, k]

    def step(p, parts, stage, whole=False):
        view, sends, receives = parts
        for cond, order in orders(p, c):

            def run(order=order):
                if stage > 0:
                    arrive(route(view, order, stage - 1, sends, receives), whole)
                if stage < 4:
                    leave(route(view, order, stage, sends, receives), whole)

            if stage == 4:
                run()
                break
            pl.when(cond)(run)

    def keep(kind, p):
        if kind == 0:
            return pltpu.make_async_copy(w1.at[p], w1h.at[p], wsem.at[p])
        cols = pl.ds((p - 16) * 128 if isinstance(p, int) else pl.multiple_of((p - 16) * 128, 128), 128)
        return pltpu.make_async_copy(w2.at[p - 16], w2h.at[:, :, :, :, :, cols], wsem.at[p])

    def tick(t):
        for stage in (4, 3, 2, 1, 0):
            p = t - 2 * stage
            for kind, low, high in ((0, 0, 16), (1, 16, 24)):

                def run(kind=kind, p=p, stage=stage):
                    step(p, place_of(kind, p), stage)
                    if stage == 4:
                        keep(kind, p).start()

                when(within(p, low, high), run)
        for stage in (2, 1, 0):
            p = t - 2 * stage - 1
            for kind, low, high in ((0, 0, 16), (1, 16, 24)):

                def run(kind=kind, p=p, stage=stage):
                    for cond, order in orders(p, c):
                        if order.index("z") == stage:
                            pl.when(jnp.logical_and(cond, inner))(lambda order=order: relay(place_of(kind, p)[0], order, *place_of(kind, p)[1:]))

                when(within(p, low, high), run)

    vectors_place = (lambda *i: vg.at[i], lambda k: vssem.at[k], lambda k: vrsem.at[k])

    def vector_step(stage):
        step(None, vectors_place, stage, whole=True)

    pl.semaphore_wait(bar, len(others))

    def exchange(src, dst, which):
        sends = []
        for k in (1, 2, 3):
            to = lax.rem(sh + k, 4)
            sends.append(
                remote(src.at[to], dst.at[sh], xssem.at[which, k - 1], xrsem.at[which, k - 1], (dp, to))
            )
        return sends, pltpu.make_async_copy(src.at[sh], dst.at[sh], xlsem.at[which])

    x_sends, x_own = exchange(x_loc, xs, 0)
    c_sends, c_own = exchange(cot_loc, cots, 1)
    vector_step(0)
    x_own.start()
    c_own.start()
    for t in range(8):
        tick(t)
        if t in (2, 4, 6):
            vector_step((2, 4, 6).index(t) + 1)
        if t in (0, 2, 4):
            x_sends[(0, 2, 4).index(t)].start()
    x_own.wait()
    for copy in x_sends:
        copy.wait_recv()
    used = lengths[sh]
    vector_step(4)

    for g in range(8):
        total = jnp.zeros((16, 128), f32)
        for i in range(4):
            total = total + vg[g // 2, g % 2, i // 2, i % 2].astype(f32)
        vec[:, g * 128 : g * 128 + 128] = total
    for h in range(2):
        bias3[h] = vec[0:1, h * 512 : h * 512 + 512]
        bias3[2 + h] = jnp.zeros((1, 512), f32)
        bias3[4 + h] = vec[1:2, h * 512 : h * 512 + 512]
    for j in range(8):
        be3[j] = vec[8 + j // 2 : 9 + j // 2, (j % 2) * 512 : (j % 2) * 512 + 512]

    outs = []

    def put(src, dst):
        copy = pltpu.make_async_copy(src, dst, osem.at[len(outs)])
        copy.start()
        outs.append(copy)

    @pl.loop(0, 8)
    def _(i):
        cols = pl.ds(pl.multiple_of(i * 128, 128), 128)
        for b in range(4):
            xt[cols, b * 128 : b * 128 + 128] = xs[b, :, cols].T

    put(xt, xt_o)

    for i in range(6):
        tick(8 + i)
        if i == 4:
            c_sends[0].start()
        got = dot(xs[...].reshape(512, D), w1[i].reshape(D, 512)) + bias3[i]
        qkv[i // 2, :, (i % 2) * 512 : (i % 2) * 512 + 512] = got.astype(bf16)

    put(qkv, qkv_o)

    lane = lax.broadcasted_iota(jnp.int32, (1, 128), 1)
    key_ok = lax.broadcasted_iota(jnp.int32, (512, 1), 0) < used

    @pl.loop(0, 8)
    def _(i):
        @pl.when(lax.rem(i, 2) == 0)
        def _():
            tick(14 + lax.div(i, 2))

        cols = pl.ds(pl.multiple_of(i * 128, 128), 128)
        q2, k2, v2 = qkv[0, :, cols], qkv[1, :, cols], qkv[2, :, cols]
        v_t = v2.T
        for h in range(2):
            mine = (lane < 64) if h == 0 else (lane >= 64)
            qm = jnp.where(mine, q2, jnp.zeros_like(q2))
            for b in range(2):
                s = dot(k2, qm[b * 256 : b * 256 + 256], 1, 1)
                s = jnp.where(key_ok, s * (HD**-0.5), masked_score)
                peak = jnp.max(s, axis=0, keepdims=True)
                e = jnp.exp(s - peak)
                total = jnp.sum(e, axis=0, keepdims=True)
                shares = (e * (1.0 / total)).astype(bf16)
                lse_o[i, h : h + 1, b * 256 : b * 256 + 256] = peak + jnp.log(total)
                mixed = dot(v_t[h * 64 : h * 64 + 64], shares)
                bt[pl.ds(pl.multiple_of(i * 128, 128) + h * 64, 64), b * 256 : b * 256 + 256] = mixed.astype(bf16)
        bl[:, cols] = bt[pl.ds(pl.multiple_of(i * 128, 128), 128), :].T

    put(bt, bt_o)
    c_sends[1].start()

    @pl.loop(0, 2)
    def _(h):
        cols = pl.ds(pl.multiple_of(h * 512, 512), 512)
        att[:, cols] = dot(bl[...], w1[6 + h].reshape(D, 512))

    tick(18)

    @pl.loop(0, 8)
    def _(r):
        rows = pl.ds(pl.multiple_of(r * 64, 64), 64)
        inp = xs[lax.div(r, 2), pl.ds(pl.multiple_of(lax.rem(r, 2) * 64, 64), 64), :].astype(f32)
        t = inp + (att[rows, :] + vec[2:3, :])
        center = t - jnp.mean(t, axis=-1, keepdims=True)
        factor = lax.rsqrt(jnp.mean(center * center, axis=-1, keepdims=True) + norm_eps)
        normed = center * factor
        out = normed * vec[3:4, :] + vec[4:5, :]
        n1[rows, :] = normed
        f1_o[rows, :] = jnp.broadcast_to(factor, (64, 128))
        settled[rows, :] = out
        sl[rows, :] = out.astype(bf16)

    tick(19)
    c_sends[2].start()

    put(n1, n1_o)

    @pl.loop(0, 8)
    def _(i):
        cols = pl.ds(pl.multiple_of(i * 128, 128), 128)
        slt[cols, :] = sl[:, cols].T

    put(slt, slt_o)

    @pl.loop(0, 8)
    def _(j):
        @pl.when(lax.rem(j, 2) == 0)
        def _():
            tick(20 + lax.div(j, 2))

        cols = pl.ds(pl.multiple_of(j * 512, 512), 512)
        for r in range(2):
            rows = slice(r * 256, r * 256 + 256)
            got = dot(sl[rows, :], w1[8 + j].reshape(D, 512)) + be3[j]
            a, slope = gelu_parts(got)
            act[rows, cols] = a.astype(bf16)
            gp[rows, cols] = slope.astype(bf16)

    put(act, act_o)
    put(gp, gp_o)

    @pl.loop(0, 8)
    def _(j):
        tick(24 + j)
        cols = pl.ds(pl.multiple_of(j * 128, 128), 128)
        att[:, cols] = dot(act[...], w2[j].reshape(FF, 128))

    c_own.wait()
    for copy in c_sends:
        copy.wait_recv()
    small_o[...] = jnp.zeros((8, D), f32)

    def row_stores(rows, r):
        pairs = ((settled, g2_o), (bl, res_o), (sl, gc_o))
        return [pltpu.make_async_copy(a.at[rows], b.at[rows], rowsem.at[r, n]) for n, (a, b) in enumerate(pairs)]

    @pl.loop(0, 8)
    def _(r):
        rows = pl.ds(pl.multiple_of(r * 64, 64), 64)
        t = settled[rows, :] + (att[rows, :] + vec[7:8, :])
        center = t - jnp.mean(t, axis=-1, keepdims=True)
        factor = lax.rsqrt(jnp.mean(center * center, axis=-1, keepdims=True) + norm_eps)
        normed = center * factor
        ok = (lax.broadcasted_iota(jnp.int32, (64, 1), 0) + r * 64) < used
        finished = jnp.where(ok, normed * vec[5:6, :] + vec[6:7, :], 0.0)
        bl[rows, :] = finished.astype(bf16)
        cot = cots[lax.div(r, 2), pl.ds(pl.multiple_of(lax.rem(r, 2) * 64, 64), 64), :].astype(f32)
        grad = jnp.where(ok, cot, 0.0)
        e = grad * vec[5:6, :]
        pull = jnp.mean(e, axis=-1, keepdims=True) + normed * jnp.mean(e * normed, axis=-1, keepdims=True)
        two = factor * (e - pull)
        settled[rows, :] = two
        sl[rows, :] = two.astype(bf16)
        for copy in row_stores(rows, r):
            copy.start()
        small_o[5:6, :] += jnp.sum(grad * normed, axis=0, keepdims=True)
        small_o[6:7, :] += jnp.sum(grad, axis=0, keepdims=True)
        small_o[7:8, :] += jnp.sum(two.astype(bf16).astype(f32), axis=0, keepdims=True)

    @pl.loop(0, 8)
    def _(i):
        cols = pl.ds(pl.multiple_of(i * 128, 128), 128)
        gct[cols, :] = sl[:, cols].T

    put(gct, gct_o)

    @pl.loop(0, 8)
    def _(r):
        for copy in row_stores(pl.ds(pl.multiple_of(r * 64, 64), 64), r):
            copy.wait()

    for copy in outs:
        copy.wait()
    for copy in x_sends + c_sends:
        copy.wait_send()

    @pl.loop(0, 16)
    def _(p):
        keep(0, p).wait()

    @pl.loop(16, 24)
    def _(p):
        keep(1, p).wait()


def forward_pass(sa, sm, se, sr, vs, x_loc, cot_loc, lengths):
    V, S = pltpu.VMEM, jax.ShapeDtypeStruct
    anywhere, vmem = pl.BlockSpec(memory_space=pl.ANY), pl.BlockSpec(memory_space=pltpu.VMEM)
    blocks = (4, 2, 2, 2)
    outs = [
        (S((16, *blocks, 32, 512), bf16), anywhere),
        (S((*blocks, 128, D), bf16), anywhere),
        (S((16, D), f32), vmem),
        (S((D, 512), bf16), anywhere),
        (S((3, 512, D), bf16), anywhere),
        (S((8, 2, 512), f32), vmem),
        (S((D, 512), bf16), anywhere),
        (S((512, D), f32), anywhere),
        (S((512, 128), f32), vmem),
        (S((D, 512), bf16), anywhere),
        (S((512, FF), bf16), anywhere),
        (S((512, FF), bf16), anywhere),
        (S((512, D), f32), anywhere),
        (S((512, D), bf16), anywhere),
        (S((512, D), bf16), anywhere),
        (S((D, 512), bf16), anywhere),
        (S((8, D), f32), vmem),
    ]
    dma = pltpu.SemaphoreType.DMA
    return pl.pallas_call(
        forward_kernel,
        out_shape=[o[0] for o in outs],
        out_specs=[o[1] for o in outs],
        in_specs=[vmem] * 5 + [anywhere] * 2 + [pl.BlockSpec(memory_space=pltpu.SMEM)],
        scratch_shapes=[
            V((16, *blocks, 32, 512), bf16),
            V((8, *blocks, 128, 128), bf16),
            V((*blocks, 16, 128), bf16),
            V((4, 128, D), bf16),
            V((4, 128, D), bf16),
            V((3, 512, D), bf16),
            V((D, 512), bf16),
            V((512, D), bf16),
            V((512, D), f32),
            V((512, D), f32),
            V((512, D), f32),
            V((512, D), bf16),
            V((512, FF), bf16),
            V((512, FF), bf16),
            V((D, 512), bf16),
            V((D, 512), bf16),
            V((D, 512), bf16),
            V((6, 1, 512), f32),
            V((8, 1, 512), f32),
            dma((24, 6)),
            dma((24, 6)),
            dma((24,)),
            dma((6,)),
            dma((6,)),
            dma((2, 3)),
            dma((2, 3)),
            dma((2,)),
            dma((16,)),
            dma((8, 3)),
        ],
        compiler_params=pltpu.CompilerParams(
            collective_id=1, has_side_effects=True, vmem_limit_bytes=62 * 1024 * 1024
        ),
        name="forward_pass",
    )(sa, sm, se, sr, vs, x_loc, cot_loc, lengths)


SCATTER_LAGS = (0, 1, 3, 5, 7)
RING = 10


def backward_kernel(
    w1h, w2h, vec, xt_i, qkv_i, lse, bt_i, n1_i, f1, slt_i, act_i, gp_i, g2_i, res_i, gc_i, gct_i, small, lengths,
    res_o, ig_o, ga_o, gm_o, ge_o, gr_o, vg_o,
    act, gp, gc, gct, slt, xt, bt, qkv, gs, n1, wr, we, wm, wa,
    gh, r1, r2, r3, r4, h2, h3, ga, gm, ge, gr,
    vg, bg, v1, v2, v3, v4, vh,
    lsem, wrsem, wesem, ssem, rsem, stsem, vssem, vrsem, xssem, xrsem, xlsem,
):
    z, y, x, c = place()
    sh = x * 2 + c
    dp = z * 2 + y
    up = [lax.rem(z + k, 4) for k in (1, 2, 3)]

    loads = []

    def load(src, dst):
        copy = pltpu.make_async_copy(src, dst, lsem.at[len(loads)])
        copy.start()
        loads.append(copy)
        return copy

    got_gct, got_act = load(gct_i, gct), load(act_i, act)

    def wr_load(j):
        slot = lax.rem(j, 2) if not isinstance(j, int) else j % 2
        a, b = (lax.div(j, 2), lax.rem(j, 2)) if not isinstance(j, int) else (j // 2, j % 2)
        return pltpu.make_async_copy(w2h.at[a, b], wr.at[slot], wrsem.at[slot])

    def we_load(j):
        slot = lax.rem(j, 2) if not isinstance(j, int) else j % 2
        return pltpu.make_async_copy(w1h.at[8 + j], we.at[slot], wesem.at[slot])

    def remote(src, dst, s, r, to):
        return pltpu.make_async_remote_copy(src, dst, s, r, device_id=to, device_id_type=MESH)

    bar = pltpu.get_barrier_semaphore()
    others = [device(z, y, x, 1 - c), device(z, y, 1 - x, c), device(z, y, 1 - x, 1 - c), device(z, 1 - y, x, c)]
    others += [device(up[k], y, x, c) for k in range(3)]
    for other in others:
        pl.semaphore_signal(bar, inc=1, device_id=other, device_id_type=MESH)

    def mod(p, n):
        return p % n if isinstance(p, int) else lax.rem(p, n)

    def copies(p, core, stage):
        own = gh.at[mod(p, RING)]
        R1, R2, R3, R4 = r1.at[mod(p, 8)], r2.at[mod(p, 8)], r3.at[mod(p, 8)], r4.at[mod(p, 8)]
        H2, H3 = h2.at[mod(p, 4)], h3.at[mod(p, 4)]

        def send(slot, a, b, to):
            return remote(a, b, ssem.at[p, slot], rsem.at[p, slot], to)

        if stage == 0:
            return [send(0, own.at[:, :, :, 1 - c], R1, device(z, y, x, 1 - c))]
        if core == 0:
            if stage == 1:
                return [send(1, own.at[:, :, 1 - x, c], R2, device(z, y, 1 - x, c))]
            if stage == 2:
                return [send(2, H2.at[:, 1 - y], R3.at[pl.ds(0, 4)], device(z, 1 - y, x, c))]
            return [send(3 + k, H3.at[up[k]], R4.at[k], device(up[k], y, x, c)) for k in range(3)]
        if stage == 1:
            return [send(1, own.at[:, 1 - y, :, c], R2, device(z, 1 - y, x, c))]
        if stage == 2:
            return [send(3 + k, H2.at[up[k]], R3.at[pl.ds(2 * k, 2)], device(up[k], y, x, c)) for k in range(3)]
        return [send(2, H3.at[1 - x], R4.at[0], device(z, y, 1 - x, c))]

    def wide(v):
        return v.astype(f32)

    def store(p, kind):
        def at(n, width):
            return pl.ds(pl.multiple_of(n * width, width), width)

        if kind == 0:
            ref, out, index = gr, gr_o, (ALL, at(p, 128))
        elif kind == 1:
            ref, out, index = ge, ge_o, (ALL, at(p - 8, 512))
        elif kind == 2:
            ref, out, index = gm, gm_o, (ALL, at(p - 16, 512))
        else:
            ref, out, index = ga, ga_o, ((p - 18) // 2, ALL, at((p - 18) % 2, 512))
        return ref, index, pltpu.make_async_copy(ref.at[index], out.at[index], stsem.at[p])

    kinds = ((0, 0, 8), (1, 8, 16), (2, 16, 18), (3, 18, 24))

    def close(p, g):
        for kind, low, high in kinds:

            def run(kind=kind):
                ref, index, out = store(p, kind)
                if kind == 0:
                    tall = jnp.concatenate([g[:, n * 128 : n * 128 + 128] for n in range(4)], axis=0)
                    ref[index] = tall.T
                else:
                    ref[index] = g
                out.start()

            when(within(p, low, high), run)

    def arrive(p, core, stage):
        GH = gh.at[mod(p, RING)]
        R1, R2, R3, R4 = r1.at[mod(p, 8)], r2.at[mod(p, 8)], r3.at[mod(p, 8)], r4.at[mod(p, 8)]
        H2, H3 = h2.at[mod(p, 4)], h3.at[mod(p, 4)]
        if stage > 0:
            for copy in copies(p, core, stage - 1):
                copy.wait()
        if stage == 1:

            @pl.loop(0, 4)
            def _(a):
                GH[a, :, :, c] = GH[a, :, :, c] + R1[a]

        elif stage == 2:

            @pl.loop(0, 4)
            def _(a):
                mine = GH[a, :, x, c] if core == 0 else GH[a, y, :, c]
                H2[a] = mine + R2[a]

        elif stage == 3 and core == 0:

            H3[...] = H2[:, y] + R3[0:4]

        elif stage == 3:

            @pl.loop(0, 2)
            def _(a):
                H3[a] = (wide(H2[z, a]) + wide(R3[a]) + wide(R3[2 + a]) + wide(R3[4 + a])).astype(bf16)

        elif stage == 4 and core == 0:
            close(p, wide(H3[z]) + wide(R4[0]) + wide(R4[1]) + wide(R4[2]))
        elif stage == 4:
            close(p, wide(H3[x]) + wide(R4[0]))
        if stage < 4:
            for copy in copies(p, core, stage):
                copy.start()

    def tick(t):
        for stage in (4, 3, 2, 1, 0):
            p = t - SCATTER_LAGS[stage]

            def run(p=p, stage=stage):
                if stage == 0:
                    arrive(p, 0, 0)
                else:
                    pl.when(c == 0)(lambda: arrive(p, 0, stage))
                    pl.when(c == 1)(lambda: arrive(p, 1, stage))

            when(within(p, 0, 24), run)

    def exchange(src, dst, which):
        sends = []
        for k in (1, 2, 3):
            to = lax.rem(sh + k, 4)
            rows = pl.ds(pl.multiple_of(to * 128, 128), 128)
            sends.append(
                remote(src.at[rows], dst.at[sh], xssem.at[which, k - 1], xrsem.at[which, k - 1], (dp, to))
            )
        rows = pl.ds(pl.multiple_of(sh * 128, 128), 128)
        sends_own = pltpu.make_async_copy(src.at[rows], dst.at[sh], xlsem.at[which])
        sends_own.start()
        return [*sends, sends_own]

    used = lengths[sh]
    moved = []

    got_two, got_gc = load(g2_i, gs), load(gc_i, gc)
    wr_load(0).start()
    we_load(0).start()
    got_gp, got_sl = load(gp_i, gp), load(slt_i, slt)
    got_gct.wait()
    got_act.wait()
    for part in range(4):

        @pl.loop(0, 8)
        def _(j):
            cols = pl.ds(pl.multiple_of(j * 512, 512), 512)
            got = dot(gct[part * 256 : part * 256 + 256, :], act[:, cols]).astype(bf16)
            for n in range(2):
                for k in range(4):
                    for g in range(4):
                        row = n * 128 + g * 32
                        gh[part * 2 + n, lax.div(j, 2), lax.rem(j, 2), k // 2, k % 2, :, g * 128 : g * 128 + 128] = got[
                            row : row + 32, k * 128 : k * 128 + 128
                        ]

        if part == 0:
            pl.semaphore_wait(bar, len(others))
            moved += exchange(res_i, res_o, 0)
        tick(part)
        if part == 3:
            moved[0].start()

    got_two.wait()
    got_gc.wait()
    got_gp.wait()
    got_sl.wait()
    got_n1, got_bt, got_wm = load(n1_i, n1), load(bt_i, bt), load(w1h.at[pl.ds(6, 2)], wm)
    got_qkv, got_xt, got_wa = load(qkv_i, qkv), load(xt_i, xt), load(w1h.at[pl.ds(0, 6)], wa)

    def produce(p, left, right):
        got = dot(left, right).astype(bf16)
        gh[mod(p, RING)] = got.reshape(4, 2, 2, 2, 32, 512)

    @pl.loop(0, 8)
    def _(j):
        @pl.when(j < 7)
        def _():
            wr_load(j + 1).start()
            we_load(j + 1).start()

        cols = pl.ds(pl.multiple_of(j * 512, 512), 512)
        slot = lax.rem(j, 2)
        wr_load(j).wait()
        got = dot(gc[...], wr[slot].reshape(512, D), 1, 1) * gp[:, cols].astype(f32)
        low = got.astype(bf16)
        gp[:, cols] = low
        bg[j] = jnp.sum(low.astype(f32), axis=0, keepdims=True)
        produce(8 + j, slt[...], gp[:, cols])
        we_load(j).wait()
        gs[...] += dot(gp[:, cols], we[slot].reshape(D, 512), 1, 1)
        tick(4 + j)


    vg[...] = jnp.zeros((16, D), f32)
    vg[5:8, :] = small[5:8, :]
    for j in range(8):
        vg[8 + j // 2 : 9 + j // 2, (j % 2) * 512 : (j % 2) * 512 + 512] = bg[j]
    got_n1.wait()

    @pl.loop(0, 8)
    def _(r):
        rows = pl.ds(pl.multiple_of(r * 64, 64), 64)
        grad, normed = gs[rows, :], n1[rows, :]
        vg[3:4, :] += jnp.sum(grad * normed, axis=0, keepdims=True)
        vg[4:5, :] += jnp.sum(grad, axis=0, keepdims=True)
        e = grad * vec[3:4, :]
        pull = jnp.mean(e, axis=-1, keepdims=True) + normed * jnp.mean(e * normed, axis=-1, keepdims=True)
        one = f1[rows, 0:1] * (e - pull)
        gs[rows, :] = one
        low = one.astype(bf16)
        gc[rows, :] = low
        vg[2:3, :] += jnp.sum(low.astype(f32), axis=0, keepdims=True)

    tick(12)
    moved[1].start()
    got_bt.wait()
    got_wm.wait()
    for h in range(2):
        produce(16 + h, bt[...], gc[:, h * 512 : h * 512 + 512])
    for h in range(2):
        rows = slice(h * 256, h * 256 + 256)
        back = dot(gc[rows, 0:512], wm[0].reshape(D, 512), 1, 1) + dot(gc[rows, 512:D], wm[1].reshape(D, 512), 1, 1)
        act[rows, 3 * D : 4 * D] = back.astype(bf16)

    got_qkv.wait()
    lane = lax.broadcasted_iota(jnp.int32, (1, 128), 1)
    key_ok = lax.broadcasted_iota(jnp.int32, (512, 1), 0) < used

    @pl.loop(0, 8)
    def _(i):
        @pl.when(lax.rem(i, 2) == 0)
        def _():
            tick(13 + lax.div(i, 2))

        start = pl.multiple_of(i * 128, 128)
        cols = pl.ds(start, 128)
        q2, k2, v2 = qkv[0, :, cols], qkv[1, :, cols], qkv[2, :, cols]
        db = act[:, pl.ds(pl.multiple_of(3 * D + i * 128, 128), 128)]
        k_t = k2.T
        dk = jnp.zeros((512, 128), f32)
        dv = jnp.zeros((512, 128), f32)
        turned = []
        for h in range(2):
            mine = (lane < 64) if h == 0 else (lane >= 64)
            qm = jnp.where(mine, q2, jnp.zeros_like(q2))
            dm = jnp.where(mine, db, jnp.zeros_like(db))
            parts = []
            for b in range(2):
                qb, gb = qm[b * 256 : b * 256 + 256], dm[b * 256 : b * 256 + 256]
                s = jnp.where(key_ok, dot(k2, qb, 1, 1) * (HD**-0.5), masked_score)
                share = jnp.exp(s - lse[i, h : h + 1, b * 256 : b * 256 + 256])
                gshare = dot(v2, gb, 1, 1)
                inner = jnp.sum(share * gshare, axis=0, keepdims=True)
                gscore = (share * (gshare - inner)).astype(bf16)
                dv = dv + dot(share.astype(bf16), gb)
                dk = dk + dot(gscore, qb)
                parts.append(dot(k_t[h * 64 : h * 64 + 64], gscore))
            turned.append(jnp.concatenate(parts, axis=1))
        dq = jnp.concatenate(turned, axis=0).T
        for n, (value, scale) in enumerate(((dq, HD**-0.5), (dk, HD**-0.5), (dv, 1.0))):
            low = (value * scale).astype(bf16)
            act[:, pl.ds(pl.multiple_of(n * D + i * 128, 128), 128)] = low
            if n != 1:
                vg[n // 2 : n // 2 + 1, cols] = jnp.sum(low.astype(f32), axis=0, keepdims=True)

    got_xt.wait()
    got_wa.wait()

    def vector_copies(stage):
        if stage == 0:
            return [remote(vg, v1, vssem.at[0], vrsem.at[0], device(z, y, x, 1 - c))]
        if stage == 1:
            return [remote(vg, v2, vssem.at[1], vrsem.at[1], device(z, y, 1 - x, c))]
        if stage == 2:
            return [remote(vh.at[:, 1 - y], v3, vssem.at[2], vrsem.at[2], device(z, 1 - y, x, c))]
        return [
            remote(vh.at[up[k], y], v4.at[k], vssem.at[3 + k], vrsem.at[3 + k], device(up[k], y, x, c))
            for k in range(3)
        ]

    def vector_step(stage):
        if stage > 0:
            for copy in vector_copies(stage - 1):
                copy.wait()
        if stage == 1:
            vg[...] += v1[...]
        elif stage == 2:
            vg[...] += v2[...]
            for g in range(8):
                vh[g // 2, g % 2] = vg[:, g * 128 : g * 128 + 128]
        elif stage == 3:
            for a in range(4):
                vh[a, y] += v3[a]
        elif stage == 4:
            vg_o[...] = vh[z, y] + v4[0] + v4[1] + v4[2]
        if stage < 4:
            for copy in vector_copies(stage):
                copy.start()

    vector_step(0)
    tick(17)
    moved[2].start()

    @pl.loop(0, 6)
    def _(i):
        cols = pl.ds(pl.multiple_of(i * 512, 512), 512)
        gs[...] += dot(act[:, cols], wa[i].reshape(D, 512), 1, 1)

    gc[...] = gs[...].astype(bf16)
    moved += exchange(gc, ig_o, 1)

    for i in range(6):
        produce(18 + i, xt[...], act[:, i * 512 : i * 512 + 512])
        tick(18 + i)
        if 18 + i in (22, 24, 26):
            moved[4 + (22, 24, 26).index(18 + i)].start()
        if i % 2:
            vector_step((i + 1) // 2)

    for t in range(24, 24 + SCATTER_LAGS[4]):
        tick(t)
        if t in (22, 24, 26):
            moved[4 + (22, 24, 26).index(t)].start()
        if t == 25:
            vector_step(4)

    for copy in moved:
        copy.wait()

    for kind, low, high in kinds:

        @pl.loop(low, high)
        def _(p):
            store(p, kind)[2].wait()


def backward_pass(kept, lengths):
    V, S = pltpu.VMEM, jax.ShapeDtypeStruct
    anywhere, vmem = pl.BlockSpec(memory_space=pl.ANY), pl.BlockSpec(memory_space=pltpu.VMEM)
    dma = pltpu.SemaphoreType.DMA
    shapes = [(3, 32, D), (32, D), (32, FF), (128, D)]
    near = [2, 5, 8, 16]
    return pl.pallas_call(
        backward_kernel,
        out_shape=[S((4, 128, D), bf16), S((4, 128, D), bf16)]
        + [S(s, f32) for s in shapes]
        + [S((16, 128), f32)],
        out_specs=[anywhere] * 6 + [vmem],
        in_specs=[vmem if n in near else anywhere for n in range(17)]
        + [pl.BlockSpec(memory_space=pltpu.SMEM)],
        scratch_shapes=[
            V((512, FF), bf16),
            V((512, FF), bf16),
            V((512, D), bf16),
            V((D, 512), bf16),
            V((D, 512), bf16),
            V((D, 512), bf16),
            V((D, 512), bf16),
            V((3, 512, D), bf16),
            V((512, D), f32),
            V((512, D), f32),
            V((2, 2, 2, 128, D), bf16),
            V((2, 4, 2, 2, 2, 32, 512), bf16),
            V((2, 4, 2, 2, 2, 32, 512), bf16),
            V((6, 4, 2, 2, 2, 32, 512), bf16),
            V((RING, 4, 2, 2, 2, 32, 512), bf16),
            V((8, 4, 2, 2, 32, 512), bf16),
            V((8, 4, 2, 32, 512), bf16),
            V((8, 6, 32, 512), bf16),
            V((8, 3, 32, 512), bf16),
            V((4, 4, 2, 32, 512), bf16),
            V((4, 4, 32, 512), bf16),
            *[V(s, f32) for s in shapes],
            V((16, D), f32),
            V((8, 1, 512), f32),
            V((16, D), f32),
            V((16, D), f32),
            V((4, 16, 128), f32),
            V((3, 16, 128), f32),
            V((4, 2, 16, 128), f32),
            dma((24,)),
            dma((2,)),
            dma((2,)),
            dma((24, 6)),
            dma((24, 6)),
            dma((24,)),
            dma((6,)),
            dma((6,)),
            dma((2, 3)),
            dma((2, 3)),
            dma((2,)),
        ],
        compiler_params=pltpu.CompilerParams(
            collective_id=2, has_side_effects=True, vmem_limit_bytes=62 * 1024 * 1024
        ),
        name="backward_pass",
    )(*kept, lengths)


def finish_kernel(*refs):
    ins, outs, held, wide, sems = refs[:22], refs[22:40], refs[40:58], refs[58], refs[59:]
    vg, mine, small = ins[0], lax.axis_index("shard"), ins[1:4]
    gains, big = ins[4:8], ins[8:20]
    moved = ins[20:22]
    isem, osem = sems

    def load(n, src):
        copy = pltpu.make_async_copy(src, held[n], isem.at[n])
        copy.start()
        return copy

    def save(n, dst):
        copy = pltpu.make_async_copy(held[n], dst, osem.at[n])
        copy.start()
        return copy

    order = (1, 0, 2, 3)
    loads = {}
    for k in order:
        loads[k] = [load(k, gains[k])] + [load(4 + 3 * k + n, big[3 * k + n]) for n in range(3)]
    passed = [load(16 + n, moved[n]) for n in range(2)]
    saves = []

    def adam(w, m, u, g, rate, decay):
        first = beta_one * m + (1.0 - beta_one) * g
        second = beta_two * u + (1.0 - beta_two) * g * g
        root = jnp.sqrt(second * (1.0 / (1.0 - beta_two**STEP))) + adam_eps
        return first, second, w - rate * (first * (1.0 / (1.0 - beta_one**STEP)) / root + decay * w)

    for k in order:
        for copy in loads[k]:
            copy.wait()
        w, m, u = held[4 + 3 * k : 7 + 3 * k]
        new = adam(w[...], m[...], u[...], held[k][...], rates[k], matrix_decay)
        m[...], u[...], w[...] = new
        saves += [save(5 + 3 * k, outs[2 + 3 * k]), save(6 + 3 * k, outs[3 + 3 * k]), save(4 + 3 * k, outs[4 + 3 * k])]
    passed[0].wait()
    saves.append(save(16, outs[0]))
    passed[1].wait()
    wide[...] = held[17][...].astype(f32)
    saves.append(pltpu.make_async_copy(wide, outs[1], osem.at[17]))
    saves[-1].start()
    grad = pltpu.roll(vg[...], lax.rem(4 - mine, 4) * 32, 1)[0:NV, 0:32]
    outs[14][...], outs[15][...], outs[16][...] = adam(small[0][...], small[1][...], small[2][...], grad, rates[4], 0.0)
    outs[17][...] = grad[2:3, :]
    for copy in saves:
        copy.wait()


def finish_step(masters, firsts, seconds, result, input_gradient, gradients, vector_gradient):
    V, S = pltpu.VMEM, jax.ShapeDtypeStruct
    anywhere, vmem = pl.BlockSpec(memory_space=pl.ANY), pl.BlockSpec(memory_space=pltpu.VMEM)
    big = [t[n] for n in range(4) for t in (masters, firsts, seconds)]
    moved = [S(t.shape, t.dtype) for t in (result, input_gradient)]
    outs = [moved[0], S(moved[1].shape, f32)] + [S(t.shape, f32) for t in big] + [S((NV, 32), f32)] * 3 + [S((1, 32), f32)]
    dma = pltpu.SemaphoreType.DMA
    *done, bias = pl.pallas_call(
        finish_kernel,
        out_shape=outs,
        out_specs=[anywhere] * 14 + [vmem] * 4,
        in_specs=[vmem] * 4 + [anywhere] * 18,
        scratch_shapes=[V(t.shape, f32) for t in gradients]
        + [V(t.shape, f32) for t in big]
        + [V(t.shape, t.dtype) for t in moved]
        + [V(moved[1].shape, f32)]
        + [dma((18,)), dma((18,))],
        compiler_params=pltpu.CompilerParams(vmem_limit_bytes=62 * 1024 * 1024),
        name="finish_step",
    )(vector_gradient, masters[4], firsts[4], seconds[4], *gradients, *big, result, input_gradient)
    return (*done, bias[0])


def product(left_side, right_side):
    return jnp.einsum("sri,ij->srj", left_side, right_side, preferred_element_type=f32)


def product_back(gradient, right_side):
    return jnp.einsum("srj,ij->sri", gradient, right_side, preferred_element_type=f32)


def outer_sum(left_side, gradient):
    return jnp.einsum("sri,srj->ij", left_side, gradient, preferred_element_type=f32)


def sum_rows(tensor):
    return jnp.sum(tensor.astype(f32), axis=(0, 1))


def split_heads(tensor):
    return tensor.reshape(tensor.shape[0], tensor.shape[1], -1, HD)


def norm_forward(tensor, gain, shift):
    center = tensor - jnp.mean(tensor, axis=-1, keepdims=True)
    spread = jnp.mean(center * center, axis=-1, keepdims=True)
    factor = lax.rsqrt(spread + norm_eps)
    normed = center * factor
    return (normed * gain + shift, normed, factor)


def norm_backward(gradient, normed, factor, gain):
    grad_normed = gradient * gain
    return factor * (
        grad_normed
        - jnp.mean(grad_normed, axis=-1, keepdims=True)
        - normed * jnp.mean(grad_normed * normed, axis=-1, keepdims=True)
    )


def attention_core(queries, keys, values, key_valid):
    score_scale = HD ** (-0.5)
    scores = (
        jnp.einsum("sqhd,skhd->shqk", split_heads(queries), split_heads(keys), preferred_element_type=f32)
        * score_scale
    )
    scores = jnp.where(key_valid[:, None, None, :], scores, masked_score)
    row_peak = jnp.max(scores, axis=-1, keepdims=True)
    row_sum = jnp.sum(jnp.exp(scores - row_peak), axis=-1, keepdims=True)
    shares = jnp.exp(scores - (row_peak + jnp.log(row_sum)))
    shares_low = shares.astype(bf16)
    blended = jnp.einsum("shqk,skhd->sqhd", shares_low, split_heads(values), preferred_element_type=f32)
    blended = blended.reshape(queries.shape).astype(bf16)
    return (blended, shares, shares_low)


def attention_back(grad_blended, queries, keys, values, shares, shares_low):
    score_scale = HD ** (-0.5)
    heads_grad = split_heads(grad_blended)
    grad_shares = jnp.einsum("sqhd,skhd->shqk", heads_grad, split_heads(values), preferred_element_type=f32)
    share_dot = jnp.sum(shares * grad_shares, axis=-1, keepdims=True)
    grad_scores = (shares * (grad_shares - share_dot)).astype(bf16)
    grad_query = (
        jnp.einsum("shqk,skhd->sqhd", grad_scores, split_heads(keys), preferred_element_type=f32) * score_scale
    )
    key_part = (
        jnp.einsum("shqk,sqhd->skhd", grad_scores, split_heads(queries), preferred_element_type=f32) * score_scale
    )
    value_part = jnp.einsum("shqk,sqhd->skhd", shares_low, heads_grad, preferred_element_type=f32)
    return (
        grad_query.reshape(queries.shape).astype(bf16),
        key_part.reshape(keys.shape).astype(bf16),
        value_part.reshape(values.shape).astype(bf16),
    )


def adam_update(weight, first, second, gradient, rate, decay):
    first_new = beta_one * first + (1.0 - beta_one) * gradient
    second_new = beta_two * second + (1.0 - beta_two) * gradient * gradient
    first_hat = first_new / (1.0 - beta_one**STEP)
    second_hat = second_new / (1.0 - beta_two**STEP)
    weight_new = weight - rate * (first_hat / (jnp.sqrt(second_hat) + adam_eps) + decay * weight)
    return (first_new, second_new, weight_new)


def finish(result, input_gradient, masters, firsts, seconds, reduced):
    updated = []
    for number in range(5):
        decay = matrix_decay if number < 4 else 0.0
        updated += adam_update(
            masters[number], firsts[number], seconds[number], reduced[number], rates[number], decay
        )
    return (result, input_gradient, *updated, reduced[4][2])


def local_fast(inputs, cotangent, lengths, *states):
    masters, firsts, seconds = states[0::3], states[1::3], states[2::3]
    kept = forward_pass(*masters, inputs, cotangent, lengths)
    result, input_gradient, *gradients, vector_gradient = backward_pass(kept, lengths)
    return finish_step(masters, firsts, seconds, result, input_gradient, gradients, vector_gradient)


def local_any(inputs, cotangent, lengths, *states):
    masters, firsts, seconds = states[0::3], states[1::3], states[2::3]
    attend_low, mixing_low, expand_low, reduce_low = [w.astype(bf16) for w in masters[:4]]
    attend_full = lax.all_gather(attend_low, ("dp", "shard"), axis=1, tiled=True)
    mixing_full, expand_full, reduce_full = [
        lax.all_gather(w, ("dp", "shard"), axis=0, tiled=True) for w in (mixing_low, expand_low, reduce_low)
    ]
    vec = lax.all_gather(masters[4].astype(bf16), ("dp", "shard"), axis=1, tiled=True).astype(f32)

    block_in = lax.all_to_all(inputs, "shard", split_axis=0, concat_axis=1, tiled=True)
    block_cot = lax.all_to_all(cotangent, "shard", split_axis=0, concat_axis=1, tiled=True)
    count, length = block_in.shape[0], block_in.shape[1]
    used = lax.dynamic_slice_in_dim(lengths, lax.axis_index("shard") * count, count)
    valid = jnp.arange(length)[None, :] < used[:, None]
    row_valid = valid.astype(f32)

    queries = (product(block_in, attend_full[0]) + vec[0]).astype(bf16)
    keys = product(block_in, attend_full[1]).astype(bf16)
    values = (product(block_in, attend_full[2]) + vec[1]).astype(bf16)
    blended, shares, shares_low = attention_core(queries, keys, values, valid)
    attended = product(blended, mixing_full) + vec[2]
    settled, normed_one, factor_one = norm_forward(block_in.astype(f32) + attended, vec[3], vec[4])
    settled_low = settled.astype(bf16)
    expanded = product(settled_low, expand_full) + vec[8:].reshape(FF)
    activated = jax.nn.gelu(expanded, approximate=False).astype(bf16)
    contracted = product(activated, reduce_full) + vec[7]
    finished, normed_two, factor_two = norm_forward(settled + contracted, vec[5], vec[6])
    result = (finished * row_valid[:, :, None]).astype(bf16)
    result = lax.all_to_all(result, "shard", split_axis=1, concat_axis=0, tiled=True)

    grad_out = block_cot.astype(f32) * row_valid[:, :, None]
    gain_two = sum_rows(grad_out * normed_two)
    shift_two = sum_rows(grad_out)
    grad_two = norm_backward(grad_out, normed_two, factor_two, vec[5])
    grad_contract = grad_two.astype(bf16)
    grad_reduce = outer_sum(activated, grad_contract)
    bias_reduce = sum_rows(grad_contract)
    grad_active = product_back(grad_contract, reduce_full)
    gelu_pull = jax.vjp(functools.partial(jax.nn.gelu, approximate=False), expanded)[1]
    grad_expanded = gelu_pull(grad_active)[0].astype(bf16)
    grad_expand = outer_sum(settled_low, grad_expanded)
    bias_expand = sum_rows(grad_expanded)
    grad_settled = grad_two + product_back(grad_expanded, expand_full)
    gain_one = sum_rows(grad_settled * normed_one)
    shift_one = sum_rows(grad_settled)
    grad_one = norm_backward(grad_settled, normed_one, factor_one, vec[3])
    grad_attended = grad_one.astype(bf16)
    grad_mixing = outer_sum(blended, grad_attended)
    bias_mixing = sum_rows(grad_attended)
    grad_blended = product_back(grad_attended, mixing_full).astype(bf16)
    query_grad, key_grad, value_grad = attention_back(grad_blended, queries, keys, values, shares, shares_low)
    grad_attend = jnp.stack([outer_sum(block_in, g) for g in (query_grad, key_grad, value_grad)])
    input_gradient = (
        grad_one
        + product_back(query_grad, attend_full[0])
        + product_back(key_grad, attend_full[1])
        + product_back(value_grad, attend_full[2])
    )
    input_gradient = lax.all_to_all(input_gradient, "shard", split_axis=1, concat_axis=0, tiled=True)
    small_rows = [sum_rows(query_grad), sum_rows(value_grad), bias_mixing, gain_one, shift_one, gain_two, shift_two]
    small_rows = jnp.stack([*small_rows, bias_reduce])
    grad_vectors = jnp.concatenate([small_rows, bias_expand.reshape(NV - 8, D)], axis=0)

    reduced = [lax.psum_scatter(grad_attend, ("dp", "shard"), scatter_dimension=1, tiled=True)]
    for g in (grad_mixing, grad_expand, grad_reduce):
        reduced.append(lax.psum_scatter(g, ("dp", "shard"), scatter_dimension=0, tiled=True))
    reduced = (*reduced, lax.psum_scatter(grad_vectors, ("dp", "shard"), scatter_dimension=1, tiled=True))
    return finish(result, input_gradient, masters, firsts, seconds, reduced)


def solution(mesh):
    fast = mesh.shape["dp"] == 8 and mesh.shape["shard"] == 4
    rows = P("dp", "shard", None)
    both = ("dp", "shard")
    middle, first, last = P(None, both, None), P(both, None), P(None, both)
    states = [middle] * 3 + [first] * 9 + [last] * 3
    return jax.shard_map(
        local_fast if fast else local_any,
        mesh=mesh,
        in_specs=(rows, rows, P("dp"), *states),
        out_specs=(rows, rows, *states, P(both)),
        check_vma=False,
    )
```

```python
import functools

import jax
import jax.numpy as jnp
from jax import lax
from jax.experimental import pallas as pl
from jax.experimental.pallas import tpu as pltpu
from jax.sharding import PartitionSpec as P

D = 1024
HD = 64
FF = 4096
STEP = 10
NV = 12
MESH = pl.DeviceIdType.MESH
ALL = slice(None)

beta_one = 0.9
beta_two = 0.999
adam_eps = 1e-08
norm_eps = 1e-05
matrix_decay = 0.01
masked_score = -1e30
rates = (0.06, 1.0, 0.06, 0.03, 0.5)
bf16 = jnp.bfloat16
f32 = jnp.float32


def place():
    dp = lax.axis_index("dp")
    sh = lax.axis_index("shard")
    return lax.div(dp, 2), lax.rem(dp, 2), lax.div(sh, 2), lax.rem(sh, 2)


def device(z, y, x, c):
    return (z * 2 + y, x * 2 + c)


GATHER_ORDER = ("zyx", "xzy")
EARLY_ORDER = ("zyx", "yzx")
EARLY = 2


def orders(p, c):
    early = isinstance(p, int) and p < EARLY
    return [(c == core, (EARLY_ORDER if early else GATHER_ORDER)[core]) for core in range(2)]


def dot(a, b, left=1, right=0):
    return lax.dot_general(a, b, (((left,), (right,)), ((), ())), preferred_element_type=f32)


def when(cond, run):
    if isinstance(cond, bool):
        if cond:
            run()
    else:
        pl.when(cond)(run)


def within(p, low, high):
    if isinstance(p, int):
        return low <= p < high
    return jnp.logical_and(p >= low, p < high)


def gelu_parts(v):
    u = jnp.abs(v) * (0.5**0.5)
    t = 1.0 / (1.0 + 0.3275911 * u)
    bell = jnp.exp(-u * u)
    poly = ((((1.061405429 * t - 1.453152027) * t + 1.421413741) * t - 0.284496736) * t + 0.254829592) * t
    tail = 0.5 * poly * bell
    share = jnp.where(v < 0.0, tail, 1.0 - tail)
    return v * share, share + v * bell * 0.3989422804014327


def forward_kernel(
    sa, sm, se, sr, vs, x_loc, cot_loc, lengths,
    w1h, w2h, vec, xt_o, qkv_o, lse_o, bt_o, n1_o, f1_o, slt_o, act_o, gp_o, g2_o, res_o, gc_o, gct_o, small_o,
    w1, w2, vg, xs, cots, qkv, bt, bl, att, settled, n1, sl, act, gp, xt, slt, gct, bias3, be3,
    ssem, rsem, wsem, vssem, vrsem, xssem, xrsem, xlsem, osem, rowsem,
):
    z, y, x, c = place()
    sh = x * 2 + c
    dp = z * 2 + y

    bar = pltpu.get_barrier_semaphore()
    others = [device(z, y, x, 1 - c), device(z, y, 1 - x, c), device(z, y, 1 - x, 1 - c), device(z, 1 - y, x, c)]
    others += [device(lax.rem(z + k, 4), y, x, c) for k in (1, 2, 3)]
    for other in others:
        pl.semaphore_signal(bar, inc=1, device_id=other, device_id_type=MESH)

    for m in range(3):
        for h in range(2):
            w1[m * 2 + h, z, y, x, c] = sa[m, :, h * 512 : h * 512 + 512].astype(bf16)
    for h in range(2):
        w1[6 + h, z, y, x, c] = sm[:, h * 512 : h * 512 + 512].astype(bf16)
    for j in range(8):
        w1[8 + j, z, y, x, c] = se[:, j * 512 : j * 512 + 512].astype(bf16)
        w2[j, z, y, x, c] = sr[:, j * 128 : j * 128 + 128].astype(bf16)
    vec[...] = jnp.zeros((16, D), f32)
    vec[0:12, 0:32] = vs[...]
    vg[z, y, x, c] = pltpu.roll(vec[:, 0:128], sh * 32, 1).astype(bf16)

    def remote(src, dst, s, r, to):
        return pltpu.make_async_remote_copy(src, dst, s, r, device_id=to, device_id_type=MESH)

    inner = jnp.logical_or(z == 1, z == 2)
    up = [lax.rem(z + k, 4) for k in (1, 2, 3)]

    def route(view, order, stage, s, r):
        if stage == 3:
            ref = view(ALL, ALL, ALL, c)
            return [remote(ref, ref, s(5), r(5), device(z, y, x, 1 - c))], "c"
        done, axis = order[:stage], order[stage]
        here = dict(z=z, y=y, x=x)
        ref = view(*[ALL if a in done else here[a] for a in "zyx"], c)
        if axis == "z":
            return [remote(ref, ref, s(k), r(k), device(up[k], y, x, c)) for k in range(3)], axis
        if axis == "y":
            return [remote(ref, ref, s(3), r(3), device(z, 1 - y, x, c))], axis
        return [remote(ref, ref, s(4), r(4), device(z, y, 1 - x, c))], axis

    def relay(view, order, s, r):
        done = order[: order.index("z")]
        here = dict(z=3 - z, y=y, x=x)
        ref = view(*[ALL if a in done else here[a] for a in "zyx"], c)
        remote(ref, ref, s(4 - 2 * z), r(4 - 2 * z), device(z, y, x, c)).wait_recv()
        remote(ref, ref, s(1), r(1), device(3 * (z - 1), y, x, c)).start()

    def leave(made, whole):
        copies, axis = made
        for k, copy in enumerate(copies):
            if axis == "z" and k == 1 and not whole:
                pl.when(jnp.logical_not(inner))(copy.start)
            else:
                copy.start()

    def arrive(made, whole):
        copies, axis = made
        for k, copy in enumerate(copies):
            copy.wait_send()
            if axis == "z" and k != 1 and not whole:
                pl.when(z != 2 - k // 2)(copy.wait_recv)
            else:
                copy.wait_recv()

    def place_of(kind, p):
        buf = w1 if kind == 0 else w2
        q = p if kind == 0 else p - 16
        return lambda *i: buf.at[(q, *i)], lambda k: ssem.at[p, k], lambda k: rsem.at[p, k]

    def step(p, parts, stage, whole=False):
        view, sends, receives = parts
        for cond, order in orders(p, c):

            def run(order=order):
                if stage > 0:
                    arrive(route(view, order, stage - 1, sends, receives), whole)
                if stage < 4:
                    leave(route(view, order, stage, sends, receives), whole)

            if stage == 4:
                run()
                break
            pl.when(cond)(run)

    def keep(kind, p):
        if kind == 0:
            return pltpu.make_async_copy(w1.at[p], w1h.at[p], wsem.at[p])
        cols = pl.ds((p - 16) * 128 if isinstance(p, int) else pl.multiple_of((p - 16) * 128, 128), 128)
        return pltpu.make_async_copy(w2.at[p - 16], w2h.at[:, :, :, :, :, cols], wsem.at[p])

    def tick(t):
        for stage in (4, 3, 2, 1, 0):
            p = t - 2 * stage
            for kind, low, high in ((0, 0, 16), (1, 16, 24)):

                def run(kind=kind, p=p, stage=stage):
                    step(p, place_of(kind, p), stage)
                    if stage == 4:
                        keep(kind, p).start()

                when(within(p, low, high), run)
        for stage in (2, 1, 0):
            p = t - 2 * stage - 1
            for kind, low, high in ((0, 0, 16), (1, 16, 24)):

                def run(kind=kind, p=p, stage=stage):
                    for cond, order in orders(p, c):
                        if order.index("z") == stage:
                            pl.when(jnp.logical_and(cond, inner))(lambda order=order: relay(place_of(kind, p)[0], order, *place_of(kind, p)[1:]))

                when(within(p, low, high), run)

    vectors_place = (lambda *i: vg.at[i], lambda k: vssem.at[k], lambda k: vrsem.at[k])

    def vector_step(stage):
        step(None, vectors_place, stage, whole=True)

    pl.semaphore_wait(bar, len(others))

    def exchange(src, dst, which):
        sends = []
        for k in (1, 2, 3):
            to = lax.rem(sh + k, 4)
            sends.append(
                remote(src.at[to], dst.at[sh], xssem.at[which, k - 1], xrsem.at[which, k - 1], (dp, to))
            )
        return sends, pltpu.make_async_copy(src.at[sh], dst.at[sh], xlsem.at[which])

    x_sends, x_own = exchange(x_loc, xs, 0)
    c_sends, c_own = exchange(cot_loc, cots, 1)
    vector_step(0)
    x_own.start()
    c_own.start()
    for t in range(8):
        tick(t)
        if t in (2, 4, 6):
            vector_step((2, 4, 6).index(t) + 1)
        if t in (0, 2, 4):
            x_sends[(0, 2, 4).index(t)].start()
    x_own.wait()
    for copy in x_sends:
        copy.wait_recv()
    used = lengths[sh]
    vector_step(4)

    for g in range(8):
        total = jnp.zeros((16, 128), f32)
        for i in range(4):
            total = total + vg[g // 2, g % 2, i // 2, i % 2].astype(f32)
        vec[:, g * 128 : g * 128 + 128] = total
    for h in range(2):
        bias3[h] = vec[0:1, h * 512 : h * 512 + 512]
        bias3[2 + h] = jnp.zeros((1, 512), f32)
        bias3[4 + h] = vec[1:2, h * 512 : h * 512 + 512]
    for j in range(8):
        be3[j] = vec[8 + j // 2 : 9 + j // 2, (j % 2) * 512 : (j % 2) * 512 + 512]

    outs = []

    def put(src, dst):
        copy = pltpu.make_async_copy(src, dst, osem.at[len(outs)])
        copy.start()
        outs.append(copy)

    @pl.loop(0, 8)
    def _(i):
        cols = pl.ds(pl.multiple_of(i * 128, 128), 128)
        for b in range(4):
            xt[cols, b * 128 : b * 128 + 128] = xs[b, :, cols].T

    put(xt, xt_o)

    for i in range(6):
        tick(8 + i)
        if i == 4:
            c_sends[0].start()
        got = dot(xs[...].reshape(512, D), w1[i].reshape(D, 512)) + bias3[i]
        qkv[i // 2, :, (i % 2) * 512 : (i % 2) * 512 + 512] = got.astype(bf16)

    put(qkv, qkv_o)

    lane = lax.broadcasted_iota(jnp.int32, (1, 128), 1)
    key_ok = lax.broadcasted_iota(jnp.int32, (512, 1), 0) < used

    @pl.loop(0, 8)
    def _(i):
        @pl.when(lax.rem(i, 2) == 0)
        def _():
            tick(14 + lax.div(i, 2))

        cols = pl.ds(pl.multiple_of(i * 128, 128), 128)
        q2, k2, v2 = qkv[0, :, cols], qkv[1, :, cols], qkv[2, :, cols]
        v_t = v2.T
        for h in range(2):
            mine = (lane < 64) if h == 0 else (lane >= 64)
            qm = jnp.where(mine, q2, jnp.zeros_like(q2))
            for b in range(2):
                s = dot(k2, qm[b * 256 : b * 256 + 256], 1, 1)
                s = jnp.where(key_ok, s * (HD**-0.5), masked_score)
                peak = jnp.max(s, axis=0, keepdims=True)
                e = jnp.exp(s - peak)
                total = jnp.sum(e, axis=0, keepdims=True)
                shares = (e * (1.0 / total)).astype(bf16)
                lse_o[i, h : h + 1, b * 256 : b * 256 + 256] = peak + jnp.log(total)
                mixed = dot(v_t[h * 64 : h * 64 + 64], shares)
                bt[pl.ds(pl.multiple_of(i * 128, 128) + h * 64, 64), b * 256 : b * 256 + 256] = mixed.astype(bf16)
        bl[:, cols] = bt[pl.ds(pl.multiple_of(i * 128, 128), 128), :].T

    put(bt, bt_o)
    c_sends[1].start()

    @pl.loop(0, 2)
    def _(h):
        cols = pl.ds(pl.multiple_of(h * 512, 512), 512)
        att[:, cols] = dot(bl[...], w1[6 + h].reshape(D, 512))

    tick(18)

    @pl.loop(0, 8)
    def _(r):
        rows = pl.ds(pl.multiple_of(r * 64, 64), 64)
        inp = xs[lax.div(r, 2), pl.ds(pl.multiple_of(lax.rem(r, 2) * 64, 64), 64), :].astype(f32)
        t = inp + (att[rows, :] + vec[2:3, :])
        center = t - jnp.mean(t, axis=-1, keepdims=True)
        factor = lax.rsqrt(jnp.mean(center * center, axis=-1, keepdims=True) + norm_eps)
        normed = center * factor
        out = normed * vec[3:4, :] + vec[4:5, :]
        n1[rows, :] = normed
        f1_o[rows, :] = jnp.broadcast_to(factor, (64, 128))
        settled[rows, :] = out
        sl[rows, :] = out.astype(bf16)

    tick(19)
    c_sends[2].start()

    put(n1, n1_o)

    @pl.loop(0, 8)
    def _(i):
        cols = pl.ds(pl.multiple_of(i * 128, 128), 128)
        slt[cols, :] = sl[:, cols].T

    put(slt, slt_o)

    @pl.loop(0, 8)
    def _(j):
        @pl.when(lax.rem(j, 2) == 0)
        def _():
            tick(20 + lax.div(j, 2))

        cols = pl.ds(pl.multiple_of(j * 512, 512), 512)
        for r in range(2):
            rows = slice(r * 256, r * 256 + 256)
            got = dot(sl[rows, :], w1[8 + j].reshape(D, 512)) + be3[j]
            a, slope = gelu_parts(got)
            act[rows, cols] = a.astype(bf16)
            gp[rows, cols] = slope.astype(bf16)

    put(act, act_o)
    put(gp, gp_o)

    @pl.loop(0, 8)
    def _(j):
        tick(24 + j)
        cols = pl.ds(pl.multiple_of(j * 128, 128), 128)
        att[:, cols] = dot(act[...], w2[j].reshape(FF, 128))

    c_own.wait()
    for copy in c_sends:
        copy.wait_recv()
    small_o[...] = jnp.zeros((8, D), f32)

    def row_stores(rows, r):
        pairs = ((settled, g2_o), (bl, res_o), (sl, gc_o))
        return [pltpu.make_async_copy(a.at[rows], b.at[rows], rowsem.at[r, n]) for n, (a, b) in enumerate(pairs)]

    @pl.loop(0, 8)
    def _(r):
        rows = pl.ds(pl.multiple_of(r * 64, 64), 64)
        t = settled[rows, :] + (att[rows, :] + vec[7:8, :])
        center = t - jnp.mean(t, axis=-1, keepdims=True)
        factor = lax.rsqrt(jnp.mean(center * center, axis=-1, keepdims=True) + norm_eps)
        normed = center * factor
        ok = (lax.broadcasted_iota(jnp.int32, (64, 1), 0) + r * 64) < used
        finished = jnp.where(ok, normed * vec[5:6, :] + vec[6:7, :], 0.0)
        bl[rows, :] = finished.astype(bf16)
        cot = cots[lax.div(r, 2), pl.ds(pl.multiple_of(lax.rem(r, 2) * 64, 64), 64), :].astype(f32)
        grad = jnp.where(ok, cot, 0.0)
        e = grad * vec[5:6, :]
        pull = jnp.mean(e, axis=-1, keepdims=True) + normed * jnp.mean(e * normed, axis=-1, keepdims=True)
        two = factor * (e - pull)
        settled[rows, :] = two
        sl[rows, :] = two.astype(bf16)
        for copy in row_stores(rows, r):
            copy.start()
        small_o[5:6, :] += jnp.sum(grad * normed, axis=0, keepdims=True)
        small_o[6:7, :] += jnp.sum(grad, axis=0, keepdims=True)
        small_o[7:8, :] += jnp.sum(two.astype(bf16).astype(f32), axis=0, keepdims=True)

        @pl.when(lax.rem(r, 2) == 1)
        def _():
            start = pl.multiple_of(lax.div(r, 2) * 128, 128)
            gct[:, pl.ds(start, 128)] = sl[pl.ds(start, 128), :].T

    put(gct, gct_o)

    @pl.loop(0, 8)
    def _(r):
        for copy in row_stores(pl.ds(pl.multiple_of(r * 64, 64), 64), r):
            copy.wait()

    for copy in outs:
        copy.wait()
    for copy in x_sends + c_sends:
        copy.wait_send()

    @pl.loop(0, 16)
    def _(p):
        keep(0, p).wait()

    @pl.loop(16, 24)
    def _(p):
        keep(1, p).wait()


def forward_pass(sa, sm, se, sr, vs, x_loc, cot_loc, lengths):
    V, S = pltpu.VMEM, jax.ShapeDtypeStruct
    anywhere, vmem = pl.BlockSpec(memory_space=pl.ANY), pl.BlockSpec(memory_space=pltpu.VMEM)
    blocks = (4, 2, 2, 2)
    outs = [
        (S((16, *blocks, 32, 512), bf16), anywhere),
        (S((*blocks, 128, D), bf16), anywhere),
        (S((16, D), f32), vmem),
        (S((D, 512), bf16), anywhere),
        (S((3, 512, D), bf16), anywhere),
        (S((8, 2, 512), f32), vmem),
        (S((D, 512), bf16), anywhere),
        (S((512, D), f32), anywhere),
        (S((512, 128), f32), vmem),
        (S((D, 512), bf16), anywhere),
        (S((512, FF), bf16), anywhere),
        (S((512, FF), bf16), anywhere),
        (S((512, D), f32), anywhere),
        (S((512, D), bf16), anywhere),
        (S((512, D), bf16), anywhere),
        (S((D, 512), bf16), anywhere),
        (S((8, D), f32), vmem),
    ]
    dma = pltpu.SemaphoreType.DMA
    return pl.pallas_call(
        forward_kernel,
        out_shape=[o[0] for o in outs],
        out_specs=[o[1] for o in outs],
        in_specs=[vmem] * 5 + [anywhere] * 2 + [pl.BlockSpec(memory_space=pltpu.SMEM)],
        scratch_shapes=[
            V((16, *blocks, 32, 512), bf16),
            V((8, *blocks, 128, 128), bf16),
            V((*blocks, 16, 128), bf16),
            V((4, 128, D), bf16),
            V((4, 128, D), bf16),
            V((3, 512, D), bf16),
            V((D, 512), bf16),
            V((512, D), bf16),
            V((512, D), f32),
            V((512, D), f32),
            V((512, D), f32),
            V((512, D), bf16),
            V((512, FF), bf16),
            V((512, FF), bf16),
            V((D, 512), bf16),
            V((D, 512), bf16),
            V((D, 512), bf16),
            V((6, 1, 512), f32),
            V((8, 1, 512), f32),
            dma((24, 6)),
            dma((24, 6)),
            dma((24,)),
            dma((6,)),
            dma((6,)),
            dma((2, 3)),
            dma((2, 3)),
            dma((2,)),
            dma((16,)),
            dma((8, 3)),
        ],
        compiler_params=pltpu.CompilerParams(
            collective_id=1, has_side_effects=True, vmem_limit_bytes=62 * 1024 * 1024
        ),
        name="forward_pass",
    )(sa, sm, se, sr, vs, x_loc, cot_loc, lengths)


SCATTER_LAGS = (0, 1, 3, 5, 7)
RING = 10


def backward_kernel(
    w1h, w2h, vec, xt_i, qkv_i, lse, bt_i, n1_i, f1, slt_i, act_i, gp_i, g2_i, res_i, gc_i, gct_i, small, lengths,
    res_o, ig_o, ga_o, gm_o, ge_o, gr_o, vg_o,
    act, gp, gc, gct, slt, xt, bt, qkv, gs, n1, wr, we, wm, wa,
    gh, r1, r2, r3, r4, h2, h3, ga, gm, ge, gr,
    vg, bg, v1, v2, v3, v4, vh,
    lsem, wrsem, wesem, ssem, rsem, stsem, vssem, vrsem, xssem, xrsem, xlsem,
):
    z, y, x, c = place()
    sh = x * 2 + c
    dp = z * 2 + y
    up = [lax.rem(z + k, 4) for k in (1, 2, 3)]

    loads = []

    def load(src, dst):
        copy = pltpu.make_async_copy(src, dst, lsem.at[len(loads)])
        copy.start()
        loads.append(copy)
        return copy

    got_gct, got_act = load(gct_i, gct), load(act_i, act)

    def wr_load(j):
        slot = lax.rem(j, 2) if not isinstance(j, int) else j % 2
        a, b = (lax.div(j, 2), lax.rem(j, 2)) if not isinstance(j, int) else (j // 2, j % 2)
        return pltpu.make_async_copy(w2h.at[a, b], wr.at[slot], wrsem.at[slot])

    def we_load(j):
        slot = lax.rem(j, 2) if not isinstance(j, int) else j % 2
        return pltpu.make_async_copy(w1h.at[8 + j], we.at[slot], wesem.at[slot])

    def remote(src, dst, s, r, to):
        return pltpu.make_async_remote_copy(src, dst, s, r, device_id=to, device_id_type=MESH)

    bar = pltpu.get_barrier_semaphore()
    others = [device(z, y, x, 1 - c), device(z, y, 1 - x, c), device(z, y, 1 - x, 1 - c), device(z, 1 - y, x, c)]
    others += [device(up[k], y, x, c) for k in range(3)]
    for other in others:
        pl.semaphore_signal(bar, inc=1, device_id=other, device_id_type=MESH)

    def mod(p, n):
        return p % n if isinstance(p, int) else lax.rem(p, n)

    def copies(p, core, stage):
        own = gh.at[mod(p, RING)]
        R1, R2, R3, R4 = r1.at[mod(p, 8)], r2.at[mod(p, 8)], r3.at[mod(p, 8)], r4.at[mod(p, 8)]
        H2, H3 = h2.at[mod(p, 4)], h3.at[mod(p, 4)]

        def send(slot, a, b, to):
            return remote(a, b, ssem.at[p, slot], rsem.at[p, slot], to)

        if stage == 0:
            return [send(0, own.at[:, :, :, 1 - c], R1, device(z, y, x, 1 - c))]
        if core == 0:
            if stage == 1:
                return [send(1, own.at[:, :, 1 - x, c], R2, device(z, y, 1 - x, c))]
            if stage == 2:
                return [send(2, H2.at[:, 1 - y], R3.at[pl.ds(0, 4)], device(z, 1 - y, x, c))]
            return [send(3 + k, H3.at[up[k]], R4.at[k], device(up[k], y, x, c)) for k in range(3)]
        if stage == 1:
            return [send(1, own.at[:, 1 - y, :, c], R2, device(z, 1 - y, x, c))]
        if stage == 2:
            return [send(3 + k, H2.at[up[k]], R3.at[pl.ds(2 * k, 2)], device(up[k], y, x, c)) for k in range(3)]
        return [send(2, H3.at[1 - x], R4.at[0], device(z, y, 1 - x, c))]

    def wide(v):
        return v.astype(f32)

    def store(p, kind):
        def at(n, width):
            return pl.ds(pl.multiple_of(n * width, width), width)

        if kind == 0:
            ref, out, index = gr, gr_o, (ALL, at(p, 128))
        elif kind == 1:
            ref, out, index = ge, ge_o, (ALL, at(p - 8, 512))
        elif kind == 2:
            ref, out, index = gm, gm_o, (ALL, at(p - 16, 512))
        else:
            ref, out, index = ga, ga_o, ((p - 18) // 2, ALL, at((p - 18) % 2, 512))
        return ref, index, pltpu.make_async_copy(ref.at[index], out.at[index], stsem.at[p])

    kinds = ((0, 0, 8), (1, 8, 16), (2, 16, 18), (3, 18, 24))

    def close(p, g):
        for kind, low, high in kinds:

            def run(kind=kind):
                ref, index, out = store(p, kind)
                if kind == 0:
                    tall = jnp.concatenate([g[:, n * 128 : n * 128 + 128] for n in range(4)], axis=0)
                    ref[index] = tall.T
                else:
                    ref[index] = g
                out.start()

            when(within(p, low, high), run)

    def arrive(p, core, stage):
        GH = gh.at[mod(p, RING)]
        R1, R2, R3, R4 = r1.at[mod(p, 8)], r2.at[mod(p, 8)], r3.at[mod(p, 8)], r4.at[mod(p, 8)]
        H2, H3 = h2.at[mod(p, 4)], h3.at[mod(p, 4)]
        if stage > 0:
            for copy in copies(p, core, stage - 1):
                copy.wait()
        if stage == 1:

            @pl.loop(0, 4)
            def _(a):
                GH[a, :, :, c] = GH[a, :, :, c] + R1[a]

        elif stage == 2:

            @pl.loop(0, 4)
            def _(a):
                mine = GH[a, :, x, c] if core == 0 else GH[a, y, :, c]
                H2[a] = mine + R2[a]

        elif stage == 3 and core == 0:

            H3[...] = H2[:, y] + R3[0:4]

        elif stage == 3:

            @pl.loop(0, 2)
            def _(a):
                H3[a] = (wide(H2[z, a]) + wide(R3[a]) + wide(R3[2 + a]) + wide(R3[4 + a])).astype(bf16)

        elif stage == 4 and core == 0:
            close(p, wide(H3[z]) + wide(R4[0]) + wide(R4[1]) + wide(R4[2]))
        elif stage == 4:
            close(p, wide(H3[x]) + wide(R4[0]))
        if stage < 4:
            for copy in copies(p, core, stage):
                copy.start()

    def tick(t):
        for stage in (4, 3, 2, 1, 0):
            p = t - SCATTER_LAGS[stage]

            def run(p=p, stage=stage):
                if stage == 0:
                    arrive(p, 0, 0)
                else:
                    pl.when(c == 0)(lambda: arrive(p, 0, stage))
                    pl.when(c == 1)(lambda: arrive(p, 1, stage))

            when(within(p, 0, 24), run)

    def exchange(src, dst, which):
        sends = []
        for k in (1, 2, 3):
            to = lax.rem(sh + k, 4)
            rows = pl.ds(pl.multiple_of(to * 128, 128), 128)
            sends.append(
                remote(src.at[rows], dst.at[sh], xssem.at[which, k - 1], xrsem.at[which, k - 1], (dp, to))
            )
        rows = pl.ds(pl.multiple_of(sh * 128, 128), 128)
        sends_own = pltpu.make_async_copy(src.at[rows], dst.at[sh], xlsem.at[which])
        sends_own.start()
        return [*sends, sends_own]

    used = lengths[sh]
    moved = []

    got_two, got_gc = load(g2_i, gs), load(gc_i, gc)
    wr_load(0).start()
    we_load(0).start()
    got_gp, got_sl = load(gp_i, gp), load(slt_i, slt)
    got_gct.wait()
    got_act.wait()
    for part in range(4):

        @pl.loop(0, 8)
        def _(j):
            cols = pl.ds(pl.multiple_of(j * 512, 512), 512)
            got = dot(gct[part * 256 : part * 256 + 256, :], act[:, cols]).astype(bf16)
            for n in range(2):
                for k in range(4):
                    for g in range(4):
                        row = n * 128 + g * 32
                        gh[part * 2 + n, lax.div(j, 2), lax.rem(j, 2), k // 2, k % 2, :, g * 128 : g * 128 + 128] = got[
                            row : row + 32, k * 128 : k * 128 + 128
                        ]

        if part == 0:
            pl.semaphore_wait(bar, len(others))
            moved += exchange(res_i, res_o, 0)
        tick(part)
        if part == 3:
            moved[0].start()

    got_two.wait()
    got_gc.wait()
    got_gp.wait()
    got_sl.wait()
    got_n1, got_bt, got_wm = load(n1_i, n1), load(bt_i, bt), load(w1h.at[pl.ds(6, 2)], wm)
    got_qkv, got_xt, got_wa = load(qkv_i, qkv), load(xt_i, xt), load(w1h.at[pl.ds(0, 6)], wa)

    def produce(p, left, right):
        got = dot(left, right).astype(bf16)
        gh[mod(p, RING)] = got.reshape(4, 2, 2, 2, 32, 512)

    @pl.loop(0, 8)
    def _(j):
        @pl.when(j < 7)
        def _():
            wr_load(j + 1).start()
            we_load(j + 1).start()

        cols = pl.ds(pl.multiple_of(j * 512, 512), 512)
        slot = lax.rem(j, 2)
        wr_load(j).wait()
        got = dot(gc[...], wr[slot].reshape(512, D), 1, 1) * gp[:, cols].astype(f32)
        low = got.astype(bf16)
        gp[:, cols] = low
        bg[j] = jnp.sum(low.astype(f32), axis=0, keepdims=True)
        produce(8 + j, slt[...], gp[:, cols])
        we_load(j).wait()
        gs[...] += dot(gp[:, cols], we[slot].reshape(D, 512), 1, 1)
        tick(4 + j)


    vg[...] = jnp.zeros((16, D), f32)
    vg[5:8, :] = small[5:8, :]
    for j in range(8):
        vg[8 + j // 2 : 9 + j // 2, (j % 2) * 512 : (j % 2) * 512 + 512] = bg[j]
    got_n1.wait()

    @pl.loop(0, 8)
    def _(r):
        rows = pl.ds(pl.multiple_of(r * 64, 64), 64)
        grad, normed = gs[rows, :], n1[rows, :]
        vg[3:4, :] += jnp.sum(grad * normed, axis=0, keepdims=True)
        vg[4:5, :] += jnp.sum(grad, axis=0, keepdims=True)
        e = grad * vec[3:4, :]
        pull = jnp.mean(e, axis=-1, keepdims=True) + normed * jnp.mean(e * normed, axis=-1, keepdims=True)
        one = f1[rows, 0:1] * (e - pull)
        gs[rows, :] = one
        low = one.astype(bf16)
        gc[rows, :] = low
        vg[2:3, :] += jnp.sum(low.astype(f32), axis=0, keepdims=True)

    tick(12)
    moved[1].start()
    got_bt.wait()
    got_wm.wait()
    for h in range(2):
        produce(16 + h, bt[...], gc[:, h * 512 : h * 512 + 512])
    for h in range(2):
        rows = slice(h * 256, h * 256 + 256)
        back = dot(gc[rows, 0:512], wm[0].reshape(D, 512), 1, 1) + dot(gc[rows, 512:D], wm[1].reshape(D, 512), 1, 1)
        act[rows, 3 * D : 4 * D] = back.astype(bf16)

    got_qkv.wait()
    lane = lax.broadcasted_iota(jnp.int32, (1, 128), 1)
    key_ok = lax.broadcasted_iota(jnp.int32, (512, 1), 0) < used

    @pl.loop(0, 8)
    def _(i):
        @pl.when(lax.rem(i, 2) == 0)
        def _():
            tick(13 + lax.div(i, 2))

        start = pl.multiple_of(i * 128, 128)
        cols = pl.ds(start, 128)
        q2, k2, v2 = qkv[0, :, cols], qkv[1, :, cols], qkv[2, :, cols]
        db = act[:, pl.ds(pl.multiple_of(3 * D + i * 128, 128), 128)]
        k_t = k2.T
        dk = jnp.zeros((512, 128), f32)
        dv = jnp.zeros((512, 128), f32)
        turned = []
        for h in range(2):
            mine = (lane < 64) if h == 0 else (lane >= 64)
            qm = jnp.where(mine, q2, jnp.zeros_like(q2))
            dm = jnp.where(mine, db, jnp.zeros_like(db))
            parts = []
            for b in range(2):
                qb, gb = qm[b * 256 : b * 256 + 256], dm[b * 256 : b * 256 + 256]
                s = jnp.where(key_ok, dot(k2, qb, 1, 1) * (HD**-0.5), masked_score)
                share = jnp.exp(s - lse[i, h : h + 1, b * 256 : b * 256 + 256])
                gshare = dot(v2, gb, 1, 1)
                inner = jnp.sum(share * gshare, axis=0, keepdims=True)
                gscore = (share * (gshare - inner)).astype(bf16)
                dv = dv + dot(share.astype(bf16), gb)
                dk = dk + dot(gscore, qb)
                parts.append(dot(k_t[h * 64 : h * 64 + 64], gscore))
            turned.append(jnp.concatenate(parts, axis=1))
        dq = jnp.concatenate(turned, axis=0).T
        for n, (value, scale) in enumerate(((dq, HD**-0.5), (dk, HD**-0.5), (dv, 1.0))):
            low = (value * scale).astype(bf16)
            act[:, pl.ds(pl.multiple_of(n * D + i * 128, 128), 128)] = low
            if n != 1:
                vg[n // 2 : n // 2 + 1, cols] = jnp.sum(low.astype(f32), axis=0, keepdims=True)

    got_xt.wait()
    got_wa.wait()

    def vector_copies(stage):
        if stage == 0:
            return [remote(vg, v1, vssem.at[0], vrsem.at[0], device(z, y, x, 1 - c))]
        if stage == 1:
            return [remote(vg, v2, vssem.at[1], vrsem.at[1], device(z, y, 1 - x, c))]
        if stage == 2:
            return [remote(vh.at[:, 1 - y], v3, vssem.at[2], vrsem.at[2], device(z, 1 - y, x, c))]
        return [
            remote(vh.at[up[k], y], v4.at[k], vssem.at[3 + k], vrsem.at[3 + k], device(up[k], y, x, c))
            for k in range(3)
        ]

    def vector_step(stage):
        if stage > 0:
            for copy in vector_copies(stage - 1):
                copy.wait()
        if stage == 1:
            vg[...] += v1[...]
        elif stage == 2:
            vg[...] += v2[...]
            for g in range(8):
                vh[g // 2, g % 2] = vg[:, g * 128 : g * 128 + 128]
        elif stage == 3:
            for a in range(4):
                vh[a, y] += v3[a]
        elif stage == 4:
            vg_o[...] = vh[z, y] + v4[0] + v4[1] + v4[2]
        if stage < 4:
            for copy in vector_copies(stage):
                copy.start()

    vector_step(0)
    tick(17)
    moved[2].start()

    @pl.loop(0, 6)
    def _(i):
        cols = pl.ds(pl.multiple_of(i * 512, 512), 512)
        gs[...] += dot(act[:, cols], wa[i].reshape(D, 512), 1, 1)

    gc[...] = gs[...].astype(bf16)
    moved += exchange(gc, ig_o, 1)

    for i in range(6):
        produce(18 + i, xt[...], act[:, i * 512 : i * 512 + 512])
        tick(18 + i)
        if 18 + i in (22, 24, 26):
            moved[4 + (22, 24, 26).index(18 + i)].start()
        if i % 2:
            vector_step((i + 1) // 2)

    for t in range(24, 24 + SCATTER_LAGS[4]):
        tick(t)
        if t in (22, 24, 26):
            moved[4 + (22, 24, 26).index(t)].start()
        if t == 25:
            vector_step(4)

    for copy in moved:
        copy.wait()

    for kind, low, high in kinds:

        @pl.loop(low, high)
        def _(p):
            store(p, kind)[2].wait()


def backward_pass(kept, lengths):
    V, S = pltpu.VMEM, jax.ShapeDtypeStruct
    anywhere, vmem = pl.BlockSpec(memory_space=pl.ANY), pl.BlockSpec(memory_space=pltpu.VMEM)
    dma = pltpu.SemaphoreType.DMA
    shapes = [(3, 32, D), (32, D), (32, FF), (128, D)]
    near = [2, 5, 8, 16]
    return pl.pallas_call(
        backward_kernel,
        out_shape=[S((4, 128, D), bf16), S((4, 128, D), bf16)]
        + [S(s, f32) for s in shapes]
        + [S((16, 128), f32)],
        out_specs=[anywhere] * 6 + [vmem],
        in_specs=[vmem if n in near else anywhere for n in range(17)]
        + [pl.BlockSpec(memory_space=pltpu.SMEM)],
        scratch_shapes=[
            V((512, FF), bf16),
            V((512, FF), bf16),
            V((512, D), bf16),
            V((D, 512), bf16),
            V((D, 512), bf16),
            V((D, 512), bf16),
            V((D, 512), bf16),
            V((3, 512, D), bf16),
            V((512, D), f32),
            V((512, D), f32),
            V((2, 2, 2, 128, D), bf16),
            V((2, 4, 2, 2, 2, 32, 512), bf16),
            V((2, 4, 2, 2, 2, 32, 512), bf16),
            V((6, 4, 2, 2, 2, 32, 512), bf16),
            V((RING, 4, 2, 2, 2, 32, 512), bf16),
            V((8, 4, 2, 2, 32, 512), bf16),
            V((8, 4, 2, 32, 512), bf16),
            V((8, 6, 32, 512), bf16),
            V((8, 3, 32, 512), bf16),
            V((4, 4, 2, 32, 512), bf16),
            V((4, 4, 32, 512), bf16),
            *[V(s, f32) for s in shapes],
            V((16, D), f32),
            V((8, 1, 512), f32),
            V((16, D), f32),
            V((16, D), f32),
            V((4, 16, 128), f32),
            V((3, 16, 128), f32),
            V((4, 2, 16, 128), f32),
            dma((24,)),
            dma((2,)),
            dma((2,)),
            dma((24, 6)),
            dma((24, 6)),
            dma((24,)),
            dma((6,)),
            dma((6,)),
            dma((2, 3)),
            dma((2, 3)),
            dma((2,)),
        ],
        compiler_params=pltpu.CompilerParams(
            collective_id=2, has_side_effects=True, vmem_limit_bytes=62 * 1024 * 1024
        ),
        name="backward_pass",
    )(*kept, lengths)


def finish_kernel(*refs):
    ins, outs, held, wide, sems = refs[:22], refs[22:40], refs[40:58], refs[58], refs[59:]
    vg, mine, small = ins[0], lax.axis_index("shard"), ins[1:4]
    gains, big = ins[4:8], ins[8:20]
    moved = ins[20:22]
    isem, osem = sems

    def load(n, src):
        copy = pltpu.make_async_copy(src, held[n], isem.at[n])
        copy.start()
        return copy

    def save(n, dst):
        copy = pltpu.make_async_copy(held[n], dst, osem.at[n])
        copy.start()
        return copy

    order = (1, 0, 2, 3)
    loads = {}
    for k in order:
        loads[k] = [load(k, gains[k])] + [load(4 + 3 * k + n, big[3 * k + n]) for n in range(3)]
    passed = [load(16 + n, moved[n]) for n in range(2)]
    saves = []

    def adam(w, m, u, g, rate, decay):
        first = beta_one * m + (1.0 - beta_one) * g
        second = beta_two * u + (1.0 - beta_two) * g * g
        root = jnp.sqrt(second * (1.0 / (1.0 - beta_two**STEP))) + adam_eps
        return first, second, w - rate * (first * (1.0 / (1.0 - beta_one**STEP)) / root + decay * w)

    for k in order:
        for copy in loads[k]:
            copy.wait()
        w, m, u = held[4 + 3 * k : 7 + 3 * k]
        new = adam(w[...], m[...], u[...], held[k][...], rates[k], matrix_decay)
        m[...], u[...], w[...] = new
        saves += [save(5 + 3 * k, outs[2 + 3 * k]), save(6 + 3 * k, outs[3 + 3 * k]), save(4 + 3 * k, outs[4 + 3 * k])]
    passed[0].wait()
    saves.append(save(16, outs[0]))
    passed[1].wait()
    wide[...] = held[17][...].astype(f32)
    saves.append(pltpu.make_async_copy(wide, outs[1], osem.at[17]))
    saves[-1].start()
    grad = pltpu.roll(vg[...], lax.rem(4 - mine, 4) * 32, 1)[0:NV, 0:32]
    outs[14][...], outs[15][...], outs[16][...] = adam(small[0][...], small[1][...], small[2][...], grad, rates[4], 0.0)
    outs[17][...] = grad[2:3, :]
    for copy in saves:
        copy.wait()


def finish_step(masters, firsts, seconds, result, input_gradient, gradients, vector_gradient):
    V, S = pltpu.VMEM, jax.ShapeDtypeStruct
    anywhere, vmem = pl.BlockSpec(memory_space=pl.ANY), pl.BlockSpec(memory_space=pltpu.VMEM)
    big = [t[n] for n in range(4) for t in (masters, firsts, seconds)]
    moved = [S(t.shape, t.dtype) for t in (result, input_gradient)]
    outs = [moved[0], S(moved[1].shape, f32)] + [S(t.shape, f32) for t in big] + [S((NV, 32), f32)] * 3 + [S((1, 32), f32)]
    dma = pltpu.SemaphoreType.DMA
    *done, bias = pl.pallas_call(
        finish_kernel,
        out_shape=outs,
        out_specs=[anywhere] * 14 + [vmem] * 4,
        in_specs=[vmem] * 4 + [anywhere] * 18,
        scratch_shapes=[V(t.shape, f32) for t in gradients]
        + [V(t.shape, f32) for t in big]
        + [V(t.shape, t.dtype) for t in moved]
        + [V(moved[1].shape, f32)]
        + [dma((18,)), dma((18,))],
        compiler_params=pltpu.CompilerParams(vmem_limit_bytes=62 * 1024 * 1024),
        name="finish_step",
    )(vector_gradient, masters[4], firsts[4], seconds[4], *gradients, *big, result, input_gradient)
    return (*done, bias[0])


def product(left_side, right_side):
    return jnp.einsum("sri,ij->srj", left_side, right_side, preferred_element_type=f32)


def product_back(gradient, right_side):
    return jnp.einsum("srj,ij->sri", gradient, right_side, preferred_element_type=f32)


def outer_sum(left_side, gradient):
    return jnp.einsum("sri,srj->ij", left_side, gradient, preferred_element_type=f32)


def sum_rows(tensor):
    return jnp.sum(tensor.astype(f32), axis=(0, 1))


def split_heads(tensor):
    return tensor.reshape(tensor.shape[0], tensor.shape[1], -1, HD)


def norm_forward(tensor, gain, shift):
    center = tensor - jnp.mean(tensor, axis=-1, keepdims=True)
    spread = jnp.mean(center * center, axis=-1, keepdims=True)
    factor = lax.rsqrt(spread + norm_eps)
    normed = center * factor
    return (normed * gain + shift, normed, factor)


def norm_backward(gradient, normed, factor, gain):
    grad_normed = gradient * gain
    return factor * (
        grad_normed
        - jnp.mean(grad_normed, axis=-1, keepdims=True)
        - normed * jnp.mean(grad_normed * normed, axis=-1, keepdims=True)
    )


def attention_core(queries, keys, values, key_valid):
    score_scale = HD ** (-0.5)
    scores = (
        jnp.einsum("sqhd,skhd->shqk", split_heads(queries), split_heads(keys), preferred_element_type=f32)
        * score_scale
    )
    scores = jnp.where(key_valid[:, None, None, :], scores, masked_score)
    row_peak = jnp.max(scores, axis=-1, keepdims=True)
    row_sum = jnp.sum(jnp.exp(scores - row_peak), axis=-1, keepdims=True)
    shares = jnp.exp(scores - (row_peak + jnp.log(row_sum)))
    shares_low = shares.astype(bf16)
    blended = jnp.einsum("shqk,skhd->sqhd", shares_low, split_heads(values), preferred_element_type=f32)
    blended = blended.reshape(queries.shape).astype(bf16)
    return (blended, shares, shares_low)


def attention_back(grad_blended, queries, keys, values, shares, shares_low):
    score_scale = HD ** (-0.5)
    heads_grad = split_heads(grad_blended)
    grad_shares = jnp.einsum("sqhd,skhd->shqk", heads_grad, split_heads(values), preferred_element_type=f32)
    share_dot = jnp.sum(shares * grad_shares, axis=-1, keepdims=True)
    grad_scores = (shares * (grad_shares - share_dot)).astype(bf16)
    grad_query = (
        jnp.einsum("shqk,skhd->sqhd", grad_scores, split_heads(keys), preferred_element_type=f32) * score_scale
    )
    key_part = (
        jnp.einsum("shqk,sqhd->skhd", grad_scores, split_heads(queries), preferred_element_type=f32) * score_scale
    )
    value_part = jnp.einsum("shqk,sqhd->skhd", shares_low, heads_grad, preferred_element_type=f32)
    return (
        grad_query.reshape(queries.shape).astype(bf16),
        key_part.reshape(keys.shape).astype(bf16),
        value_part.reshape(values.shape).astype(bf16),
    )


def adam_update(weight, first, second, gradient, rate, decay):
    first_new = beta_one * first + (1.0 - beta_one) * gradient
    second_new = beta_two * second + (1.0 - beta_two) * gradient * gradient
    first_hat = first_new / (1.0 - beta_one**STEP)
    second_hat = second_new / (1.0 - beta_two**STEP)
    weight_new = weight - rate * (first_hat / (jnp.sqrt(second_hat) + adam_eps) + decay * weight)
    return (first_new, second_new, weight_new)


def finish(result, input_gradient, masters, firsts, seconds, reduced):
    updated = []
    for number in range(5):
        decay = matrix_decay if number < 4 else 0.0
        updated += adam_update(
            masters[number], firsts[number], seconds[number], reduced[number], rates[number], decay
        )
    return (result, input_gradient, *updated, reduced[4][2])


def local_fast(inputs, cotangent, lengths, *states):
    masters, firsts, seconds = states[0::3], states[1::3], states[2::3]
    kept = forward_pass(*masters, inputs, cotangent, lengths)
    result, input_gradient, *gradients, vector_gradient = backward_pass(kept, lengths)
    return finish_step(masters, firsts, seconds, result, input_gradient, gradients, vector_gradient)


def local_any(inputs, cotangent, lengths, *states):
    masters, firsts, seconds = states[0::3], states[1::3], states[2::3]
    attend_low, mixing_low, expand_low, reduce_low = [w.astype(bf16) for w in masters[:4]]
    attend_full = lax.all_gather(attend_low, ("dp", "shard"), axis=1, tiled=True)
    mixing_full, expand_full, reduce_full = [
        lax.all_gather(w, ("dp", "shard"), axis=0, tiled=True) for w in (mixing_low, expand_low, reduce_low)
    ]
    vec = lax.all_gather(masters[4].astype(bf16), ("dp", "shard"), axis=1, tiled=True).astype(f32)

    block_in = lax.all_to_all(inputs, "shard", split_axis=0, concat_axis=1, tiled=True)
    block_cot = lax.all_to_all(cotangent, "shard", split_axis=0, concat_axis=1, tiled=True)
    count, length = block_in.shape[0], block_in.shape[1]
    used = lax.dynamic_slice_in_dim(lengths, lax.axis_index("shard") * count, count)
    valid = jnp.arange(length)[None, :] < used[:, None]
    row_valid = valid.astype(f32)

    queries = (product(block_in, attend_full[0]) + vec[0]).astype(bf16)
    keys = product(block_in, attend_full[1]).astype(bf16)
    values = (product(block_in, attend_full[2]) + vec[1]).astype(bf16)
    blended, shares, shares_low = attention_core(queries, keys, values, valid)
    attended = product(blended, mixing_full) + vec[2]
    settled, normed_one, factor_one = norm_forward(block_in.astype(f32) + attended, vec[3], vec[4])
    settled_low = settled.astype(bf16)
    expanded = product(settled_low, expand_full) + vec[8:].reshape(FF)
    activated = jax.nn.gelu(expanded, approximate=False).astype(bf16)
    contracted = product(activated, reduce_full) + vec[7]
    finished, normed_two, factor_two = norm_forward(settled + contracted, vec[5], vec[6])
    result = (finished * row_valid[:, :, None]).astype(bf16)
    result = lax.all_to_all(result, "shard", split_axis=1, concat_axis=0, tiled=True)

    grad_out = block_cot.astype(f32) * row_valid[:, :, None]
    gain_two = sum_rows(grad_out * normed_two)
    shift_two = sum_rows(grad_out)
    grad_two = norm_backward(grad_out, normed_two, factor_two, vec[5])
    grad_contract = grad_two.astype(bf16)
    grad_reduce = outer_sum(activated, grad_contract)
    bias_reduce = sum_rows(grad_contract)
    grad_active = product_back(grad_contract, reduce_full)
    gelu_pull = jax.vjp(functools.partial(jax.nn.gelu, approximate=False), expanded)[1]
    grad_expanded = gelu_pull(grad_active)[0].astype(bf16)
    grad_expand = outer_sum(settled_low, grad_expanded)
    bias_expand = sum_rows(grad_expanded)
    grad_settled = grad_two + product_back(grad_expanded, expand_full)
    gain_one = sum_rows(grad_settled * normed_one)
    shift_one = sum_rows(grad_settled)
    grad_one = norm_backward(grad_settled, normed_one, factor_one, vec[3])
    grad_attended = grad_one.astype(bf16)
    grad_mixing = outer_sum(blended, grad_attended)
    bias_mixing = sum_rows(grad_attended)
    grad_blended = product_back(grad_attended, mixing_full).astype(bf16)
    query_grad, key_grad, value_grad = attention_back(grad_blended, queries, keys, values, shares, shares_low)
    grad_attend = jnp.stack([outer_sum(block_in, g) for g in (query_grad, key_grad, value_grad)])
    input_gradient = (
        grad_one
        + product_back(query_grad, attend_full[0])
        + product_back(key_grad, attend_full[1])
        + product_back(value_grad, attend_full[2])
    )
    input_gradient = lax.all_to_all(input_gradient, "shard", split_axis=1, concat_axis=0, tiled=True)
    small_rows = [sum_rows(query_grad), sum_rows(value_grad), bias_mixing, gain_one, shift_one, gain_two, shift_two]
    small_rows = jnp.stack([*small_rows, bias_reduce])
    grad_vectors = jnp.concatenate([small_rows, bias_expand.reshape(NV - 8, D)], axis=0)

    reduced = [lax.psum_scatter(grad_attend, ("dp", "shard"), scatter_dimension=1, tiled=True)]
    for g in (grad_mixing, grad_expand, grad_reduce):
        reduced.append(lax.psum_scatter(g, ("dp", "shard"), scatter_dimension=0, tiled=True))
    reduced = (*reduced, lax.psum_scatter(grad_vectors, ("dp", "shard"), scatter_dimension=1, tiled=True))
    return finish(result, input_gradient, masters, firsts, seconds, reduced)


def solution(mesh):
    fast = mesh.shape["dp"] == 8 and mesh.shape["shard"] == 4
    rows = P("dp", "shard", None)
    both = ("dp", "shard")
    middle, first, last = P(None, both, None), P(both, None), P(None, both)
    states = [middle] * 3 + [first] * 9 + [last] * 3
    return jax.shard_map(
        local_fast if fast else local_any,
        mesh=mesh,
        in_specs=(rows, rows, P("dp"), *states),
        out_specs=(rows, rows, *states, P(both)),
        check_vma=False,
    )
```
